256 devices in a mesh: band: 32 (over z, y), mp: 8 (over x, core).
Axes of the slice: x: 4, y: 4, z: 8, core: 2. Of those that a mesh axis runs over, the one named last changes fastest.
Arguments:
- skip_features: bfloat16 [192, 48, 512], P('band'), may hold values from -6 to 6
- deep_features: bfloat16 [96, 24, 2048], P('band'), may hold values from -6 to 6
- top_gains: float32 [2, 2, 512], replicated, may hold values from 0.5 to 1.5
- top_heads_in: bfloat16 [2, 512, 3, 512], P(None, 'band', None, 'mp'), may hold values from -0.25 to 0.25
- top_heads_out: bfloat16 [2, 512, 512], P(None, 'mp', 'band'), may hold values from -0.25 to 0.25
- top_hidden_in: bfloat16 [2, 512, 2048], P(None, 'band', 'mp'), may hold values from -0.25 to 0.25
- top_hidden_out: bfloat16 [2, 2048, 512], P(None, 'mp', 'band'), may hold values from -0.125 to 0.125
- top_offsets: float32 [2, 16, 11, 23], P(None, 'mp'), may hold values from -4 to 400
- deep_gains: float32 [2, 2048], replicated, may hold values from 0.5 to 1.5
- deep_offsets: float32 [64, 5, 11], P('mp'), may hold values from -4 to 400
- deep_heads_in: bfloat16 [2048, 3, 2048], P('band', None, 'mp'), may hold values from -0.125 to 0.125
- deep_heads_out: bfloat16 [2048, 2048], P('mp', 'band'), may hold values from -0.125 to 0.125
- deep_hidden_in: bfloat16 [2048, 8192], P('band', 'mp'), may hold values from -0.125 to 0.125
- deep_hidden_out: bfloat16 [8192, 2048], P('mp', 'band'), may hold values from -0.0625 to 0.0625
- expand_weight: bfloat16 [2048, 4, 512], P('band', None, 'mp'), may hold values from -0.125 to 0.125
Outputs:
- decoded: bfloat16 [192, 48, 512], P('band')
The draws below stay inside these ranges and needn't reach their ends.
All inputs are finite; a program needn't handle non-finite values.
Results may differ from the reference program's by a relative error of at most 0.03.
Values may be sent and summed in bfloat16 or wider, within the bound.
A program may use at most 64 MiB of HBM per device.

```python
import jax
import jax.numpy as jnp
import numpy as np
from jax import lax

D = 512
FF = 2048
DD = 2048
DFF = 8192
HS = 32
HEADS = 16
DHEADS = 64
WH = 6
WW = 12
DWH = 3
DWW = 6
LON = 48
LAT = 192
DLAT = 96
DLON = 24
N_MP = 8


def draw_top_offsets(key, part):
    key = jax.random.fold_in(key, 11)
    base_key = jax.random.fold_in(key, 0)
    array_shape = (2, HEADS, 2 * WH - 1, 2 * WW - 1)
    return jnp.clip(jax.random.normal(base_key, array_shape, jnp.float32), -4.0, 4.0)


def draw_deep_offsets(key, part):
    key = jax.random.fold_in(key, 23)
    base_key = jax.random.fold_in(key, 0)
    array_shape = (DHEADS, 2 * DWH - 1, 2 * DWW - 1)
    return jnp.clip(jax.random.normal(base_key, array_shape, jnp.float32), -4.0, 4.0)


def level_of(own_key, dims, shards, least, top_value):
    def one(position, shards_of):
        heights = jax.random.uniform(jax.random.fold_in(jax.random.fold_in(own_key, 6), position), (shards_of,), jnp.float32, least / len(shards), top_value / len(shards))
        return jnp.repeat(jnp.exp(heights), dims[position] // shards_of).reshape((-1,) + (1,) * (len(dims) - position - 1))

    gain = one(*shards[0])
    for cut in shards[1:]:
        gain = gain * one(*cut)
    return gain


def gaussian(rng, shape, scale, most, cuts=(), kind=jnp.bfloat16):
    factor_of = level_of(rng, shape, cuts, -0.22, 0.18) if cuts else 1.0
    values = jax.random.normal(rng, shape, jnp.float32) * scale * factor_of
    return jnp.minimum(jnp.maximum(values, -most), most).astype(kind)


def setup_inputs(seed: int = 0) -> dict:
    seeds = jax.random.split(jax.random.key(seed), 16)
    skip_features = gaussian(seeds[0], (LAT, LON, D), 1.0, 6.0, ((0, 32),))
    deep_features = gaussian(seeds[1], (DLAT, DLON, DD), 1.0, 6.0, ((0, 32),))
    top_gains = jnp.clip(1.0 + 0.1 * jax.random.normal(seeds[2], (2, 2, D), jnp.float32), 0.5, 1.5)
    top_heads_in = gaussian(seeds[3], (2, D, 3, D), D ** -0.5, 0.25, ((1, 32), (3, 8)))
    top_heads_out = gaussian(seeds[4], (2, D, D), D ** -0.5, 0.25, ((1, 8), (2, 32)))
    top_hidden_in = gaussian(seeds[5], (2, D, FF), D ** -0.5, 0.25, ((1, 32), (2, 8)))
    top_hidden_out = gaussian(seeds[6], (2, FF, D), FF ** -0.5, 0.125, ((1, 8), (2, 32)))
    top_offsets = draw_top_offsets(jax.random.fold_in(seeds[15], 71), 0)
    deep_gains = jnp.clip(1.0 + 0.1 * jax.random.normal(seeds[8], (2, DD), jnp.float32), 0.5, 1.5)
    deep_offsets = draw_deep_offsets(jax.random.fold_in(seeds[15], 71), 0)
    deep_heads_in = gaussian(seeds[10], (DD, 3, DD), DD ** -0.5, 0.125, ((0, 32), (2, 8)))
    deep_heads_out = gaussian(seeds[11], (DD, DD), DD ** -0.5, 0.125, ((0, 8), (1, 32)))
    deep_hidden_in = gaussian(seeds[12], (DD, DFF), DD ** -0.5, 0.125, ((0, 32), (1, 8)))
    deep_hidden_out = gaussian(seeds[13], (DFF, DD), DFF ** -0.5, 0.0625, ((0, 8), (1, 32)))
    expand_weight = gaussian(seeds[14], (DD, 4, D), DD ** -0.5, 0.125, ((0, 32), (2, 8)))
    return {"skip_features": skip_features, "deep_features": deep_features, "top_gains": top_gains, "top_heads_in": top_heads_in, "top_heads_out": top_heads_out, "top_hidden_in": top_hidden_in, "top_hidden_out": top_hidden_out, "top_offsets": top_offsets, "deep_gains": deep_gains, "deep_offsets": deep_offsets, "deep_heads_in": deep_heads_in, "deep_heads_out": deep_heads_out, "deep_hidden_in": deep_hidden_in, "deep_hidden_out": deep_hidden_out, "expand_weight": expand_weight}


eps = 1e-05

def norm_rows(values, scales):
    floats = values.astype(jnp.float32)
    centred = floats - lax.optimization_barrier(jnp.mean(floats, axis=-1, keepdims=True))
    spread = lax.optimization_barrier(jnp.mean(centred * centred, axis=-1, keepdims=True))
    return (centred * lax.rsqrt(spread + eps) * scales.astype(jnp.float32)).astype(jnp.bfloat16)

def to_windows(values, window_rows, window_cols):
    count_rows = values.shape[0] // window_rows
    count_cols = values.shape[1] // window_cols
    trailing = values.shape[2:]
    shaped = values.reshape((count_rows, window_rows, count_cols, window_cols) + trailing)
    shaped = jnp.moveaxis(shaped, 2, 1)
    return shaped.reshape((count_rows, count_cols, window_rows * window_cols) + trailing)

def from_windows(values, window_rows, window_cols):
    count_rows, count_cols = (values.shape[0], values.shape[1])
    trailing = values.shape[3:]
    shaped = values.reshape((count_rows, count_cols, window_rows, window_cols) + trailing)
    shaped = jnp.moveaxis(shaped, 1, 2)
    return shaped.reshape((count_rows * window_rows, count_cols * window_cols) + trailing)

def offset_hot(extent):
    places = np.arange(extent)
    marks = places[:, None, None] - places[None, :, None] + extent - 1 == np.arange(2 * extent - 1)[None, None, :]
    return jnp.asarray(marks.astype(np.float32))

def position_bias(offsets, window_rows, window_cols):
    expanded = jnp.einsum('hab,ija,klb->hikjl', offsets.astype(jnp.float32), offset_hot(window_rows), offset_hot(window_cols), precision=lax.Precision.HIGHEST)
    return expanded.reshape(offsets.shape[0], window_rows * window_cols, window_rows * window_cols)

def window_attend(queries, key_heads, value_heads, query_rows, key_rows, window_cols, additive):
    query_win = to_windows(queries, query_rows, window_cols).astype(jnp.float32)
    key_win = to_windows(key_heads, key_rows, window_cols).astype(jnp.float32)
    value_win = to_windows(value_heads, key_rows, window_cols).astype(jnp.float32)
    scale_factor = queries.shape[-1] ** (-0.5)
    scores = jnp.einsum('abnhs,abmhs->abhnm', query_win, key_win) * scale_factor + additive
    highest = lax.optimization_barrier(jnp.max(scores, axis=-1, keepdims=True))
    weights = jnp.exp(scores - highest)
    attention = (weights / lax.optimization_barrier(jnp.sum(weights, axis=-1, keepdims=True))).astype(jnp.bfloat16)
    blended = jnp.einsum('abhnm,abmhs->abnhs', attention.astype(jnp.float32), value_win).astype(jnp.bfloat16)
    return from_windows(blended, query_rows, window_cols)

def grouped_project(activations, weight):
    group_size = activations.shape[1] // N_MP
    running = jnp.zeros((activations.shape[0], weight.shape[1]), jnp.float32)
    for group_index in range(N_MP):
        lower = group_index * group_size
        partial_term = jnp.dot(activations[:, lower:lower + group_size], weight[lower:lower + group_size], preferred_element_type=jnp.float32)
        rounded = lax.optimization_barrier(partial_term.astype(jnp.bfloat16))
        running = running + rounded.astype(jnp.float32)
    return running

def project_heads(state, scales, heads_in):
    count_rows, count_cols, width_all = state.shape
    normed = norm_rows(state, scales).reshape(count_rows * count_cols, width_all)
    projected = jnp.dot(normed, heads_in.reshape(width_all, 3 * width_all), preferred_element_type=jnp.float32).astype(jnp.bfloat16)
    return projected.reshape(count_rows, count_cols, 3, width_all // HS, HS)

def finish_block(state, blended, heads_out, scales, hidden_in, hidden_out):
    count_rows, count_cols, width_all = state.shape
    tokens_all = count_rows * count_cols
    delta = grouped_project(blended.reshape(tokens_all, width_all), heads_out)
    middle = (state.astype(jnp.float32) + delta.reshape(state.shape)).astype(jnp.bfloat16)
    normed = norm_rows(middle, scales).reshape(tokens_all, width_all)
    activated = jax.nn.gelu(jnp.dot(normed, hidden_in, preferred_element_type=jnp.float32), approximate=False).astype(jnp.bfloat16)
    delta_two = grouped_project(activated, hidden_out)
    return (middle.astype(jnp.float32) + delta_two.reshape(state.shape)).astype(jnp.bfloat16)

def reference(skip_features, deep_features, top_gains, top_heads_in, top_heads_out, top_hidden_in, top_hidden_out, top_offsets, deep_gains, deep_offsets, deep_heads_in, deep_heads_out, deep_hidden_in, deep_hidden_out, expand_weight):
    projected = project_heads(deep_features, deep_gains[0], deep_heads_in)
    deep_additive = position_bias(deep_offsets, DWH, DWW)[None, None]
    blended = window_attend(projected[:, :, 0], projected[:, :, 1], projected[:, :, 2], DWH, DWH, DWW, deep_additive)
    deep_out = finish_block(deep_features, blended, deep_heads_out, deep_gains[1], deep_hidden_in, deep_hidden_out)
    flat_deep = deep_out.reshape(DLAT * DLON, DD)
    grown = jnp.dot(flat_deep, expand_weight.reshape(DD, 4 * D), preferred_element_type=jnp.float32).astype(jnp.bfloat16)
    grown = grown.reshape(DLAT, DLON, 2, 2, D).transpose(0, 2, 1, 3, 4).reshape(LAT, LON, D)
    state = (skip_features.astype(jnp.float32) + grown.astype(jnp.float32)).astype(jnp.bfloat16)
    half_rows = WH // 2
    half_cols = WW // 2
    for section_index in range(2):
        bias_full = position_bias(top_offsets[section_index], WH, WW)
        projected = project_heads(state, top_gains[section_index, 0], top_heads_in[section_index])
        queries = projected[:, :, 0]
        key_heads = projected[:, :, 1]
        value_heads = projected[:, :, 2]
        if section_index == 0:
            blended = window_attend(queries, key_heads, value_heads, WH, WH, WW, bias_full[None, None])
        else:
            padding = ((half_rows, half_rows), (0, 0), (0, 0), (0, 0))
            queries = jnp.roll(jnp.pad(queries, padding), -half_cols, axis=1)
            key_heads = jnp.roll(jnp.pad(key_heads, padding), -half_cols, axis=1)
            value_heads = jnp.roll(jnp.pad(value_heads, padding), -half_cols, axis=1)
            row_index = jnp.arange(LAT + WH, dtype=jnp.int32)
            valid_key = ((row_index >= half_rows) & (row_index < LAT + half_rows)).astype(jnp.float32)
            valid_grid = jnp.broadcast_to(valid_key[:, None], (LAT + WH, LON))
            valid_win = to_windows(valid_grid, WH, WW)
            additive = bias_full[None, None] + (valid_win[:, :, None, None, :] - 1.0) * 1e+30
            blended = window_attend(queries, key_heads, value_heads, WH, WH, WW, additive)
            blended = jnp.roll(blended, half_cols, axis=1)[half_rows:half_rows + LAT]
        state = finish_block(state, blended, top_heads_out[section_index], top_gains[section_index, 1], top_hidden_in[section_index], top_hidden_out[section_index])
    return state
```

```python
import functools

import jax
import jax.numpy as jnp
import numpy as np
from jax import lax
from jax.experimental import pallas as pl
from jax.experimental.pallas import tpu as pltpu
from jax.sharding import PartitionSpec as P

BF = jnp.bfloat16
F32 = jnp.float32
EPS = 1e-05
NEG = -1e30
T = 80
USED = 72
EXT = 400
SCALE = 32 ** (-0.5)
STAGES = ((0, 1024), (1024, 1024), (2048, 1280))
MESH = pl.DeviceIdType.MESH

PIECES = (
    (-1, 0, 3, 3, 0, 12, 80, 48),
    (1, 0, 0, 3, 0, 12, 128, 48),
    (0, -1, 0, 6, 6, 6, 176, 48),
    (0, 1, 0, 6, 0, 6, 224, 48),
    (-1, -1, 3, 3, 6, 6, 272, 32),
    (-1, 1, 3, 3, 0, 6, 304, 32),
    (1, -1, 0, 3, 6, 6, 336, 32),
    (1, 1, 0, 3, 0, 6, 368, 32),
)


@functools.lru_cache(None)
def tables():
    key_row = np.zeros(EXT, np.int32)
    key_col = np.zeros(EXT, np.int32)
    key_ok = np.zeros(EXT, bool)
    key_step = np.zeros(EXT, np.int32)
    t = np.arange(USED)
    key_row[:USED], key_col[:USED], key_ok[:USED] = t // 12, t % 12, True
    take = np.zeros((EXT, T), np.float32)
    for band_step, x_step, r0, nr, c0, nc, off, _ in PIECES:
        p = np.arange(nr * nc)
        r, c = r0 + p // nc, c0 + p % nc
        key_row[off : off + nr * nc] = r + 6 * band_step
        key_col[off : off + nr * nc] = c + 12 * x_step
        key_ok[off : off + nr * nc] = True
        key_step[off : off + nr * nc] = band_step
        take[off + p, r * 12 + c] = 1.0
    keys = np.zeros((8, EXT), np.int32)
    keys[0] = np.where(key_ok, 23 * key_row + key_col, -100000)
    keys[1] = key_step
    q_row, q_col = np.zeros(T, np.int32), np.zeros(T, np.int32)
    q_row[:USED], q_col[:USED] = t // 12, t % 12
    same = ((q_row >= 3)[:, None] == (key_row >= 3)[None]) & (
        (q_col >= 6)[:, None] == (key_col >= 6)[None]
    )
    mask_one = np.where(same & key_ok[None], 0.0, NEG).astype(np.float32)
    mask_zero = np.where((np.arange(T) < USED)[None], 0.0, NEG).astype(np.float32)
    mask_zero = np.broadcast_to(mask_zero, (T, T)).copy()
    deep_row, deep_col = np.zeros(T, np.int32), np.zeros(T, np.int32)
    deep_row[:USED], deep_col[:USED] = t // 24, t % 24
    deep_keys = np.full((8, T), -100000, np.int32)
    deep_keys[:, :USED] = 11 * deep_row[:USED] + deep_col[:USED] % 6
    ok = (np.arange(T) < USED)[None] & ((deep_col // 6)[:, None] == (deep_col // 6)[None])
    mask_deep = np.where(ok, 0.0, NEG).astype(np.float32)
    grow = np.zeros((4, T, T), np.float32)
    part = np.zeros((T, 4), np.float32)
    i, k = t // 12, t % 12
    for w in range(4):
        grow[w, t, (i // 2) * 24 + 6 * w + k // 2] = 1.0
    part[t, 2 * (i % 2) + k % 2] = 1.0
    part = np.repeat(part[:, :, None], 64, axis=2).reshape(T, 256)
    pick = np.zeros((4, T, 288), np.float32)
    place = np.zeros((288, 4 * T), np.float32)
    for w in range(4):
        pick[w, t, i * 48 + 12 * w + k] = 1.0
        place[i * 48 + 12 * w + k, w * T + t] = 1.0
    heads = np.zeros((8 * T, 256), np.float32)
    for h in range(8):
        heads[h * T : (h + 1) * T, h * 32 : (h + 1) * 32] = 1.0
    return (
        keys,
        mask_one,
        mask_zero,
        deep_keys,
        mask_deep,
        grow.astype(jnp.bfloat16),
        part,
        pick.astype(jnp.bfloat16),
        place.astype(jnp.bfloat16),
        take[T:].astype(jnp.bfloat16),
        heads.astype(jnp.bfloat16),
    )


def dot(a, b):
    return jnp.dot(a, b, preferred_element_type=F32)


def dot_t(a, b):
    return lax.dot_general(a, b, (((1,), (1,)), ((), ())), preferred_element_type=F32)


def thirds(values):
    first = values.astype(BF)
    rest = values - first.astype(F32)
    second = rest.astype(BF)
    third = (rest - second.astype(F32)).astype(BF)
    return jnp.concatenate([first, second, third], axis=0)


def norm_rows(values, scales):
    centred = values - jnp.mean(values, axis=-1, keepdims=True)
    spread = jnp.mean(centred * centred, axis=-1, keepdims=True)
    return (centred * lax.rsqrt(spread + EPS) * scales).astype(BF)


def gelu(values):
    return values * 0.5 * (1.0 + lax.erf(values * (0.5**0.5)))


def attend(q, k, v, bias, heads):
    stacked = jnp.concatenate([q] * 8, axis=0) * heads
    scores = dot_t(stacked, k) * SCALE + bias
    weights = jnp.exp(scores - jnp.max(scores, axis=-1, keepdims=True))
    weights = (weights * (1.0 / jnp.sum(weights, axis=-1, keepdims=True))).astype(BF)
    mixed = dot(weights, v) * heads.astype(F32)
    total = mixed[0:T]
    for h in range(1, 8):
        total = total + mixed[h * T : (h + 1) * T]
    return total.astype(BF)


def kernel(
    skip_ref,
    deep_ref,
    top_gain_ref,
    deep_gain_ref,
    top_tab_ref,
    deep_tab_ref,
    deep_pack_ref,
    top_pack_ref,
    keys_ref,
    mask_one_ref,
    mask_zero_ref,
    deep_keys_ref,
    mask_deep_ref,
    grow_ref,
    part_ref,
    pick_ref,
    place_ref,
    take_ref,
    heads_ref,
    out_ref,
    dw,
    tw,
    tabs,
    deep_raw,
    deep_bias,
    top_raw,
    bias_zero,
    bias_one,
    deep_x,
    rs_send,
    rs_recv,
    mids,
    grow_send,
    grow_recv,
    swap_send,
    swap_recv,
    halo_send,
    halo,
    fin,
    s_o1y,
    r_o1y,
    s_o1z,
    r_o1z,
    s_o2z,
    r_o2z,
    s_o2y,
    r_o2y,
    s_tz,
    r_tz,
    s_ty,
    r_ty,
    s_tx,
    r_tx,
    s_tab,
    r_tab,
    s_rs,
    r_rs,
    s_ag,
    r_ag,
    s_grow,
    r_grow,
    s_swap,
    r_swap,
    s_halo,
    r_halo,
    s_fin,
    r_fin,
):
    band = lax.axis_index("band")
    m = lax.axis_index("mp")
    z, y, x, c = band // 4, band % 4, m // 2, m % 2
    zs = [lax.rem(z + d, 8) for d in range(8)]
    ys = [lax.rem(y + d, 4) for d in range(4)]
    xs = [lax.rem(x + d, 4) for d in range(4)]
    ms = [lax.rem(m + d, 8) for d in range(8)]
    other = 1 - c

    def at_z(d):
        return {"band": zs[d % 8] * 4 + y, "mp": m}

    def at_y(d):
        return {"band": z * 4 + ys[d % 4], "mp": m}

    def at_m(d):
        return {"band": band, "mp": ms[d % 8]}

    def at_x(d, core):
        return {"band": band, "mp": xs[d % 4] * 2 + core}

    def at_piece(band_step, x_step):
        return {"band": lax.rem(band + band_step + 32, 32), "mp": xs[x_step % 4] * 2 + c}

    barrier = pltpu.get_barrier_semaphore()
    greeted = [at_z(1), at_z(7)] + [at_y(d) for d in (1, 2, 3)] + [at_m(d) for d in range(1, 8)]
    greeted += [at_piece(b, d) for b in (-1, 1) for d in (-1, 0, 1)]
    for who in greeted:
        pl.semaphore_signal(barrier, inc=1, device_id=who, device_id_type=MESH)

    sends = []

    def copy(src, dst, ss, rs, who):
        return pltpu.make_async_remote_copy(
            src_ref=src, dst_ref=dst, send_sem=ss, recv_sem=rs, device_id=who, device_id_type=MESH
        )

    def send(src, dst, ss, rs, who):
        cp = copy(src, dst, ss, rs, who)
        cp.start()
        sends.append(cp)

    def await_at(dst, ss, rs, who):
        copy(dst, dst, ss, rs, who).wait_recv()

    for half in range(2):
        dw[z, y, half] = deep_pack_ref[32 * half : 32 * half + 32, :]
    tw[x, z, y] = top_pack_ref[...]
    tabs[x] = top_tab_ref[...]
    pl.semaphore_wait(barrier, len(greeted))

    def o1(zz, s):
        lo, n = STAGES[s]
        return dw.at[zz, :, 0, :, pl.ds(lo, n)]

    def o1_own(yy, s):
        lo, n = STAGES[s]
        return dw.at[z, yy, 0, :, pl.ds(lo, n)]

    def o2(zz, yy, s):
        lo, n = STAGES[s]
        return dw.at[zz, yy, 1, :, pl.ds(lo, n)]

    def slot(order, way, dist):
        most = 4 if order == 1 else 3
        return dist - 1 if way > 0 else most + dist - 1

    def limit(order, way):
        return 4 if (order == 1) == (way > 0) else 3

    def hop(order, s, way, dist):
        origin = zs[(-way * (dist - 1)) % 8]
        k = slot(order, way, dist)
        if order == 1:
            send(o1(origin, s), o1(origin, s), s_o1z.at[s, k], r_o1z.at[s, k], at_z(way))
        else:
            send(o2(origin, y, s), o2(origin, y, s), s_o2z.at[s, k], r_o2z.at[s, k], at_z(way))

    def spread(s, origin, k):
        for d in (1, 2, 3):
            send(o2(origin, y, s), o2(origin, y, s), s_o2y.at[s, k, d - 1], r_o2y.at[s, k, d - 1], at_y(d))

    def begin(s):
        for d in (1, 2, 3):
            send(o1_own(y, s), o1_own(y, s), s_o1y.at[s, d - 1], r_o1y.at[s, d - 1], at_y(d))
        hop(2, s, 1, 1)
        hop(2, s, -1, 1)
        spread(s, z, 0)

    def begin_z(s):
        for d in (1, 2, 3):
            await_at(o1_own(ys[(-d) % 4], s), s_o1y.at[s, d - 1], r_o1y.at[s, d - 1], at_y(d))
        hop(1, s, 1, 1)
        hop(1, s, -1, 1)

    def step(s, dist):
        for order in (1, 2):
            for way in (1, -1):
                if dist > limit(order, way):
                    continue
                origin = zs[(-way * dist) % 8]
                k = slot(order, way, dist)
                if order == 1:
                    await_at(o1(origin, s), s_o1z.at[s, k], r_o1z.at[s, k], at_z(way))
                else:
                    await_at(o2(origin, y, s), s_o2z.at[s, k], r_o2z.at[s, k], at_z(way))
                if dist < limit(order, way):
                    hop(order, s, way, dist + 1)
                if order == 2:
                    spread(s, origin, k + 1)

    def finish(s):
        for way, most in ((0, 1), (1, 3), (-1, 4)):
            for dist in range(1, most + 1):
                origin = zs[(-way * dist) % 8]
                k = 0 if way == 0 else slot(2, way, dist) + 1
                for d in (1, 2, 3):
                    await_at(
                        o2(origin, ys[(-d) % 4], s),
                        s_o2y.at[s, k, d - 1],
                        r_o2y.at[s, k, d - 1],
                        at_y(d),
                    )

    def top_hop(way, dist):
        origin = zs[(-way * (dist - 1)) % 8]
        k = slot(1, way, dist)
        send(tw.at[x, origin, y], tw.at[x, origin, y], s_tz.at[k], r_tz.at[k], at_z(way))

    def top_step(dist):
        for way in (1, -1):
            if dist > limit(1, way):
                continue
            origin = zs[(-way * dist) % 8]
            k = slot(1, way, dist)
            await_at(tw.at[x, origin, y], s_tz.at[k], r_tz.at[k], at_z(way))
            if dist < limit(1, way):
                top_hop(way, dist + 1)

    def top_y():
        for d in (1, 2, 3):
            send(tw.at[x, :, y], tw.at[x, :, y], s_ty.at[d - 1], r_ty.at[d - 1], at_y(d))

    def layer_of(xx, layer):
        return tw.at[xx, :, :, :, pl.ds(768 * layer, 768)]

    def top_x():
        for d in (1, 2, 3):
            yy = ys[(-d) % 4]
            await_at(tw.at[x, :, yy], s_ty.at[d - 1], r_ty.at[d - 1], at_y(d))
        for layer in range(2):
            for d in (1, 3, 2):
                ss, rs = s_tx.at[layer, d - 1], r_tx.at[layer, d - 1]
                send(layer_of(x, layer), layer_of(x, layer), ss, rs, at_x(d, c))

    def top_ready(layer):
        for d in (1, 2, 3):
            ss, rs = s_tx.at[layer, d - 1], r_tx.at[layer, d - 1]
            await_at(layer_of(xs[(-d) % 4], layer), ss, rs, at_x(d, c))

    def scatter(which):
        for d in range(1, 8):
            ss, rs = s_rs.at[which, d - 1], r_rs.at[which, d - 1]
            send(rs_send.at[which, ms[d]], rs_recv.at[which, m], ss, rs, at_m(d))
        rs_recv[which, m] = rs_send[which, m]

    def gathered_sum(which):
        for d in range(1, 8):
            ss, rs = s_rs.at[which, d - 1], r_rs.at[which, d - 1]
            await_at(rs_recv.at[which, ms[(-d) % 8]], ss, rs, at_m(d))
        total = rs_recv[which, 0].astype(F32)
        for j in range(1, 8):
            total = total + rs_recv[which, j].astype(F32)
        return total

    def share(which):
        for d in range(1, 8):
            ss, rs = s_ag.at[which, d - 1], r_ag.at[which, d - 1]
            send(mids.at[which, m], mids.at[which, m], ss, rs, at_m(d))

    def shared(which):
        for d in range(1, 8):
            ss, rs = s_ag.at[which, d - 1], r_ag.at[which, d - 1]
            await_at(mids.at[which, ms[(-d) % 8]], ss, rs, at_m(d))

    def swap(which, partial):
        swap_send[which] = partial.astype(BF)
        send(swap_send.at[which], swap_recv.at[which], s_swap.at[which], r_swap.at[which], at_x(0, other))

    def swapped(which):
        await_at(swap_recv.at[which], s_swap.at[which], r_swap.at[which], at_x(0, other))
        return swap_send[which].astype(F32) + swap_recv[which].astype(F32)

    top_hop(1, 1)
    top_hop(-1, 1)
    begin(0)
    for d in (1, 2, 3):
        send(tabs.at[x], tabs.at[x], s_tab.at[d - 1], r_tab.at[d - 1], at_x(d, c))

    for i in range(3):
        deep_x[24 * i : 24 * i + 24, :] = deep_ref[i].astype(F32)
    deep_x[USED:T, :] = jnp.zeros((T - USED, 2048), F32)
    begin_z(0)
    normed = norm_rows(deep_x[...], deep_gain_ref[0:1, :])

    deep_tab = thirds(deep_tab_ref[...])
    deep_iota = lax.broadcasted_iota(jnp.int32, (128, T), 0) + deep_keys_ref[0:1, :]

    def deep_row(n, carry):
        r = n // 24
        col = n - 24 * r
        want = (r + 2) * 11 + lax.rem(col, 6) + 5
        hot = jnp.where(deep_iota == want, 1.0, 0.0).astype(BF)
        got = dot(deep_tab, hot)
        deep_raw[n] = got[0:8] + got[8:16] + got[16:24]
        return carry

    lax.fori_loop(0, USED, deep_row, 0)
    top_step(1)
    step(0, 1)
    begin(1)
    for h in range(8):
        deep_bias[h * T : h * T + USED, :] = deep_raw[:, h, :] + mask_deep_ref[0:USED, :]
        deep_bias[h * T + USED : (h + 1) * T, :] = mask_deep_ref[USED:T, :]
    top_step(2)
    step(0, 2)
    begin_z(1)
    top_step(3)
    top_step(4)
    top_y()

    for d in (1, 2, 3):
        await_at(tabs.at[xs[(-d) % 4]], s_tab.at[d - 1], r_tab.at[d - 1], at_x(d, c))
    top_tab = thirds(tabs[...].reshape(32, 256))
    top_iota = lax.broadcasted_iota(jnp.int32, (256, EXT), 0) + keys_ref[0:1, :]

    def top_row(n, carry):
        i = n // 12
        want = (i + 5) * 23 + (n - 12 * i) + 11
        hot = jnp.where(top_iota == want, 1.0, 0.0).astype(BF)
        got = dot(top_tab, hot)
        top_raw[n] = got[0:32] + got[32:64] + got[64:96]
        return carry

    lax.fori_loop(0, 36, top_row, 0)
    step(0, 3)
    step(1, 1)
    begin(2)
    lax.fori_loop(36, USED, top_row, 0)
    step(0, 4)
    step(1, 2)
    begin_z(2)
    top_x()
    step_key = keys_ref[1:2, :]
    gone = ((step_key < 0) & (band == 0)) | ((step_key > 0) & (band == 31))
    mask_one = mask_one_ref[...] + jnp.where(gone, NEG, 0.0)
    for w in range(4):
        for h in range(2):
            g = (2 * w + h) * T
            bias_zero[g : g + USED, :] = top_raw[:, 8 * w + h, 0:T] + mask_zero_ref[0:USED, :]
            bias_zero[g + USED : g + T, :] = mask_zero_ref[USED:T, :]
            bias_one[g : g + USED, :] = top_raw[:, 8 * w + 2 + h, :] + mask_one[0:USED, :]
            bias_one[g + USED : g + T, :] = mask_one[USED:T, :]

    heads = heads_ref[...]
    finish(0)
    acc = jnp.zeros((T, 768), F32)
    for j in range(8):
        block = dw[j, :, :, :, 0:768].reshape(256, 768)
        acc = acc + dot(normed[:, 256 * j : 256 * j + 256], block)
    qkv = acc.astype(BF)
    mixed = attend(qkv[:, 0:256], qkv[:, 256:512], qkv[:, 512:768], deep_bias[...], heads)
    step(1, 3)
    for j in range(8):
        block = dw[j, :, :, :, 768:1024].reshape(256, 256)
        rs_send[0, j] = dot_t(mixed, block).astype(BF)
    scatter(0)
    step(2, 1)
    step(1, 4)
    column = pl.ds(pl.multiple_of(m * 256, 256), 256)
    mids[0, m] = (deep_x[:, column] + gathered_sum(0)).astype(BF)
    share(0)
    step(2, 2)
    shared(0)
    middle = jnp.concatenate([mids[0, j] for j in range(8)], axis=1).astype(F32)
    normed_two = norm_rows(middle, deep_gain_ref[1:2, :])
    finish(1)
    acc = jnp.zeros((T, 1024), F32)
    for j in range(8):
        block = dw[j, :, :, :, 1024:2048].reshape(256, 1024)
        acc = acc + dot(normed_two[:, 256 * j : 256 * j + 256], block)
    hidden = gelu(acc).astype(BF)
    step(2, 3)
    step(2, 4)
    own_skip = dot(pick_ref[x], skip_ref[...].reshape(288, 512))
    finish(2)
    for j in range(8):
        block = dw[j, :, :, :, 2048:3072].reshape(256, 1024)
        rs_send[1, j] = dot_t(hidden, block).astype(BF)
    scatter(1)
    mids[1, m] = (mids[0, m].astype(F32) + gathered_sum(1)).astype(BF)
    share(1)
    shared(1)
    acc = jnp.zeros((T, 256), F32)
    for j in range(8):
        acc = acc + dot(mids[1, j], dw[j, :, :, :, 3072:3328].reshape(256, 256))
    grown = acc.astype(BF)
    for w in range(4):
        chosen = dot(grow_ref[w], grown) * part_ref[...]
        piece = chosen[:, 0:64] + chosen[:, 64:128] + chosen[:, 128:192] + chosen[:, 192:256]
        grow_send[w] = jnp.concatenate([piece, jnp.zeros((T, 64), F32)], axis=1).astype(BF)
    for d in range(1, 8):
        send(grow_send.at[ms[d] // 2], grow_recv.at[m], s_grow.at[d - 1], r_grow.at[d - 1], at_m(d))
    grow_recv[m] = grow_send[x]
    for d in range(1, 8):
        await_at(grow_recv.at[ms[(-d) % 8]], s_grow.at[d - 1], r_grow.at[d - 1], at_m(d))
    window = jnp.concatenate([grow_recv[j][:, 0:64] for j in range(8)], axis=1)
    state = (own_skip + window.astype(F32)).astype(BF)

    for layer in range(2):
        top_ready(layer)
        base = 768 * layer
        normed = norm_rows(state.astype(F32), top_gain_ref[2 * layer : 2 * layer + 1, :])
        parts = []
        for w in range(4):
            block = tw[w, :, :, :, base : base + 256].reshape(512, 256)
            parts.append(dot(normed, block).astype(BF))
        q = jnp.concatenate([p[:, 0:64] for p in parts], axis=1)
        k = jnp.concatenate([p[:, 64:128] for p in parts], axis=1)
        v = jnp.concatenate([p[:, 128:192] for p in parts], axis=1)
        if layer == 0:
            mixed = attend(q, k, v, bias_zero[...], heads)
        else:
            kv = jnp.concatenate([k, v], axis=1)
            halo_send[...] = dot(take_ref[...], kv).astype(BF)
            halo[0:T, :] = kv
            for e, (band_step, x_step, r0, nr, c0, nc, off, size) in enumerate(PIECES):
                src = halo_send.at[pl.ds(off - T, size)]
                dst = halo.at[pl.ds(off, size)]
                send(src, dst, s_halo.at[e], r_halo.at[e], at_piece(-band_step, -x_step))
            for e, (band_step, x_step, r0, nr, c0, nc, off, size) in enumerate(PIECES):
                dst = halo.at[pl.ds(off, size)]
                await_at(dst, s_halo.at[e], r_halo.at[e], at_piece(-band_step, -x_step))
            mixed = attend(q, halo[:, 0:256], halo[:, 256:512], bias_one[...], heads)
        total = jnp.zeros((T, 512), F32)
        for w in range(4):
            block = tw[w, :, :, :, base : base + 256].reshape(512, 256)
            wide = jnp.concatenate([jnp.zeros((T, 192), BF), mixed[:, 64 * w : 64 * w + 64]], axis=1)
            total = total + dot_t(wide, block)
        swap(2 * layer, total)
        middle = (state.astype(F32) + swapped(2 * layer)).astype(BF)
        normed = norm_rows(middle.astype(F32), top_gain_ref[2 * layer + 1 : 2 * layer + 2, :])
        total = jnp.zeros((T, 512), F32)
        for w in range(4):
            block = tw[w, :, :, :, base + 256 : base + 512].reshape(512, 256)
            hidden = gelu(dot(normed, block)).astype(BF)
            total = total + dot_t(hidden, tw[w, :, :, :, base + 512 : base + 768].reshape(512, 256))
        swap(2 * layer + 1, total)
        state = (middle.astype(F32) + swapped(2 * layer + 1)).astype(BF)

    for half in range(2):
        fin[x, half] = state[:, 256 * half : 256 * half + 256]
    for d in (1, 2, 3):
        for e in range(2):
            core = lax.rem(c + e, 2)
            ss, rs = s_fin.at[d - 1, e], r_fin.at[d - 1, e]
            send(fin.at[x, c], fin.at[x, c], ss, rs, at_x(d, core))
    for d in (1, 2, 3):
        for e in range(2):
            core = lax.rem(c + e, 2)
            ss, rs = s_fin.at[d - 1, e], r_fin.at[d - 1, e]
            await_at(fin.at[xs[(-d) % 4], core], ss, rs, at_x(d, core))
    for half in range(2):
        stacked = jnp.concatenate([fin[w, half] for w in range(4)], axis=0)
        rows = dot(place_ref[...], stacked).astype(BF).reshape(6, 48, 256)
        out_ref[:, :, 256 * half : 256 * half + 256] = rows
    for cp in sends:
        cp.wait_send()


def local(
    skip_features,
    deep_features,
    top_gains,
    top_heads_in,
    top_heads_out,
    top_hidden_in,
    top_hidden_out,
    top_offsets,
    deep_gains,
    deep_offsets,
    deep_heads_in,
    deep_heads_out,
    deep_hidden_in,
    deep_hidden_out,
    expand_weight,
):
    deep_pack = jnp.concatenate(
        [
            deep_heads_in.reshape(64, 768),
            deep_heads_out.T,
            deep_hidden_in,
            deep_hidden_out.T,
            expand_weight.reshape(64, 256),
        ],
        axis=1,
    )
    top_pack = jnp.concatenate(
        [
            part
            for s in range(2)
            for part in (
                top_heads_in[s].reshape(16, 192),
                top_heads_out[s].T,
                top_hidden_in[s],
                top_hidden_out[s].T,
            )
        ],
        axis=1,
    )
    top_tab = jnp.pad(top_offsets.reshape(4, 253), ((0, 4), (0, 3)))
    deep_tab = jnp.pad(deep_offsets.reshape(8, 55), ((0, 0), (0, 73)))
    constants = [jnp.asarray(a) for a in tables()]
    operands = [
        skip_features,
        deep_features,
        top_gains.reshape(4, 512),
        deep_gains,
        top_tab,
        deep_tab,
        deep_pack,
        top_pack,
        *constants,
    ]
    dma = pltpu.SemaphoreType.DMA
    shapes = [(3, 3), (3, 7), (3, 7), (3, 8, 3), (7,), (3,), (2, 3), (3,), (2, 7), (2, 7), (7,), (4,), (8,), (3, 2)]
    vmem = pl.BlockSpec(memory_space=pltpu.VMEM)
    return pl.pallas_call(
        kernel,
        out_shape=jax.ShapeDtypeStruct((6, 48, 512), BF),
        in_specs=[vmem] * len(operands),
        out_specs=vmem,
        scratch_shapes=[
            pltpu.VMEM((8, 4, 2, 32, 3328), BF),
            pltpu.VMEM((4, 8, 4, 16, 1536), BF),
            pltpu.VMEM((4, 8, 256), F32),
            pltpu.VMEM((USED, 8, T), F32),
            pltpu.VMEM((8 * T, T), F32),
            pltpu.VMEM((USED, 32, EXT), F32),
            pltpu.VMEM((8 * T, T), F32),
            pltpu.VMEM((8 * T, EXT), F32),
            pltpu.VMEM((T, 2048), F32),
            pltpu.VMEM((2, 8, T, 256), BF),
            pltpu.VMEM((2, 8, T, 256), BF),
            pltpu.VMEM((2, 8, T, 256), BF),
            pltpu.VMEM((4, T, 128), BF),
            pltpu.VMEM((8, T, 128), BF),
            pltpu.VMEM((4, T, 512), BF),
            pltpu.VMEM((4, T, 512), BF),
            pltpu.VMEM((EXT - T, 512), BF),
            pltpu.VMEM((EXT, 512), BF),
            pltpu.VMEM((4, 2, T, 256), BF),
        ]
        + [dma(s) for s in shapes for _ in range(2)],
        compiler_params=pltpu.CompilerParams(
            collective_id=0, has_side_effects=True, vmem_limit_bytes=56 * 2**20
        ),
    )(*operands)


def solution(mesh):
    placed = (
        P("band", None, None),
        P("band", None, None),
        P(),
        P(None, "band", None, "mp"),
        P(None, "mp", "band"),
        P(None, "band", "mp"),
        P(None, "mp", "band"),
        P(None, "mp", None, None),
        P(),
        P("mp", None, None),
        P("band", None, "mp"),
        P("mp", "band"),
        P("band", "mp"),
        P("mp", "band"),
        P("band", None, "mp"),
    )
    return jax.shard_map(
        local, mesh=mesh, in_specs=placed, out_specs=P("band", None, None), check_vma=False
    )
```

```python
import functools

import jax
import jax.numpy as jnp
import numpy as np
from jax import lax
from jax.experimental import pallas as pl
from jax.experimental.pallas import tpu as pltpu
from jax.sharding import PartitionSpec as P

BF = jnp.bfloat16
F32 = jnp.float32
EPS = 1e-05
NEG = -1e30
T = 80
USED = 72
EXT = 400
SCALE = 32 ** (-0.5)
MESH = pl.DeviceIdType.MESH
BANDS = 4

PIECES = (
    (-1, 0, 3, 3, 0, 12, 80, 48),
    (1, 0, 0, 3, 0, 12, 128, 48),
    (0, -1, 0, 6, 6, 6, 176, 48),
    (0, 1, 0, 6, 0, 6, 224, 48),
    (-1, -1, 3, 3, 6, 6, 272, 32),
    (-1, 1, 3, 3, 0, 6, 304, 32),
    (1, -1, 0, 3, 6, 6, 336, 32),
    (1, 1, 0, 3, 0, 6, 368, 32),
)


@functools.lru_cache(None)
def tables():
    key_row = np.zeros(EXT, np.int32)
    key_col = np.zeros(EXT, np.int32)
    key_ok = np.zeros(EXT, bool)
    key_step = np.zeros(EXT, np.int32)
    t = np.arange(USED)
    key_row[:USED], key_col[:USED], key_ok[:USED] = t // 12, t % 12, True
    take = np.zeros((EXT, T), np.float32)
    for band_step, x_step, r0, nr, c0, nc, off, _ in PIECES:
        p = np.arange(nr * nc)
        r, c = r0 + p // nc, c0 + p % nc
        key_row[off : off + nr * nc] = r + 6 * band_step
        key_col[off : off + nr * nc] = c + 12 * x_step
        key_ok[off : off + nr * nc] = True
        key_step[off : off + nr * nc] = band_step
        take[off + p, r * 12 + c] = 1.0
    keys = np.zeros((8, EXT), np.int32)
    keys[0] = np.where(key_ok, 23 * key_row + key_col, -100000)
    keys[1] = key_step
    q_row, q_col = np.zeros(T, np.int32), np.zeros(T, np.int32)
    q_row[:USED], q_col[:USED] = t // 12, t % 12
    same = ((q_row >= 3)[:, None] == (key_row >= 3)[None]) & (
        (q_col >= 6)[:, None] == (key_col >= 6)[None]
    )
    mask_one = np.where(same & key_ok[None], 0.0, NEG).astype(np.float32)
    mask_zero = np.where((np.arange(T) < USED)[None], 0.0, NEG).astype(np.float32)
    mask_zero = np.broadcast_to(mask_zero, (T, T)).copy()
    deep_row, deep_col = np.zeros(T, np.int32), np.zeros(T, np.int32)
    deep_row[:USED], deep_col[:USED] = t // 24, t % 24
    deep_keys = np.full((8, T), -100000, np.int32)
    deep_keys[:, :USED] = 11 * deep_row[:USED] + deep_col[:USED] % 6
    ok = (np.arange(T) < USED)[None] & ((deep_col // 6)[:, None] == (deep_col // 6)[None])
    mask_deep = np.where(ok, 0.0, NEG).astype(np.float32)
    grow = np.zeros((4, T, T), np.float32)
    part = np.zeros((T, 4), np.float32)
    i, k = t // 12, t % 12
    for w in range(4):
        grow[w, t, (i // 2) * 24 + 6 * w + k // 2] = 1.0
    part[t, 2 * (i % 2) + k % 2] = 1.0
    part = np.repeat(part[:, :, None], 64, axis=2).reshape(T, 256)
    pick = np.zeros((4, T, 288), np.float32)
    place = np.zeros((288, 4 * T), np.float32)
    for w in range(4):
        pick[w, t, i * 48 + 12 * w + k] = 1.0
        place[i * 48 + 12 * w + k, w * T + t] = 1.0
    heads = np.zeros((8 * T, 256), np.float32)
    for h in range(8):
        heads[h * T : (h + 1) * T, h * 32 : (h + 1) * 32] = 1.0
    return (
        keys,
        mask_one,
        mask_zero,
        deep_keys,
        mask_deep,
        grow.astype(jnp.bfloat16),
        part,
        pick.astype(jnp.bfloat16),
        place.astype(jnp.bfloat16),
        take[T:].astype(jnp.bfloat16),
        heads.astype(jnp.bfloat16),
    )


def dot(a, b):
    return jnp.dot(a, b, preferred_element_type=F32)


def dot_t(a, b):
    return lax.dot_general(a, b, (((1,), (1,)), ((), ())), preferred_element_type=F32)


def thirds(values):
    first = values.astype(BF)
    rest = values - first.astype(F32)
    second = rest.astype(BF)
    third = (rest - second.astype(F32)).astype(BF)
    return jnp.concatenate([first, second, third], axis=0)


def norm_rows(values, scales):
    centred = values - jnp.mean(values, axis=-1, keepdims=True)
    spread = jnp.mean(centred * centred, axis=-1, keepdims=True)
    return (centred * lax.rsqrt(spread + EPS) * scales).astype(BF)


def gelu(values):
    return values * 0.5 * (1.0 + lax.erf(values * (0.5**0.5)))


def attend(q, k, v, bias, heads):
    count = heads.shape[0] // T
    stacked = jnp.concatenate([q] * count, axis=0) * heads
    scores = dot_t(stacked, k) * SCALE + bias
    weights = jnp.exp(scores - jnp.max(scores, axis=-1, keepdims=True))
    weights = (weights * (1.0 / jnp.sum(weights, axis=-1, keepdims=True))).astype(BF)
    mixed = dot(weights, v) * heads.astype(F32)
    total = mixed[0:T]
    for h in range(1, count):
        total = total + mixed[h * T : (h + 1) * T]
    return total.astype(BF)


def kernel(
    skip_ref,
    deep_ref,
    top_gain_ref,
    deep_gain_ref,
    top_tab_ref,
    deep_tab_ref,
    heads_in_ref,
    heads_out_ref,
    hidden_in_ref,
    hidden_out_ref,
    expand_ref,
    top_heads_in_ref,
    top_heads_out_ref,
    top_hidden_in_ref,
    top_hidden_out_ref,
    keys_ref,
    mask_one_ref,
    mask_zero_ref,
    deep_keys_ref,
    mask_deep_ref,
    grow_ref,
    part_ref,
    pick_ref,
    place_ref,
    take_ref,
    heads_ref,
    out_ref,
    dw,
    quarters,
    tw,
    tabs,
    deep_raw,
    deep_bias,
    top_raw,
    bias_zero,
    bias_one,
    deep_x,
    deep_n,
    rs_send,
    rs_core,
    rs_mid,
    rs_recv,
    mids,
    outs,
    grow_send,
    grow_recv,
    swap_send,
    swap_recv,
    halo_send,
    halo,
    fin,
    s_q,
    r_q,
    s_z,
    r_z,
    s_n,
    r_n,
    s_ez,
    r_ez,
    s_ey,
    r_ey,
    s_ef,
    r_ef,
    s_tz,
    r_tz,
    s_tf,
    r_tf,
    s_tg,
    r_tg,
    s_tab,
    r_tab,
    s_core,
    r_core,
    s_rs,
    r_rs,
    s_ag,
    r_ag,
    s_mid,
    r_mid,
    s_out,
    r_out,
    s_grow,
    r_grow,
    s_swap,
    r_swap,
    s_halo,
    r_halo,
    s_fin,
    r_fin,
):
    band = lax.axis_index("band")
    m = lax.axis_index("mp")
    z, y, x, c = band // 4, band % 4, m // 2, m % 2
    zs = [lax.rem(z + d, 8) for d in range(8)]
    ys = [lax.rem(y + d, 4) for d in range(4)]
    xs = [lax.rem(x + d, 4) for d in range(4)]
    ms = [lax.rem(m + d, 8) for d in range(8)]
    other = 1 - c

    def at_z(d):
        return {"band": zs[d % 8] * 4 + y, "mp": m}

    def at_y(d):
        return {"band": z * 4 + ys[d % 4], "mp": m}

    def at_m(d):
        return {"band": band, "mp": ms[d % 8]}

    def at_plane(dx, dy):
        return {"band": z * 4 + ys[dy % 4], "mp": xs[dx % 4] * 2 + c}

    def at_x(d, core):
        return {"band": band, "mp": xs[d % 4] * 2 + core}

    def at_piece(band_step, x_step):
        return {"band": lax.rem(band + band_step + 32, 32), "mp": xs[x_step % 4] * 2 + c}

    barrier = pltpu.get_barrier_semaphore()
    greeted = [at_z(1), at_z(7)] + [at_m(d) for d in range(1, 8)]
    greeted += [at_plane(dx, dy) for dy in (1, 2, 3) for dx in range(4)]
    greeted += [at_piece(b, d) for b in (-1, 1) for d in (-1, 0, 1)]
    for who in greeted:
        pl.semaphore_signal(barrier, inc=1, device_id=who, device_id_type=MESH)

    sends = []

    def copy(src, dst, ss, rs, who):
        return pltpu.make_async_remote_copy(
            src_ref=src, dst_ref=dst, send_sem=ss, recv_sem=rs, device_id=who, device_id_type=MESH
        )

    def send(src, dst, ss, rs, who):
        cp = copy(src, dst, ss, rs, who)
        cp.start()
        sends.append(cp)

    def await_at(dst, ss, rs, who):
        copy(dst, dst, ss, rs, who).wait_recv()

    for yy in range(BANDS):
        lanes = slice(64 * yy, 64 * yy + 64)
        quarters[yy, :, 0:256] = jnp.concatenate(
            [heads_in_ref[0, :, lanes], heads_in_ref[1, :, lanes], heads_in_ref[2, :, lanes], heads_out_ref[:, lanes]],
            axis=1,
        )
        lanes = slice(256 * yy, 256 * yy + 256)
        quarters[yy, :, 256:512] = hidden_in_ref[:, lanes]
        quarters[yy, :, 512:768] = hidden_out_ref[:, lanes]
    dw[z, y, :, 0:768] = quarters[y]
    dw[z, y, :, 768:1024] = expand_ref[...]
    for layer in range(2):
        pieces = [top_heads_in_ref[layer, i] for i in range(3)] + [top_heads_out_ref[layer]]
        pieces += [top_hidden_in_ref[layer], top_hidden_out_ref[layer]]
        tw[x, z, y, :, 768 * layer : 768 * layer + 768] = jnp.concatenate(pieces, axis=1)
    tabs[x] = jnp.zeros((8, 256), F32)
    for layer in range(2):
        flat = jnp.concatenate([top_tab_ref[layer, a] for a in range(11)] + [jnp.zeros((2, 3), F32)], axis=1)
        tabs[x, 2 * layer : 2 * layer + 2, :] = flat
    pl.semaphore_wait(barrier, len(greeted))

    def plane(zz, s, part=None):
        yy = pl.ds(0, 4) if part is None else pl.ds(2 * part, 2)
        return dw.at[zz, yy, :, pl.ds(256 * s, 256)]

    def own(yy, s):
        return dw.at[z, yy, :, pl.ds(256 * s, 256)]

    def slot(way, dist):
        return dist - 1 if way > 0 else 3 + dist

    def part_of(way, dist):
        return None if dist < 4 else (0 if way > 0 else 1)

    def hop(s, way, dist):
        ref = plane(zs[(-way * (dist - 1)) % 8], s, part_of(way, dist))
        k = slot(way, dist)
        send(ref, ref, s_z.at[s, k], r_z.at[s, k], at_z(way))

    def begin(s):
        for d in (1, 3, 2):
            src = quarters.at[ys[d], :, pl.ds(256 * s, 256)]
            send(src, own(y, s), s_q.at[s, d - 1], r_q.at[s, d - 1], at_y(d))

    def begin_z(s):
        for d in (1, 3, 2):
            await_at(own(ys[(-d) % 4], s), s_q.at[s, d - 1], r_q.at[s, d - 1], at_y(d))
        hop(s, 1, 1)
        hop(s, -1, 1)

    def step(s, dist):
        for way in (1, -1):
            k = slot(way, dist)
            ref = plane(zs[(-way * dist) % 8], s, part_of(way, dist))
            await_at(ref, s_z.at[s, k], r_z.at[s, k], at_z(way))
            if dist < 4:
                hop(s, way, dist + 1)

    def expand_part(zz, part=None):
        rows = pl.ds(0, 64) if part is None else pl.ds(32 * part, 32)
        return dw.at[zz, y, rows, pl.ds(768, 256)]

    def top_part(zz, part=None):
        lanes = pl.ds(0, 1536) if part is None else pl.ds(768 * part, 768)
        return tw.at[x, zz, y, :, lanes]

    def top_hop(way, dist):
        origin, k, part = zs[(-way * (dist - 1)) % 8], slot(way, dist), part_of(way, dist)
        ref = top_part(origin, part)
        send(ref, ref, s_tz.at[k], r_tz.at[k], at_z(way))
        ref = expand_part(origin, part)
        send(ref, ref, s_ez.at[k], r_ez.at[k], at_z(way))

    def top_step(dist):
        for way in (1, -1):
            origin, k, part = zs[(-way * dist) % 8], slot(way, dist), part_of(way, dist)
            await_at(top_part(origin, part), s_tz.at[k], r_tz.at[k], at_z(way))
            await_at(expand_part(origin, part), s_ez.at[k], r_ez.at[k], at_z(way))
            if dist < 4:
                top_hop(way, dist + 1)

    def expand_of(yy, half=None):
        zz = pl.ds(0, 8) if half is None else pl.ds(4 * half, 4)
        return dw.at[zz, yy, :, pl.ds(768, 256)]

    def top_of(layer, xx, yy, half=None):
        zz = pl.ds(0, 8) if half is None else pl.ds(4 * half, 4)
        xx = pl.ds(0, 4) if xx is None else xx
        yy = pl.ds(0, 4) if yy is None else yy
        return tw.at[xx, zz, yy, :, pl.ds(768 * layer, 768)]

    def top_ref(layer, phase, d, half=None):
        along_y = (layer == 0) == (phase == 0)
        if along_y:
            return top_of(layer, x if phase == 0 else None, ys[d % 4], half)
        return top_of(layer, xs[d % 4], y if phase == 0 else None, half)

    def top_who(layer, phase, d):
        return at_y(d) if (layer == 0) == (phase == 0) else at_x(d, c)

    def top_send(layer, phase):
        ref = top_ref(layer, phase, 0)
        for e, d in enumerate((1, 3)):
            ss, rs = s_tf.at[layer, phase, e], r_tf.at[layer, phase, e]
            send(ref, ref, ss, rs, top_who(layer, phase, d))

    def top_relay(layer, phase):
        for e, d in enumerate((1, 3)):
            ss, rs = s_tf.at[layer, phase, e], r_tf.at[layer, phase, e]
            await_at(top_ref(layer, phase, -d), ss, rs, top_who(layer, phase, d))
            half = top_ref(layer, phase, -d, e)
            ss, rs = s_tg.at[layer, phase, e], r_tg.at[layer, phase, e]
            send(half, half, ss, rs, top_who(layer, phase, d))

    def top_ready(layer, phase):
        for e, d in enumerate((1, 3)):
            ss, rs = s_tg.at[layer, phase, e], r_tg.at[layer, phase, e]
            await_at(top_ref(layer, phase, 2, e), ss, rs, top_who(layer, phase, d))

    def expand_send():
        for e, d in enumerate((1, 3)):
            send(expand_of(y), expand_of(y), s_ey.at[e], r_ey.at[e], at_y(d))

    def expand_relay():
        for e, d in enumerate((1, 3)):
            yy = ys[4 - d]
            await_at(expand_of(yy), s_ey.at[e], r_ey.at[e], at_y(d))
            send(expand_of(yy, e), expand_of(yy, e), s_ef.at[e], r_ef.at[e], at_y(d))

    def expand_ready():
        for e, d in enumerate((1, 3)):
            await_at(expand_of(ys[2], e), s_ef.at[e], r_ef.at[e], at_y(d))

    steps = [(dx, dy) for dy in range(4) for dx in range(4) if dx or dy]

    def scatter(which):
        ss, rs = s_core.at[which], r_core.at[which]
        send(rs_send.at[which, other], rs_core.at[which], ss, rs, at_x(0, other))
        await_at(rs_core.at[which], ss, rs, at_x(0, other))
        rs_mid[which] = (rs_send[which, c].astype(F32) + rs_core[which].astype(F32)).astype(BF)
        for e, (dx, dy) in enumerate(steps):
            ss, rs = s_rs.at[which, e], r_rs.at[which, e]
            send(rs_mid.at[which, xs[dx], ys[dy]], rs_recv.at[which, x, y], ss, rs, at_plane(dx, dy))
        rs_recv[which, x, y] = rs_mid[which, x, y]

    def gathered_sum(which):
        for e, (dx, dy) in enumerate(steps):
            dst = rs_recv.at[which, xs[(-dx) % 4], ys[(-dy) % 4]]
            await_at(dst, s_rs.at[which, e], r_rs.at[which, e], at_plane(dx, dy))
        total = rs_recv[which, 0, 0].astype(F32)
        for j in range(1, 16):
            total = total + rs_recv[which, j // 4, j % 4].astype(F32)
        return total

    def share():
        for e, (dx, dy) in enumerate(steps):
            ref = mids.at[c, x, y]
            send(ref, ref, s_ag.at[e], r_ag.at[e], at_plane(dx, dy))

    def shared():
        for e, (dx, dy) in enumerate(steps):
            dst = mids.at[c, xs[(-dx) % 4], ys[(-dy) % 4]]
            await_at(dst, s_ag.at[e], r_ag.at[e], at_plane(dx, dy))
        send(mids.at[c], mids.at[c], s_mid.at[0], r_mid.at[0], at_x(0, other))
        await_at(mids.at[other], s_mid.at[0], r_mid.at[0], at_x(0, other))

    def share_out():
        for d in range(1, 8):
            send(outs.at[m], outs.at[m], s_out.at[d - 1], r_out.at[d - 1], at_m(d))

    def shared_out():
        for d in range(1, 8):
            await_at(outs.at[ms[(-d) % 8]], s_out.at[d - 1], r_out.at[d - 1], at_m(d))

    def swap(which, partial):
        swap_send[which] = partial.astype(BF)
        send(swap_send.at[which], swap_recv.at[which], s_swap.at[which], r_swap.at[which], at_x(0, other))

    def swapped(which):
        await_at(swap_recv.at[which], s_swap.at[which], r_swap.at[which], at_x(0, other))
        return swap_send[which].astype(F32) + swap_recv[which].astype(F32)

    begin(0)
    top_hop(1, 1)
    top_hop(-1, 1)
    for d in (1, 2, 3):
        send(tabs.at[x], tabs.at[x], s_tab.at[d - 1], r_tab.at[d - 1], at_x(d, c))

    for i in range(3):
        deep_x[24 * i : 24 * i + 24, :] = deep_ref[i].astype(F32)
    deep_x[USED:T, :] = jnp.zeros((T - USED, 2048), F32)
    deep_n[y] = norm_rows(deep_x[...], deep_gain_ref[0:1, :])
    for d in (1, 3, 2):
        send(deep_n.at[y], deep_n.at[y], s_n.at[d - 1], r_n.at[d - 1], at_y(d))
    begin(1)
    begin(2)
    begin_z(0)

    flat = jnp.concatenate([deep_tab_ref[a] for a in range(5)] + [jnp.zeros((8, 73), F32)], axis=1)
    deep_tab = thirds(flat)
    deep_iota = lax.broadcasted_iota(jnp.int32, (128, T), 0) + deep_keys_ref[0:1, :]

    def deep_rows(g, carry):
        for e in range(8):
            n = 8 * g + e
            r = n // 24
            col = n - 24 * r
            want = (r + 2) * 11 + lax.rem(col, 6) + 5
            hot = jnp.where(deep_iota == want, 1.0, 0.0).astype(BF)
            got = dot(deep_tab, hot)
            deep_raw[n] = got[0:8] + got[8:16] + got[16:24]
        return carry

    lax.fori_loop(0, 5, deep_rows, 0)
    step(0, 1)
    begin_z(1)
    top_step(1)
    lax.fori_loop(5, 9, deep_rows, 0)
    step(0, 2)
    top_step(2)
    for h in range(8):
        deep_bias[h * T : h * T + USED, :] = deep_raw[:, h, :] + mask_deep_ref[0:USED, :]
        deep_bias[h * T + USED : (h + 1) * T, :] = mask_deep_ref[USED:T, :]
    step(0, 3)
    top_step(3)
    step(1, 1)

    for d in (1, 2, 3):
        await_at(tabs.at[xs[(-d) % 4]], s_tab.at[d - 1], r_tab.at[d - 1], at_x(d, c))
    top_tab = thirds(tabs[...].reshape(32, 256))
    top_iota = lax.broadcasted_iota(jnp.int32, (256, EXT), 0) + keys_ref[0:1, :]

    def top_rows(g, carry):
        for e in range(4):
            n = 4 * g + e
            i = n // 12
            want = (i + 5) * 23 + (n - 12 * i) + 11
            hot = jnp.where(top_iota == want, 1.0, 0.0).astype(BF)
            got = dot(top_tab, hot)
            top_raw[n] = got[0:32] + got[32:64] + got[64:96]
        return carry

    step(0, 4)
    top_step(4)
    top_send(0, 0)
    top_send(1, 0)
    expand_send()
    begin_z(2)
    step(1, 2)
    for d in (1, 3, 2):
        await_at(deep_n.at[ys[(-d) % 4]], s_n.at[d - 1], r_n.at[d - 1], at_y(d))

    acc = jnp.zeros((BANDS * T, 256), F32)
    for j in range(8):
        block = dw[j, :, :, 0:256].reshape(256, 256)
        acc = acc + dot(deep_n[:, :, 256 * j : 256 * j + 256].reshape(BANDS * T, 256), block)
    qkv = acc.astype(BF)
    bias = deep_bias[pl.ds(pl.multiple_of(y * 2 * T, 2 * T), 2 * T), :]
    two = heads_ref[0 : 2 * T, 0:64]
    mixed = []
    for b in range(BANDS):
        rows = qkv[b * T : (b + 1) * T]
        mixed.append(attend(rows[:, 0:64], rows[:, 64:128], rows[:, 128:192], bias, two))
    mixed = jnp.concatenate(mixed, axis=0)
    wide = jnp.concatenate([jnp.zeros((BANDS * T, 192), BF), mixed], axis=1)
    for j in range(8):
        got = dot_t(wide, dw[j, :, :, 0:256].reshape(256, 256)).astype(BF)
        rs_send[0, j % 2, j // 2] = got.reshape(BANDS, T, 256)
    scatter(0)
    top_relay(0, 0)
    top_relay(1, 0)
    step(2, 1)
    step(1, 3)
    top_ready(0, 0)
    top_send(0, 1)
    top_ready(1, 0)
    expand_relay()
    lax.fori_loop(0, 9, top_rows, 0)
    column = pl.ds(pl.multiple_of(m * 256, 256), 256)
    mids[c, x, y] = (deep_x[:, column] + gathered_sum(0)).astype(BF)
    share()
    step(2, 2)
    step(1, 4)
    top_send(1, 1)
    step(2, 3)
    lax.fori_loop(9, 18, top_rows, 0)
    step(2, 4)
    step_key = keys_ref[1:2, :]
    gone = ((step_key < 0) & (band == 0)) | ((step_key > 0) & (band == 31))
    mask_one = mask_one_ref[...] + jnp.where(gone, NEG, 0.0)
    for w in range(4):
        for h in range(2):
            g = (2 * w + h) * T
            bias_zero[g : g + USED, :] = top_raw[:, 8 * w + h, 0:T] + mask_zero_ref[0:USED, :]
            bias_zero[g + USED : g + T, :] = mask_zero_ref[USED:T, :]
            bias_one[g : g + USED, :] = top_raw[:, 8 * w + 2 + h, :] + mask_one[0:USED, :]
            bias_one[g + USED : g + T, :] = mask_one[USED:T, :]
    heads = heads_ref[...]
    own_skip = dot(pick_ref[x], skip_ref[...].reshape(288, 512))
    shared()
    normed_two = []
    for b in range(BANDS):
        middle = jnp.concatenate([mids[j % 2, j // 2, b] for j in range(8)], axis=1).astype(F32)
        normed_two.append(norm_rows(middle, deep_gain_ref[1:2, :]))
    normed_two = jnp.concatenate(normed_two, axis=0)
    acc = jnp.zeros((BANDS * T, 256), F32)
    for j in range(8):
        block = dw[j, :, :, 256:512].reshape(256, 256)
        acc = acc + dot(normed_two[:, 256 * j : 256 * j + 256], block)
    hidden = gelu(acc).astype(BF)
    for j in range(8):
        got = dot_t(hidden, dw[j, :, :, 512:768].reshape(256, 256)).astype(BF)
        rs_send[1, j % 2, j // 2] = got.reshape(BANDS, T, 256)
    scatter(1)
    top_relay(0, 1)
    expand_ready()
    outs[m] = (mids[c, x, y].astype(F32) + gathered_sum(1)).astype(BF)
    share_out()
    top_relay(1, 1)
    shared_out()
    acc = jnp.zeros((T, 256), F32)
    for j in range(8):
        acc = acc + dot(outs[j], dw[j, :, :, 768:1024].reshape(256, 256))
    grown = acc.astype(BF)
    for w in range(4):
        chosen = dot(grow_ref[w], grown) * part_ref[...]
        piece = chosen[:, 0:64] + chosen[:, 64:128] + chosen[:, 128:192] + chosen[:, 192:256]
        grow_send[w] = jnp.concatenate([piece, jnp.zeros((T, 64), F32)], axis=1).astype(BF)
    for d in range(1, 8):
        send(grow_send.at[ms[d] // 2], grow_recv.at[m], s_grow.at[d - 1], r_grow.at[d - 1], at_m(d))
    grow_recv[m] = grow_send[x]
    for d in range(1, 8):
        await_at(grow_recv.at[ms[(-d) % 8]], s_grow.at[d - 1], r_grow.at[d - 1], at_m(d))
    window = jnp.concatenate([grow_recv[j][:, 0:64] for j in range(8)], axis=1)
    state = (own_skip + window.astype(F32)).astype(BF)

    for layer in range(2):
        top_ready(layer, 1)
        base = 768 * layer
        normed = norm_rows(state.astype(F32), top_gain_ref[layer, 0:1, :])
        parts = []
        for w in range(4):
            block = tw[w, :, :, :, base : base + 256].reshape(512, 256)
            parts.append(dot(normed, block).astype(BF))
        q = jnp.concatenate([p[:, 0:64] for p in parts], axis=1)
        k = jnp.concatenate([p[:, 64:128] for p in parts], axis=1)
        v = jnp.concatenate([p[:, 128:192] for p in parts], axis=1)
        if layer == 0:
            mixed = attend(q, k, v, bias_zero[...], heads)
        else:
            kv = jnp.concatenate([k, v], axis=1)
            halo_send[...] = dot(take_ref[...], kv).astype(BF)
            halo[0:T, :] = kv
            for e, (band_step, x_step, r0, nr, c0, nc, off, size) in enumerate(PIECES):
                src = halo_send.at[pl.ds(off - T, size)]
                dst = halo.at[pl.ds(off, size)]
                send(src, dst, s_halo.at[e], r_halo.at[e], at_piece(-band_step, -x_step))
            for e, (band_step, x_step, r0, nr, c0, nc, off, size) in enumerate(PIECES):
                dst = halo.at[pl.ds(off, size)]
                await_at(dst, s_halo.at[e], r_halo.at[e], at_piece(-band_step, -x_step))
            mixed = attend(q, halo[:, 0:256], halo[:, 256:512], bias_one[...], heads)
        total = jnp.zeros((T, 512), F32)
        for w in range(4):
            block = tw[w, :, :, :, base : base + 256].reshape(512, 256)
            wide = jnp.concatenate([jnp.zeros((T, 192), BF), mixed[:, 64 * w : 64 * w + 64]], axis=1)
            total = total + dot_t(wide, block)
        swap(2 * layer, total)
        middle = (state.astype(F32) + swapped(2 * layer)).astype(BF)
        normed = norm_rows(middle.astype(F32), top_gain_ref[layer, 1:2, :])
        total = jnp.zeros((T, 512), F32)
        for w in range(4):
            block = tw[w, :, :, :, base + 256 : base + 512].reshape(512, 256)
            hidden = gelu(dot(normed, block)).astype(BF)
            total = total + dot_t(hidden, tw[w, :, :, :, base + 512 : base + 768].reshape(512, 256))
        swap(2 * layer + 1, total)
        state = (middle.astype(F32) + swapped(2 * layer + 1)).astype(BF)

    for half in range(2):
        fin[x, half] = state[:, 256 * half : 256 * half + 256]
    for d in (1, 2, 3):
        for e in range(2):
            core = lax.rem(c + e, 2)
            ss, rs = s_fin.at[d - 1, e], r_fin.at[d - 1, e]
            send(fin.at[x, c], fin.at[x, c], ss, rs, at_x(d, core))
    for d in (1, 2, 3):
        for e in range(2):
            core = lax.rem(c + e, 2)
            ss, rs = s_fin.at[d - 1, e], r_fin.at[d - 1, e]
            await_at(fin.at[xs[(-d) % 4], core], ss, rs, at_x(d, core))
    for half in range(2):
        stacked = jnp.concatenate([fin[w, half] for w in range(4)], axis=0)
        rows = dot(place_ref[...], stacked).astype(BF).reshape(6, 48, 256)
        out_ref[:, :, 256 * half : 256 * half + 256] = rows
    for cp in sends:
        cp.wait_send()


def local(
    skip_features,
    deep_features,
    top_gains,
    top_heads_in,
    top_heads_out,
    top_hidden_in,
    top_hidden_out,
    top_offsets,
    deep_gains,
    deep_offsets,
    deep_heads_in,
    deep_heads_out,
    deep_hidden_in,
    deep_hidden_out,
    expand_weight,
):
    constants = [jnp.asarray(a) for a in tables()]
    operands = [
        skip_features,
        deep_features,
        top_gains,
        deep_gains,
        top_offsets.transpose(0, 2, 1, 3),
        deep_offsets.transpose(1, 0, 2),
        deep_heads_in.transpose(1, 0, 2),
        deep_heads_out.T,
        deep_hidden_in,
        deep_hidden_out.T,
        expand_weight.reshape(64, 256),
        top_heads_in.transpose(0, 2, 1, 3),
        top_heads_out.transpose(0, 2, 1),
        top_hidden_in,
        top_hidden_out.transpose(0, 2, 1),
        *constants,
    ]
    dma = pltpu.SemaphoreType.DMA
    shapes = [(3, 3), (3, 8), (3,), (8,), (2,), (2,), (8,), (2, 2, 2), (2, 2, 2), (3,)]
    shapes += [(2,), (2, 15), (15,), (1,), (7,), (7,), (4,), (8,), (3, 2)]
    vmem = pl.BlockSpec(memory_space=pltpu.VMEM)
    return pl.pallas_call(
        kernel,
        out_shape=jax.ShapeDtypeStruct((6, 48, 512), BF),
        in_specs=[vmem] * len(operands),
        out_specs=vmem,
        scratch_shapes=[
            pltpu.VMEM((8, 4, 64, 1024), BF),
            pltpu.VMEM((4, 64, 768), BF),
            pltpu.VMEM((4, 8, 4, 16, 1536), BF),
            pltpu.VMEM((4, 8, 256), F32),
            pltpu.VMEM((USED, 8, T), F32),
            pltpu.VMEM((8 * T, T), F32),
            pltpu.VMEM((USED, 32, EXT), F32),
            pltpu.VMEM((8 * T, T), F32),
            pltpu.VMEM((8 * T, EXT), F32),
            pltpu.VMEM((T, 2048), F32),
            pltpu.VMEM((BANDS, T, 2048), BF),
            pltpu.VMEM((2, 2, 4, BANDS, T, 256), BF),
            pltpu.VMEM((2, 4, BANDS, T, 256), BF),
            pltpu.VMEM((2, 4, BANDS, T, 256), BF),
            pltpu.VMEM((2, 4, BANDS, T, 256), BF),
            pltpu.VMEM((2, 4, BANDS, T, 256), BF),
            pltpu.VMEM((8, T, 256), BF),
            pltpu.VMEM((4, T, 128), BF),
            pltpu.VMEM((8, T, 128), BF),
            pltpu.VMEM((4, T, 512), BF),
            pltpu.VMEM((4, T, 512), BF),
            pltpu.VMEM((EXT - T, 512), BF),
            pltpu.VMEM((EXT, 512), BF),
            pltpu.VMEM((4, 2, T, 256), BF),
        ]
        + [dma(s) for s in shapes for _ in range(2)],
        compiler_params=pltpu.CompilerParams(
            collective_id=0, has_side_effects=True, vmem_limit_bytes=56 * 2**20
        ),
    )(*operands)


def solution(mesh):
    placed = (
        P("band", None, None),
        P("band", None, None),
        P(),
        P(None, "band", None, "mp"),
        P(None, "mp", "band"),
        P(None, "band", "mp"),
        P(None, "mp", "band"),
        P(None, "mp", None, None),
        P(),
        P("mp", None, None),
        P("band", None, "mp"),
        P("mp", "band"),
        P("band", "mp"),
        P("mp", "band"),
        P("band", None, "mp"),
    )
    return jax.shard_map(
        local, mesh=mesh, in_specs=placed, out_specs=P("band", None, None), check_vma=False
    )
```

```python
import functools

import jax
import jax.numpy as jnp
import numpy as np
from jax import lax
from jax.experimental import pallas as pl
from jax.experimental.pallas import tpu as pltpu
from jax.sharding import PartitionSpec as P

BF = jnp.bfloat16
F32 = jnp.float32
EPS = 1e-05
NEG = -1e30
T = 80
USED = 72
EXT = 400
SCALE = 32 ** (-0.5)
MESH = pl.DeviceIdType.MESH
BANDS = 4

PIECES = (
    (-1, 0, 3, 3, 0, 12, 80, 48),
    (1, 0, 0, 3, 0, 12, 128, 48),
    (0, -1, 0, 6, 6, 6, 176, 48),
    (0, 1, 0, 6, 0, 6, 224, 48),
    (-1, -1, 3, 3, 6, 6, 272, 32),
    (-1, 1, 3, 3, 0, 6, 304, 32),
    (1, -1, 0, 3, 6, 6, 336, 32),
    (1, 1, 0, 3, 0, 6, 368, 32),
)


@functools.lru_cache(None)
def tables():
    key_row = np.zeros(EXT, np.int32)
    key_col = np.zeros(EXT, np.int32)
    key_ok = np.zeros(EXT, bool)
    key_step = np.zeros(EXT, np.int32)
    t = np.arange(USED)
    key_row[:USED], key_col[:USED], key_ok[:USED] = t // 12, t % 12, True
    take = np.zeros((EXT, T), np.float32)
    for band_step, x_step, r0, nr, c0, nc, off, _ in PIECES:
        p = np.arange(nr * nc)
        r, c = r0 + p // nc, c0 + p % nc
        key_row[off : off + nr * nc] = r + 6 * band_step
        key_col[off : off + nr * nc] = c + 12 * x_step
        key_ok[off : off + nr * nc] = True
        key_step[off : off + nr * nc] = band_step
        take[off + p, r * 12 + c] = 1.0
    keys = np.zeros((8, EXT), np.int32)
    keys[0] = np.where(key_ok, 23 * key_row + key_col, -100000)
    keys[1] = key_step
    q_row, q_col = np.zeros(T, np.int32), np.zeros(T, np.int32)
    q_row[:USED], q_col[:USED] = t // 12, t % 12
    same = ((q_row >= 3)[:, None] == (key_row >= 3)[None]) & (
        (q_col >= 6)[:, None] == (key_col >= 6)[None]
    )
    mask_one = np.where(same & key_ok[None], 0.0, NEG).astype(np.float32)
    mask_zero = np.where((np.arange(T) < USED)[None], 0.0, NEG).astype(np.float32)
    mask_zero = np.broadcast_to(mask_zero, (T, T)).copy()
    deep_row, deep_col = np.zeros(T, np.int32), np.zeros(T, np.int32)
    deep_row[:USED], deep_col[:USED] = t // 24, t % 24
    deep_keys = np.full((8, T), -100000, np.int32)
    deep_keys[:, :USED] = 11 * deep_row[:USED] + deep_col[:USED] % 6
    ok = (np.arange(T) < USED)[None] & ((deep_col // 6)[:, None] == (deep_col // 6)[None])
    mask_deep = np.where(ok, 0.0, NEG).astype(np.float32)
    grow = np.zeros((4, T, T), np.float32)
    part = np.zeros((T, 4), np.float32)
    i, k = t // 12, t % 12
    for w in range(4):
        grow[w, t, (i // 2) * 24 + 6 * w + k // 2] = 1.0
    part[t, 2 * (i % 2) + k % 2] = 1.0
    part = np.repeat(part[:, :, None], 64, axis=2).reshape(T, 256)
    pick = np.zeros((4, T, 288), np.float32)
    place = np.zeros((288, 4 * T), np.float32)
    for w in range(4):
        pick[w, t, i * 48 + 12 * w + k] = 1.0
        place[i * 48 + 12 * w + k, w * T + t] = 1.0
    heads = np.zeros((8 * T, 256), np.float32)
    for h in range(8):
        heads[h * T : (h + 1) * T, h * 32 : (h + 1) * 32] = 1.0
    return (
        keys,
        mask_one,
        mask_zero,
        deep_keys,
        mask_deep,
        grow.astype(jnp.bfloat16),
        part,
        pick.astype(jnp.bfloat16),
        place.astype(jnp.bfloat16),
        take[T:].astype(jnp.bfloat16),
        heads.astype(jnp.bfloat16),
    )


def dot(a, b):
    return jnp.dot(a, b, preferred_element_type=F32)


def dot_t(a, b):
    return lax.dot_general(a, b, (((1,), (1,)), ((), ())), preferred_element_type=F32)


def thirds(values):
    first = values.astype(BF)
    rest = values - first.astype(F32)
    second = rest.astype(BF)
    third = (rest - second.astype(F32)).astype(BF)
    return jnp.concatenate([first, second, third], axis=0)


def norm_rows(values, scales):
    centred = values - jnp.mean(values, axis=-1, keepdims=True)
    spread = jnp.mean(centred * centred, axis=-1, keepdims=True)
    return (centred * lax.rsqrt(spread + EPS) * scales).astype(BF)


def gelu(values):
    return values * 0.5 * (1.0 + lax.erf(values * (0.5**0.5)))


def attend(q, k, v, bias, heads):
    count = heads.shape[0] // T
    stacked = jnp.concatenate([q] * count, axis=0) * heads
    scores = dot_t(stacked, k) * SCALE + bias
    weights = jnp.exp(scores - jnp.max(scores, axis=-1, keepdims=True))
    weights = (weights * (1.0 / jnp.sum(weights, axis=-1, keepdims=True))).astype(BF)
    mixed = dot(weights, v) * heads.astype(F32)
    total = mixed[0:T]
    for h in range(1, count):
        total = total + mixed[h * T : (h + 1) * T]
    return total.astype(BF)


def kernel(
    skip_ref,
    deep_ref,
    top_gain_ref,
    deep_gain_ref,
    top_tab_ref,
    deep_tab_ref,
    heads_in_ref,
    heads_out_ref,
    hidden_in_ref,
    hidden_out_ref,
    expand_ref,
    top_heads_in_ref,
    top_heads_out_ref,
    top_hidden_in_ref,
    top_hidden_out_ref,
    keys_ref,
    mask_one_ref,
    mask_zero_ref,
    deep_keys_ref,
    mask_deep_ref,
    grow_ref,
    part_ref,
    pick_ref,
    place_ref,
    take_ref,
    heads_ref,
    out_ref,
    dw,
    quarters,
    tw,
    tabs,
    deep_raw,
    deep_bias,
    top_raw,
    bias_zero,
    bias_one,
    deep_x,
    deep_n,
    rs_send,
    rs_core,
    rs_mid,
    rs_recv,
    mids,
    outs,
    grow_send,
    grow_recv,
    swap_send,
    swap_recv,
    halo_send,
    halo,
    fin,
    s_q,
    r_q,
    s_z,
    r_z,
    s_n,
    r_n,
    s_ez,
    r_ez,
    s_ey,
    r_ey,
    s_ef,
    r_ef,
    s_tz,
    r_tz,
    s_ty,
    r_ty,
    s_tx,
    r_tx,
    s_tf,
    r_tf,
    s_tg,
    r_tg,
    s_tab,
    r_tab,
    s_core,
    r_core,
    s_rs,
    r_rs,
    s_ag,
    r_ag,
    s_mid,
    r_mid,
    s_out,
    r_out,
    s_grow,
    r_grow,
    s_swap,
    r_swap,
    s_halo,
    r_halo,
    s_fin,
    r_fin,
):
    band = lax.axis_index("band")
    m = lax.axis_index("mp")
    z, y, x, c = band // 4, band % 4, m // 2, m % 2
    zs = [lax.rem(z + d, 8) for d in range(8)]
    ys = [lax.rem(y + d, 4) for d in range(4)]
    xs = [lax.rem(x + d, 4) for d in range(4)]
    ms = [lax.rem(m + d, 8) for d in range(8)]
    other = 1 - c

    def at_z(d):
        return {"band": zs[d % 8] * 4 + y, "mp": m}

    def at_y(d):
        return {"band": z * 4 + ys[d % 4], "mp": m}

    def at_m(d):
        return {"band": band, "mp": ms[d % 8]}

    def at_plane(dx, dy):
        return {"band": z * 4 + ys[dy % 4], "mp": xs[dx % 4] * 2 + c}

    def at_x(d, core):
        return {"band": band, "mp": xs[d % 4] * 2 + core}

    def at_piece(band_step, x_step):
        return {"band": lax.rem(band + band_step + 32, 32), "mp": xs[x_step % 4] * 2 + c}

    barrier = pltpu.get_barrier_semaphore()
    greeted = [at_z(1), at_z(7), at_x(0, other)]
    greeted += [at_y(d) for d in (1, 2, 3)] + [at_x(d, c) for d in (1, 2, 3)]
    for who in greeted:
        pl.semaphore_signal(barrier, inc=1, device_id=who, device_id_type=MESH)

    sends = []

    def copy(src, dst, ss, rs, who):
        return pltpu.make_async_remote_copy(
            src_ref=src, dst_ref=dst, send_sem=ss, recv_sem=rs, device_id=who, device_id_type=MESH
        )

    def send(src, dst, ss, rs, who):
        cp = copy(src, dst, ss, rs, who)
        cp.start()
        sends.append(cp)

    def await_at(dst, ss, rs, who):
        copy(dst, dst, ss, rs, who).wait_recv()

    for yy in range(BANDS):
        lanes = slice(64 * yy, 64 * yy + 64)
        quarters[yy, :, 0:256] = jnp.concatenate(
            [heads_in_ref[0, :, lanes], heads_in_ref[1, :, lanes], heads_in_ref[2, :, lanes], heads_out_ref[:, lanes]],
            axis=1,
        )
        lanes = slice(256 * yy, 256 * yy + 256)
        quarters[yy, :, 256:512] = hidden_in_ref[:, lanes]
        quarters[yy, :, 512:768] = hidden_out_ref[:, lanes]
    dw[z, y, :, 0:768] = quarters[y]
    dw[z, y, :, 768:1024] = jnp.concatenate([expand_ref[:, i, :] for i in range(4)], axis=1)
    for layer in range(2):
        pieces = [top_heads_in_ref[layer, i] for i in range(3)] + [top_heads_out_ref[layer]]
        pieces += [top_hidden_in_ref[layer], top_hidden_out_ref[layer]]
        tw[x, z, y, :, 768 * layer : 768 * layer + 768] = jnp.concatenate(pieces, axis=1)
    tabs[x] = jnp.zeros((8, 256), F32)
    for layer in range(2):
        flat = jnp.concatenate([top_tab_ref[layer, a] for a in range(11)] + [jnp.zeros((2, 3), F32)], axis=1)
        tabs[x, 2 * layer : 2 * layer + 2, :] = flat
    pl.semaphore_wait(barrier, len(greeted))

    def plane(zz, s, part):
        some = pl.ds(2 * part, 2)
        if s == 3:
            return tw.at[some, zz, :, :, pl.ds(768, 768)]
        return dw.at[zz, some, :, pl.ds(256 * s, 256)]

    def own(yy, s):
        return dw.at[z, yy, :, pl.ds(256 * s, 256)]

    def slot(way, dist):
        return dist - 1 if way > 0 else 3 + dist

    def part_of(way, dist):
        return None if dist < 4 else (0 if way > 0 else 1)

    def limit(part, way):
        return 4 if (part == 0) == (way > 0) else 3

    def hop(s, part, way, dist):
        ref = plane(zs[(-way * (dist - 1)) % 8], s, part)
        k = slot(way, dist)
        send(ref, ref, s_z.at[s, part, k], r_z.at[s, part, k], at_z(way))

    def hops(s):
        for part in range(2):
            for way in (1, -1):
                hop(s, part, way, 1)

    def begin(s):
        for d in (1, 3, 2):
            src = quarters.at[ys[d], :, pl.ds(256 * s, 256)]
            send(src, own(y, s), s_q.at[s, d - 1], r_q.at[s, d - 1], at_y(d))

    def second(yy=None, xx=None):
        return tw.at[x if xx is None else xx, z, pl.ds(0, 4) if yy is None else yy, :, pl.ds(768, 768)]

    def second_y():
        for d in (1, 3, 2):
            send(second(y), second(y), s_ty.at[d - 1], r_ty.at[d - 1], at_y(d))

    def second_x():
        for d in (1, 3, 2):
            await_at(second(ys[(-d) % 4]), s_ty.at[d - 1], r_ty.at[d - 1], at_y(d))
        for d in (1, 3, 2):
            send(second(), second(), s_tx.at[d - 1], r_tx.at[d - 1], at_x(d, c))

    def second_z():
        for d in (1, 3, 2):
            await_at(second(None, xs[(-d) % 4]), s_tx.at[d - 1], r_tx.at[d - 1], at_x(d, c))
        hops(3)

    def begin_z(s):
        for d in (1, 3, 2):
            await_at(own(ys[(-d) % 4], s), s_q.at[s, d - 1], r_q.at[s, d - 1], at_y(d))
        hops(s)

    def step(s, dist):
        for part in range(2):
            for way in (1, -1):
                if dist > limit(part, way):
                    continue
                k = slot(way, dist)
                ref = plane(zs[(-way * dist) % 8], s, part)
                await_at(ref, s_z.at[s, part, k], r_z.at[s, part, k], at_z(way))
                if dist < limit(part, way):
                    hop(s, part, way, dist + 1)

    def expand_part(zz, part=None):
        rows = pl.ds(0, 64) if part is None else pl.ds(32 * part, 32)
        return dw.at[zz, y, rows, pl.ds(768, 256)]

    def top_part(zz, part=None):
        lanes = pl.ds(0, 768) if part is None else pl.ds(384 * part, 384)
        return tw.at[x, zz, y, :, lanes]

    def top_hop(way, dist):
        origin, k, part = zs[(-way * (dist - 1)) % 8], slot(way, dist), part_of(way, dist)
        ref = top_part(origin, part)
        send(ref, ref, s_tz.at[k], r_tz.at[k], at_z(way))

    def top_step(dist):
        for way in (1, -1):
            origin, k, part = zs[(-way * dist) % 8], slot(way, dist), part_of(way, dist)
            await_at(top_part(origin, part), s_tz.at[k], r_tz.at[k], at_z(way))
            if dist < 4:
                top_hop(way, dist + 1)

    def expand_hop(way, dist):
        origin, k, part = zs[(-way * (dist - 1)) % 8], slot(way, dist), part_of(way, dist)
        ref = expand_part(origin, part)
        send(ref, ref, s_ez.at[k], r_ez.at[k], at_z(way))

    def expand_step(dist):
        for way in (1, -1):
            origin, k, part = zs[(-way * dist) % 8], slot(way, dist), part_of(way, dist)
            await_at(expand_part(origin, part), s_ez.at[k], r_ez.at[k], at_z(way))
            if dist < 4:
                expand_hop(way, dist + 1)

    def expand_of(yy, half=None):
        zz = pl.ds(0, 8) if half is None else pl.ds(4 * half, 4)
        return dw.at[zz, yy, :, pl.ds(768, 256)]

    def top_of(half_of, xx, yy, half=None):
        zz = pl.ds(0, 8) if half is None else pl.ds(4 * half, 4)
        xx = pl.ds(0, 4) if xx is None else xx
        yy = pl.ds(0, 4) if yy is None else yy
        return tw.at[xx, zz, yy, :, pl.ds(384 * half_of, 384)]

    def top_ref(half_of, phase, d, half=None):
        along_y = (half_of == 0) == (phase == 0)
        if along_y:
            return top_of(half_of, x if phase == 0 else None, ys[d % 4], half)
        return top_of(half_of, xs[d % 4], y if phase == 0 else None, half)

    def top_who(half_of, phase, d):
        return at_y(d) if (half_of == 0) == (phase == 0) else at_x(d, c)

    def top_send(half_of, phase):
        ref = top_ref(half_of, phase, 0)
        for e, d in enumerate((1, 3)):
            ss, rs = s_tf.at[half_of, phase, e], r_tf.at[half_of, phase, e]
            send(ref, ref, ss, rs, top_who(half_of, phase, d))

    def top_relay(half_of, phase):
        for e, d in enumerate((1, 3)):
            ss, rs = s_tf.at[half_of, phase, e], r_tf.at[half_of, phase, e]
            await_at(top_ref(half_of, phase, -d), ss, rs, top_who(half_of, phase, d))
            half = top_ref(half_of, phase, -d, e)
            ss, rs = s_tg.at[half_of, phase, e], r_tg.at[half_of, phase, e]
            send(half, half, ss, rs, top_who(half_of, phase, d))

    def top_ready(half_of, phase):
        for e, d in enumerate((1, 3)):
            ss, rs = s_tg.at[half_of, phase, e], r_tg.at[half_of, phase, e]
            await_at(top_ref(half_of, phase, 2, e), ss, rs, top_who(half_of, phase, d))

    def expand_send():
        for e, d in enumerate((1, 3)):
            send(expand_of(y), expand_of(y), s_ey.at[e], r_ey.at[e], at_y(d))

    def expand_relay():
        for e, d in enumerate((1, 3)):
            yy = ys[4 - d]
            await_at(expand_of(yy), s_ey.at[e], r_ey.at[e], at_y(d))
            send(expand_of(yy, e), expand_of(yy, e), s_ef.at[e], r_ef.at[e], at_y(d))

    def expand_ready():
        for e, d in enumerate((1, 3)):
            await_at(expand_of(ys[2], e), s_ef.at[e], r_ef.at[e], at_y(d))

    steps = [(dx, dy) for dy in range(4) for dx in range(4) if dx or dy]
    steps.sort(key=lambda d: min(d[0], 4 - d[0]) + min(d[1], 4 - d[1]))

    def scatter(which):
        order = (2, 1, 3, 0)
        for dx in order:
            ss, rs = s_core.at[which, dx], r_core.at[which, dx]
            send(rs_send.at[which, other, xs[dx]], rs_core.at[which, xs[dx]], ss, rs, at_x(0, other))
        for dx in order:
            ss, rs = s_core.at[which, dx], r_core.at[which, dx]
            await_at(rs_core.at[which, xs[dx]], ss, rs, at_x(0, other))
            both = rs_send[which, c, xs[dx]].astype(F32) + rs_core[which, xs[dx]].astype(F32)
            rs_mid[which, xs[dx]] = both.astype(BF)
            for e, (ex, dy) in enumerate(steps):
                if ex == dx:
                    ss, rs = s_rs.at[which, e], r_rs.at[which, e]
                    send(rs_mid.at[which, xs[dx], ys[dy]], rs_recv.at[which, x, y], ss, rs, at_plane(dx, dy))
        rs_recv[which, x, y] = rs_mid[which, x, y]

    def gathered_sum(which):
        for e, (dx, dy) in enumerate(steps):
            dst = rs_recv.at[which, xs[(-dx) % 4], ys[(-dy) % 4]]
            await_at(dst, s_rs.at[which, e], r_rs.at[which, e], at_plane(dx, dy))
        total = rs_recv[which, 0, 0].astype(F32)
        for j in range(1, 16):
            total = total + rs_recv[which, j // 4, j % 4].astype(F32)
        return total

    def pass_mid(ref, e):
        send(ref, ref, s_mid.at[e], r_mid.at[e], at_x(0, other))

    def share():
        for e, (dx, dy) in enumerate(steps):
            ref = mids.at[c, x, y]
            send(ref, ref, s_ag.at[e], r_ag.at[e], at_plane(dx, dy))
        pass_mid(mids.at[c, x, y], 15)

    def shared():
        for e, (dx, dy) in enumerate(steps):
            dst = mids.at[c, xs[(-dx) % 4], ys[(-dy) % 4]]
            await_at(dst, s_ag.at[e], r_ag.at[e], at_plane(dx, dy))
            pass_mid(dst, e)
        for e, (dx, dy) in enumerate(steps + [(0, 0)]):
            dst = mids.at[other, xs[(-dx) % 4], ys[(-dy) % 4]]
            await_at(dst, s_mid.at[e], r_mid.at[e], at_x(0, other))

    def share_out():
        for d in range(1, 8):
            send(outs.at[m], outs.at[m], s_out.at[d - 1], r_out.at[d - 1], at_m(d))

    def shared_out():
        for d in range(1, 8):
            await_at(outs.at[ms[(-d) % 8]], s_out.at[d - 1], r_out.at[d - 1], at_m(d))

    def swap(which, partial):
        swap_send[which] = partial.astype(BF)
        send(swap_send.at[which], swap_recv.at[which], s_swap.at[which], r_swap.at[which], at_x(0, other))

    def swapped(which):
        await_at(swap_recv.at[which], s_swap.at[which], r_swap.at[which], at_x(0, other))
        return swap_send[which].astype(F32) + swap_recv[which].astype(F32)

    begin(0)
    top_hop(1, 1)
    top_hop(-1, 1)
    second_y()
    for d in (1, 2, 3):
        send(tabs.at[x], tabs.at[x], s_tab.at[d - 1], r_tab.at[d - 1], at_x(d, c))

    for i in range(3):
        deep_x[24 * i : 24 * i + 24, :] = deep_ref[i].astype(F32)
    deep_x[USED:T, :] = jnp.zeros((T - USED, 2048), F32)
    deep_n[y] = norm_rows(deep_x[...], deep_gain_ref[0:1, :])
    for d in (1, 3, 2):
        send(deep_n.at[y], deep_n.at[y], s_n.at[d - 1], r_n.at[d - 1], at_y(d))

    begin(1)
    begin(2)
    begin_z(0)
    top_step(1)

    flat = jnp.concatenate([deep_tab_ref[a] for a in range(5)] + [jnp.zeros((8, 73), F32)], axis=1)
    deep_tab = thirds(flat)
    deep_iota = lax.broadcasted_iota(jnp.int32, (128, T), 0) + deep_keys_ref[0:1, :]

    def deep_rows(g, carry):
        for e in range(8):
            n = 8 * g + e
            r = n // 24
            col = n - 24 * r
            want = (r + 2) * 11 + lax.rem(col, 6) + 5
            hot = jnp.where(deep_iota == want, 1.0, 0.0).astype(BF)
            got = dot(deep_tab, hot)
            deep_raw[n] = got[0:8] + got[8:16] + got[16:24]
        return carry

    step(0, 1)
    top_step(2)
    second_x()
    lax.fori_loop(0, 4, deep_rows, 0)
    step(0, 2)
    top_step(3)
    lax.fori_loop(4, 9, deep_rows, 0)
    step(0, 3)
    begin_z(1)
    begin_z(2)
    expand_hop(1, 1)
    expand_hop(-1, 1)
    top_step(4)
    top_send(0, 0)
    top_send(1, 0)
    for h in range(8):
        deep_bias[h * T : h * T + USED, :] = deep_raw[:, h, :] + mask_deep_ref[0:USED, :]
        deep_bias[h * T + USED : (h + 1) * T, :] = mask_deep_ref[USED:T, :]

    for d in (1, 2, 3):
        await_at(tabs.at[xs[(-d) % 4]], s_tab.at[d - 1], r_tab.at[d - 1], at_x(d, c))
    top_tab = thirds(tabs[...].reshape(32, 256))
    top_iota = lax.broadcasted_iota(jnp.int32, (256, EXT), 0) + keys_ref[0:1, :]

    def top_rows(g, carry):
        for e in range(4):
            n = 4 * g + e
            i = n // 12
            want = (i + 5) * 23 + (n - 12 * i) + 11
            hot = jnp.where(top_iota == want, 1.0, 0.0).astype(BF)
            got = dot(top_tab, hot)
            top_raw[n] = got[0:32] + got[32:64] + got[64:96]
        return carry

    lax.fori_loop(0, 6, top_rows, 0)
    step(0, 4)
    for d in (1, 3, 2):
        await_at(deep_n.at[ys[(-d) % 4]], s_n.at[d - 1], r_n.at[d - 1], at_y(d))

    acc = jnp.zeros((BANDS * T, 256), F32)
    for j in range(8):
        block = dw[j, :, :, 0:256].reshape(256, 256)
        acc = acc + dot(deep_n[:, :, 256 * j : 256 * j + 256].reshape(BANDS * T, 256), block)
    qkv = acc.astype(BF)
    bias = deep_bias[pl.ds(pl.multiple_of(y * 2 * T, 2 * T), 2 * T), :]
    two = heads_ref[0 : 2 * T, 0:64]
    mixed = []
    for b in range(BANDS):
        rows = qkv[b * T : (b + 1) * T]
        mixed.append(attend(rows[:, 0:64], rows[:, 64:128], rows[:, 128:192], bias, two))
    mixed = jnp.concatenate(mixed, axis=0)
    wide = jnp.concatenate([jnp.zeros((BANDS * T, 192), BF), mixed], axis=1)
    for j in range(8):
        got = dot_t(wide, dw[j, :, :, 0:256].reshape(256, 256)).astype(BF)
        rs_send[0, j % 2, j // 2] = got.reshape(BANDS, T, 256)
    scatter(0)
    top_relay(0, 0)
    top_relay(1, 0)
    step(1, 1)
    step(2, 1)
    expand_step(1)
    lax.fori_loop(6, 12, top_rows, 0)
    step(1, 2)
    step(2, 2)
    expand_step(2)
    column = pl.ds(pl.multiple_of(m * 256, 256), 256)
    mids[c, x, y] = (deep_x[:, column] + gathered_sum(0)).astype(BF)
    share()
    top_ready(0, 0)
    top_send(0, 1)
    top_ready(1, 0)
    top_send(1, 1)
    step(1, 3)
    step(2, 3)
    expand_step(3)
    second_z()
    lax.fori_loop(12, 18, top_rows, 0)
    step_key = keys_ref[1:2, :]
    gone = ((step_key < 0) & (band == 0)) | ((step_key > 0) & (band == 31))
    mask_one = mask_one_ref[...] + jnp.where(gone, NEG, 0.0)
    for w in range(4):
        for h in range(2):
            g = (2 * w + h) * T
            bias_zero[g : g + USED, :] = top_raw[:, 8 * w + h, 0:T] + mask_zero_ref[0:USED, :]
            bias_zero[g + USED : g + T, :] = mask_zero_ref[USED:T, :]
            bias_one[g : g + USED, :] = top_raw[:, 8 * w + 2 + h, :] + mask_one[0:USED, :]
            bias_one[g + USED : g + T, :] = mask_one[USED:T, :]
    heads = heads_ref[...]
    own_skip = dot(pick_ref[x], skip_ref[...].reshape(288, 512))
    step(1, 4)
    step(2, 4)
    expand_step(4)
    expand_send()
    shared()
    normed_two = []
    for b in range(BANDS):
        middle = jnp.concatenate([mids[j % 2, j // 2, b] for j in range(8)], axis=1).astype(F32)
        normed_two.append(norm_rows(middle, deep_gain_ref[1:2, :]))
    normed_two = jnp.concatenate(normed_two, axis=0)
    acc = jnp.zeros((BANDS * T, 256), F32)
    for j in range(8):
        block = dw[j, :, :, 256:512].reshape(256, 256)
        acc = acc + dot(normed_two[:, 256 * j : 256 * j + 256], block)
    hidden = gelu(acc).astype(BF)
    for j in range(8):
        got = dot_t(hidden, dw[j, :, :, 512:768].reshape(256, 256)).astype(BF)
        rs_send[1, j % 2, j // 2] = got.reshape(BANDS, T, 256)
    scatter(1)
    top_relay(0, 1)
    top_relay(1, 1)
    expand_relay()
    step(3, 1)
    outs[m] = (mids[c, x, y].astype(F32) + gathered_sum(1)).astype(BF)
    share_out()
    step(3, 2)
    expand_ready()
    shared_out()
    acc = jnp.zeros((T, 256), F32)
    for j in range(8):
        acc = acc + dot(outs[j], dw[j, :, :, 768:1024].reshape(256, 256))
    grown = acc.astype(BF)
    for w in range(4):
        chosen = dot(grow_ref[w], grown) * part_ref[...]
        piece = chosen[:, 0:64] + chosen[:, 64:128] + chosen[:, 128:192] + chosen[:, 192:256]
        grow_send[w] = jnp.concatenate([piece, jnp.zeros((T, 64), F32)], axis=1).astype(BF)
    for d in range(1, 8):
        send(grow_send.at[ms[d] // 2], grow_recv.at[m], s_grow.at[d - 1], r_grow.at[d - 1], at_m(d))
    step(3, 3)
    grow_recv[m] = grow_send[x]
    for d in range(1, 8):
        await_at(grow_recv.at[ms[(-d) % 8]], s_grow.at[d - 1], r_grow.at[d - 1], at_m(d))
    window = jnp.concatenate([grow_recv[j][:, 0:64] for j in range(8)], axis=1)
    state = (own_skip + window.astype(F32)).astype(BF)

    for layer in range(2):
        if layer == 0:
            top_ready(0, 1)
            top_ready(1, 1)
        else:
            step(3, 4)
        base = 768 * layer
        normed = norm_rows(state.astype(F32), top_gain_ref[layer, 0:1, :])
        parts = []
        for w in range(4):
            block = tw[w, :, :, :, base : base + 256].reshape(512, 256)
            parts.append(dot(normed, block).astype(BF))
        q = jnp.concatenate([p[:, 0:64] for p in parts], axis=1)
        k = jnp.concatenate([p[:, 64:128] for p in parts], axis=1)
        v = jnp.concatenate([p[:, 128:192] for p in parts], axis=1)
        if layer == 0:
            mixed = attend(q, k, v, bias_zero[...], heads)
        else:
            kv = jnp.concatenate([k, v], axis=1)
            halo_send[...] = dot(take_ref[...], kv).astype(BF)
            halo[0:T, :] = kv
            for e, (band_step, x_step, r0, nr, c0, nc, off, size) in enumerate(PIECES):
                src = halo_send.at[pl.ds(off - T, size)]
                dst = halo.at[pl.ds(off, size)]
                send(src, dst, s_halo.at[e], r_halo.at[e], at_piece(-band_step, -x_step))
            for e, (band_step, x_step, r0, nr, c0, nc, off, size) in enumerate(PIECES):
                dst = halo.at[pl.ds(off, size)]
                await_at(dst, s_halo.at[e], r_halo.at[e], at_piece(-band_step, -x_step))
            mixed = attend(q, halo[:, 0:256], halo[:, 256:512], bias_one[...], heads)
        total = jnp.zeros((T, 512), F32)
        for w in range(4):
            block = tw[w, :, :, :, base : base + 256].reshape(512, 256)
            wide = jnp.concatenate([jnp.zeros((T, 192), BF), mixed[:, 64 * w : 64 * w + 64]], axis=1)
            total = total + dot_t(wide, block)
        swap(2 * layer, total)
        middle = (state.astype(F32) + swapped(2 * layer)).astype(BF)
        normed = norm_rows(middle.astype(F32), top_gain_ref[layer, 1:2, :])
        total = jnp.zeros((T, 512), F32)
        for w in range(4):
            block = tw[w, :, :, :, base + 256 : base + 512].reshape(512, 256)
            hidden = gelu(dot(normed, block)).astype(BF)
            total = total + dot_t(hidden, tw[w, :, :, :, base + 512 : base + 768].reshape(512, 256))
        swap(2 * layer + 1, total)
        state = (middle.astype(F32) + swapped(2 * layer + 1)).astype(BF)

    for half in range(2):
        fin[x, half] = state[:, 256 * half : 256 * half + 256]
    for d in (1, 2, 3):
        for e in range(2):
            core = lax.rem(c + e, 2)
            ss, rs = s_fin.at[d - 1, e], r_fin.at[d - 1, e]
            send(fin.at[x, c], fin.at[x, c], ss, rs, at_x(d, core))
    for d in (1, 2, 3):
        for e in range(2):
            core = lax.rem(c + e, 2)
            ss, rs = s_fin.at[d - 1, e], r_fin.at[d - 1, e]
            await_at(fin.at[xs[(-d) % 4], core], ss, rs, at_x(d, core))
    for half in range(2):
        stacked = jnp.concatenate([fin[w, half] for w in range(4)], axis=0)
        rows = dot(place_ref[...], stacked).astype(BF).reshape(6, 48, 256)
        out_ref[:, :, 256 * half : 256 * half + 256] = rows
    for cp in sends:
        cp.wait_send()


def local(
    skip_features,
    deep_features,
    top_gains,
    top_heads_in,
    top_heads_out,
    top_hidden_in,
    top_hidden_out,
    top_offsets,
    deep_gains,
    deep_offsets,
    deep_heads_in,
    deep_heads_out,
    deep_hidden_in,
    deep_hidden_out,
    expand_weight,
):
    constants = [jnp.asarray(a) for a in tables()]
    operands = [
        skip_features,
        deep_features,
        top_gains,
        deep_gains,
        top_offsets.transpose(0, 2, 1, 3),
        deep_offsets.transpose(1, 0, 2),
        deep_heads_in.transpose(1, 0, 2),
        deep_heads_out.T,
        deep_hidden_in,
        deep_hidden_out.T,
        expand_weight,
        top_heads_in.transpose(0, 2, 1, 3),
        top_heads_out.transpose(0, 2, 1),
        top_hidden_in,
        top_hidden_out.transpose(0, 2, 1),
        *constants,
    ]
    dma = pltpu.SemaphoreType.DMA
    shapes = [(3, 3), (4, 2, 8), (3,), (8,), (2,), (2,), (8,), (3,), (3,), (2, 2, 2), (2, 2, 2), (3,)]
    shapes += [(2, 4), (2, 15), (15,), (16,), (7,), (7,), (4,), (8,), (3, 2)]
    vmem = pl.BlockSpec(memory_space=pltpu.VMEM)
    return pl.pallas_call(
        kernel,
        out_shape=jax.ShapeDtypeStruct((6, 48, 512), BF),
        in_specs=[vmem] * len(operands),
        out_specs=vmem,
        scratch_shapes=[
            pltpu.VMEM((8, 4, 64, 1024), BF),
            pltpu.VMEM((4, 64, 768), BF),
            pltpu.VMEM((4, 8, 4, 16, 1536), BF),
            pltpu.VMEM((4, 8, 256), F32),
            pltpu.VMEM((USED, 8, T), F32),
            pltpu.VMEM((8 * T, T), F32),
            pltpu.VMEM((USED, 32, EXT), F32),
            pltpu.VMEM((8 * T, T), F32),
            pltpu.VMEM((8 * T, EXT), F32),
            pltpu.VMEM((T, 2048), F32),
            pltpu.VMEM((BANDS, T, 2048), BF),
            pltpu.VMEM((2, 2, 4, BANDS, T, 256), BF),
            pltpu.VMEM((2, 4, BANDS, T, 256), BF),
            pltpu.VMEM((2, 4, BANDS, T, 256), BF),
            pltpu.VMEM((2, 4, BANDS, T, 256), BF),
            pltpu.VMEM((2, 4, BANDS, T, 256), BF),
            pltpu.VMEM((8, T, 256), BF),
            pltpu.VMEM((4, T, 128), BF),
            pltpu.VMEM((8, T, 128), BF),
            pltpu.VMEM((4, T, 512), BF),
            pltpu.VMEM((4, T, 512), BF),
            pltpu.VMEM((EXT - T, 512), BF),
            pltpu.VMEM((EXT, 512), BF),
            pltpu.VMEM((4, 2, T, 256), BF),
        ]
        + [dma(s) for s in shapes for _ in range(2)],
        compiler_params=pltpu.CompilerParams(
            collective_id=0, has_side_effects=True, vmem_limit_bytes=56 * 2**20
        ),
    )(*operands)


def solution(mesh):
    placed = (
        P("band", None, None),
        P("band", None, None),
        P(),
        P(None, "band", None, "mp"),
        P(None, "mp", "band"),
        P(None, "band", "mp"),
        P(None, "mp", "band"),
        P(None, "mp", None, None),
        P(),
        P("mp", None, None),
        P("band", None, "mp"),
        P("mp", "band"),
        P("band", "mp"),
        P("mp", "band"),
        P("band", None, "mp"),
    )
    return jax.shard_map(
        local, mesh=mesh, in_specs=placed, out_specs=P("band", None, None), check_vma=False
    )
```

```python
import functools

import jax
import jax.numpy as jnp
import numpy as np
from jax import lax
from jax.experimental import pallas as pl
from jax.experimental.pallas import tpu as pltpu
from jax.sharding import PartitionSpec as P

BF = jnp.bfloat16
F32 = jnp.float32
EPS = 1e-05
NEG = -1e30
T = 80
USED = 72
EXT = 400
SCALE = 32 ** (-0.5)
MESH = pl.DeviceIdType.MESH
BANDS = 2

PIECES = (
    (-1, 0, 3, 3, 0, 12, 80, 48),
    (1, 0, 0, 3, 0, 12, 128, 48),
    (0, -1, 0, 6, 6, 6, 176, 48),
    (0, 1, 0, 6, 0, 6, 224, 48),
    (-1, -1, 3, 3, 6, 6, 272, 32),
    (-1, 1, 3, 3, 0, 6, 304, 32),
    (1, -1, 0, 3, 6, 6, 336, 32),
    (1, 1, 0, 3, 0, 6, 368, 32),
)


@functools.lru_cache(None)
def tables():
    key_row = np.zeros(EXT, np.int32)
    key_col = np.zeros(EXT, np.int32)
    key_ok = np.zeros(EXT, bool)
    key_step = np.zeros(EXT, np.int32)
    t = np.arange(USED)
    key_row[:USED], key_col[:USED], key_ok[:USED] = t // 12, t % 12, True
    take = np.zeros((EXT, T), np.float32)
    for band_step, x_step, r0, nr, c0, nc, off, _ in PIECES:
        p = np.arange(nr * nc)
        r, c = r0 + p // nc, c0 + p % nc
        key_row[off : off + nr * nc] = r + 6 * band_step
        key_col[off : off + nr * nc] = c + 12 * x_step
        key_ok[off : off + nr * nc] = True
        key_step[off : off + nr * nc] = band_step
        take[off + p, r * 12 + c] = 1.0
    keys = np.zeros((8, EXT), np.int32)
    keys[0] = np.where(key_ok, 23 * key_row + key_col, -100000)
    keys[1] = key_step
    q_row, q_col = np.zeros(T, np.int32), np.zeros(T, np.int32)
    q_row[:USED], q_col[:USED] = t // 12, t % 12
    same = ((q_row >= 3)[:, None] == (key_row >= 3)[None]) & (
        (q_col >= 6)[:, None] == (key_col >= 6)[None]
    )
    mask_one = np.where(same & key_ok[None], 0.0, NEG).astype(np.float32)
    mask_zero = np.where((np.arange(T) < USED)[None], 0.0, NEG).astype(np.float32)
    mask_zero = np.broadcast_to(mask_zero, (T, T)).copy()
    deep_row, deep_col = np.zeros(T, np.int32), np.zeros(T, np.int32)
    deep_row[:USED], deep_col[:USED] = t // 24, t % 24
    deep_keys = np.full((8, T), -100000, np.int32)
    deep_keys[:, :USED] = 11 * deep_row[:USED] + deep_col[:USED] % 6
    ok = (np.arange(T) < USED)[None] & ((deep_col // 6)[:, None] == (deep_col // 6)[None])
    mask_deep = np.where(ok, 0.0, NEG).astype(np.float32)
    grow = np.zeros((4, T, T), np.float32)
    part = np.zeros((T, 4), np.float32)
    i, k = t // 12, t % 12
    for w in range(4):
        grow[w, t, (i // 2) * 24 + 6 * w + k // 2] = 1.0
    part[t, 2 * (i % 2) + k % 2] = 1.0
    part = np.repeat(part[:, :, None], 64, axis=2).reshape(T, 256)
    pick = np.zeros((4, T, 288), np.float32)
    place = np.zeros((288, 4 * T), np.float32)
    for w in range(4):
        pick[w, t, i * 48 + 12 * w + k] = 1.0
        place[i * 48 + 12 * w + k, w * T + t] = 1.0
    heads = np.zeros((8 * T, 256), np.float32)
    for h in range(8):
        heads[h * T : (h + 1) * T, h * 32 : (h + 1) * 32] = 1.0
    return (
        keys,
        mask_one,
        mask_zero,
        deep_keys,
        mask_deep,
        grow.astype(jnp.bfloat16),
        part,
        pick.astype(jnp.bfloat16),
        place.astype(jnp.bfloat16),
        take[T:].astype(jnp.bfloat16),
        heads.astype(jnp.bfloat16),
    )


def dot(a, b):
    return jnp.dot(a, b, preferred_element_type=F32)


def dot_t(a, b):
    return lax.dot_general(a, b, (((1,), (1,)), ((), ())), preferred_element_type=F32)


def thirds(values):
    first = values.astype(BF)
    rest = values - first.astype(F32)
    second = rest.astype(BF)
    third = (rest - second.astype(F32)).astype(BF)
    return jnp.concatenate([first, second, third], axis=0)


def norm_rows(values, scales):
    centred = values - jnp.mean(values, axis=-1, keepdims=True)
    spread = jnp.mean(centred * centred, axis=-1, keepdims=True)
    return (centred * lax.rsqrt(spread + EPS) * scales).astype(BF)


def gelu(values):
    return values * 0.5 * (1.0 + lax.erf(values * (0.5**0.5)))


def attend(q, k, v, bias, heads):
    count = heads.shape[0] // T
    stacked = jnp.concatenate([q] * count, axis=0) * heads
    scores = dot_t(stacked, k) * SCALE + bias
    weights = jnp.exp(scores - jnp.max(scores, axis=-1, keepdims=True))
    weights = (weights * (1.0 / jnp.sum(weights, axis=-1, keepdims=True))).astype(BF)
    mixed = dot(weights, v) * heads.astype(F32)
    total = mixed[0:T]
    for h in range(1, count):
        total = total + mixed[h * T : (h + 1) * T]
    return total.astype(BF)


def kernel(
    skip_ref,
    deep_ref,
    top_gain_ref,
    deep_gain_ref,
    top_tab_ref,
    deep_tab_ref,
    heads_in_ref,
    heads_out_ref,
    hidden_in_ref,
    hidden_out_ref,
    expand_ref,
    top_heads_in_ref,
    top_heads_out_ref,
    top_hidden_in_ref,
    top_hidden_out_ref,
    keys_ref,
    mask_one_ref,
    mask_zero_ref,
    deep_keys_ref,
    mask_deep_ref,
    grow_ref,
    part_ref,
    pick_ref,
    place_ref,
    take_ref,
    heads_ref,
    out_ref,
    dw,
    quarters,
    tw,
    tabs,
    deep_tabs,
    deep_raw,
    deep_bias,
    top_raw,
    bias_zero,
    bias_one,
    deep_x,
    deep_n,
    rs_send,
    rs_recv,
    own_mid,
    mids,
    outs,
    grow_send,
    grow_recv,
    swap_send,
    swap_recv,
    halo_send,
    halo,
    fin,
    s_q,
    r_q,
    s_z,
    r_z,
    s_n,
    r_n,
    s_ez,
    r_ez,
    s_ey,
    r_ey,
    s_ef,
    r_ef,
    s_tz,
    r_tz,
    s_ty,
    r_ty,
    s_tx,
    r_tx,
    s_tf,
    r_tf,
    s_tg,
    r_tg,
    s_tab,
    r_tab,
    s_f,
    r_f,
    s_dt,
    r_dt,
    s_rs,
    r_rs,
    s_ag,
    r_ag,
    s_out,
    r_out,
    s_grow,
    r_grow,
    s_swap,
    r_swap,
    s_halo,
    r_halo,
    s_fin,
    r_fin,
):
    band = lax.axis_index("band")
    m = lax.axis_index("mp")
    z, y, x, c = band // 4, band % 4, m // 2, m % 2
    zs = [lax.rem(z + d, 8) for d in range(8)]
    ys = [lax.rem(y + d, 4) for d in range(4)]
    xs = [lax.rem(x + d, 4) for d in range(4)]
    ms = [lax.rem(m + d, 8) for d in range(8)]
    other = 1 - c

    def at_z(d):
        return {"band": zs[d % 8] * 4 + y, "mp": m}

    def at_y(d):
        return {"band": z * 4 + ys[d % 4], "mp": m}

    def at_m(d):
        return {"band": band, "mp": ms[d % 8]}

    def at_plane(dx, dy):
        return {"band": z * 4 + ys[dy % 4], "mp": xs[dx % 4] * 2 + c}

    def at_x(d, core):
        return {"band": band, "mp": xs[d % 4] * 2 + core}

    def at_piece(band_step, x_step):
        return {"band": lax.rem(band + band_step + 32, 32), "mp": xs[x_step % 4] * 2 + c}

    barrier = pltpu.get_barrier_semaphore()
    greeted = [at_z(1), at_z(7), at_x(0, other)]
    greeted += [at_y(d) for d in (1, 2, 3)] + [at_x(d, c) for d in (1, 2, 3)]
    for who in greeted:
        pl.semaphore_signal(barrier, inc=1, device_id=who, device_id_type=MESH)

    sends = []

    def copy(src, dst, ss, rs, who):
        return pltpu.make_async_remote_copy(
            src_ref=src, dst_ref=dst, send_sem=ss, recv_sem=rs, device_id=who, device_id_type=MESH
        )

    def send(src, dst, ss, rs, who):
        cp = copy(src, dst, ss, rs, who)
        cp.start()
        sends.append(cp)

    conditional = []

    def send_if(cond, src, dst, ss, rs, who):
        cp = copy(src, dst, ss, rs, who)
        pl.when(cond)(cp.start)
        conditional.append((cond, cp))

    def await_if(cond, dst, ss, rs, who):
        pl.when(cond)(copy(dst, dst, ss, rs, who).wait_recv)

    def await_at(dst, ss, rs, who):
        copy(dst, dst, ss, rs, who).wait_recv()

    for yy in range(4):
        lanes = slice(64 * yy, 64 * yy + 64)
        quarters[yy, :, 0:256] = jnp.concatenate(
            [heads_in_ref[0, :, lanes], heads_in_ref[1, :, lanes], heads_in_ref[2, :, lanes], heads_out_ref[:, lanes]],
            axis=1,
        )
        lanes = slice(256 * yy, 256 * yy + 256)
        quarters[yy, :, 256:512] = hidden_in_ref[:, lanes]
        quarters[yy, :, 512:768] = hidden_out_ref[:, lanes]
    dw[c, z, y, :, 0:768] = quarters[y]
    dw[c, z, y, :, 768:1024] = jnp.concatenate([expand_ref[:, i, :] for i in range(4)], axis=1)
    for layer in range(2):
        pieces = [top_heads_in_ref[layer, i] for i in range(3)] + [top_heads_out_ref[layer]]
        pieces += [top_hidden_in_ref[layer], top_hidden_out_ref[layer]]
        tw[x, z, y, :, 768 * layer : 768 * layer + 768] = jnp.concatenate(pieces, axis=1)
    flat = jnp.concatenate([deep_tab_ref[a] for a in range(5)] + [jnp.zeros((8, 73), F32)], axis=1)
    deep_tabs[c] = flat
    tabs[x] = jnp.zeros((8, 256), F32)
    for layer in range(2):
        flat = jnp.concatenate([top_tab_ref[layer, a] for a in range(11)] + [jnp.zeros((2, 3), F32)], axis=1)
        tabs[x, 2 * layer : 2 * layer + 2, :] = flat
    pl.semaphore_wait(barrier, len(greeted))

    def plane(zz, s, part):
        some = pl.ds(2 * part, 2)
        if s == 3:
            return tw.at[some, zz, :, :, pl.ds(768, 768)]
        return dw.at[c, zz, some, :, pl.ds(256 * s, 256)]

    def own(yy, s):
        return dw.at[c, z, yy, :, pl.ds(256 * s, 256)]

    def slot(way, dist):
        return dist - 1 if way > 0 else 3 + dist

    def part_of(way, dist):
        return None if dist < 4 else (0 if way > 0 else 1)

    def limit(part, way):
        return 4 if (part == 0) == (way > 0) else 3

    def hop(s, part, way, dist):
        ref = plane(zs[(-way * (dist - 1)) % 8], s, part)
        k = slot(way, dist)
        send(ref, ref, s_z.at[s, part, k], r_z.at[s, part, k], at_z(way))

    def hops(s):
        for part in range(2):
            for way in (1, -1):
                hop(s, part, way, 1)

    def forward(s, zz, part, k):
        if s < 3:
            ref = plane(zz, s, part)
            send(ref, ref, s_f.at[s, part, k], r_f.at[s, part, k], at_x(0, other))

    def finish(s):
        for part in range(2):
            for way, most in ((0, 1), (1, limit(part, 1)), (-1, limit(part, -1))):
                for dist in range(1, most + 1):
                    k = 8 if way == 0 else slot(way, dist)
                    zz = zs[(-way * dist) % 8]
                    ref = dw.at[other, zz, pl.ds(2 * part, 2), :, pl.ds(256 * s, 256)]
                    await_at(ref, s_f.at[s, part, k], r_f.at[s, part, k], at_x(0, other))

    def begin(s):
        for d in (1, 3, 2):
            src = quarters.at[ys[d], :, pl.ds(256 * s, 256)]
            send(src, own(y, s), s_q.at[s, d - 1], r_q.at[s, d - 1], at_y(d))

    def second(yy=None, xx=None):
        return tw.at[x if xx is None else xx, z, pl.ds(0, 4) if yy is None else yy, :, pl.ds(768, 768)]

    def second_y():
        for d in (1, 3, 2):
            send(second(y), second(y), s_ty.at[d - 1], r_ty.at[d - 1], at_y(d))

    def second_x():
        for d in (1, 3, 2):
            await_at(second(ys[(-d) % 4]), s_ty.at[d - 1], r_ty.at[d - 1], at_y(d))
        for d in (1, 3, 2):
            send(second(), second(), s_tx.at[d - 1], r_tx.at[d - 1], at_x(d, c))

    def second_z():
        for d in (1, 3, 2):
            await_at(second(None, xs[(-d) % 4]), s_tx.at[d - 1], r_tx.at[d - 1], at_x(d, c))
        hops(3)

    def begin_z(s):
        for d in (1, 3, 2):
            await_at(own(ys[(-d) % 4], s), s_q.at[s, d - 1], r_q.at[s, d - 1], at_y(d))
        hops(s)
        for part in range(2):
            forward(s, z, part, 8)

    def step(s, dist):
        for part in range(2):
            for way in (1, -1):
                if dist > limit(part, way):
                    continue
                k = slot(way, dist)
                ref = plane(zs[(-way * dist) % 8], s, part)
                await_at(ref, s_z.at[s, part, k], r_z.at[s, part, k], at_z(way))
                if dist < limit(part, way):
                    hop(s, part, way, dist + 1)
                forward(s, zs[(-way * dist) % 8], part, k)

    def expand_part(zz, part=None):
        rows = pl.ds(0, 64) if part is None else pl.ds(32 * part, 32)
        return dw.at[c, zz, y, rows, pl.ds(768, 256)]

    def top_part(zz, part=None):
        lanes = pl.ds(0, 768) if part is None else pl.ds(384 * part, 384)
        return tw.at[x, zz, y, :, lanes]

    def top_hop(way, dist):
        origin, k, part = zs[(-way * (dist - 1)) % 8], slot(way, dist), part_of(way, dist)
        ref = top_part(origin, part)
        send(ref, ref, s_tz.at[k], r_tz.at[k], at_z(way))

    def top_step(dist):
        for way in (1, -1):
            origin, k, part = zs[(-way * dist) % 8], slot(way, dist), part_of(way, dist)
            await_at(top_part(origin, part), s_tz.at[k], r_tz.at[k], at_z(way))
            if dist < 4:
                top_hop(way, dist + 1)

    def expand_hop(way, dist):
        origin, k, part = zs[(-way * (dist - 1)) % 8], slot(way, dist), part_of(way, dist)
        ref = expand_part(origin, part)
        send(ref, ref, s_ez.at[k], r_ez.at[k], at_z(way))

    def expand_step(dist):
        for way in (1, -1):
            origin, k, part = zs[(-way * dist) % 8], slot(way, dist), part_of(way, dist)
            await_at(expand_part(origin, part), s_ez.at[k], r_ez.at[k], at_z(way))
            if dist < 4:
                expand_hop(way, dist + 1)

    def expand_of(yy, half=None):
        zz = pl.ds(0, 8) if half is None else pl.ds(4 * half, 4)
        return dw.at[c, zz, yy, :, pl.ds(768, 256)]

    def top_of(half_of, xx, yy, half=None):
        zz = pl.ds(0, 8) if half is None else pl.ds(4 * half, 4)
        xx = pl.ds(0, 4) if xx is None else xx
        yy = pl.ds(0, 4) if yy is None else yy
        return tw.at[xx, zz, yy, :, pl.ds(384 * half_of, 384)]

    def top_ref(half_of, phase, d, half=None):
        along_y = (half_of == 0) == (phase == 0)
        if along_y:
            return top_of(half_of, x if phase == 0 else None, ys[d % 4], half)
        return top_of(half_of, xs[d % 4], y if phase == 0 else None, half)

    def top_who(half_of, phase, d):
        return at_y(d) if (half_of == 0) == (phase == 0) else at_x(d, c)

    def top_send(half_of, phase):
        ref = top_ref(half_of, phase, 0)
        for e, d in enumerate((1, 3)):
            ss, rs = s_tf.at[half_of, phase, e], r_tf.at[half_of, phase, e]
            send(ref, ref, ss, rs, top_who(half_of, phase, d))

    def top_relay(half_of, phase):
        for e, d in enumerate((1, 3)):
            ss, rs = s_tf.at[half_of, phase, e], r_tf.at[half_of, phase, e]
            await_at(top_ref(half_of, phase, -d), ss, rs, top_who(half_of, phase, d))
            half = top_ref(half_of, phase, -d, e)
            ss, rs = s_tg.at[half_of, phase, e], r_tg.at[half_of, phase, e]
            send(half, half, ss, rs, top_who(half_of, phase, d))

    def top_ready(half_of, phase):
        for e, d in enumerate((1, 3)):
            ss, rs = s_tg.at[half_of, phase, e], r_tg.at[half_of, phase, e]
            await_at(top_ref(half_of, phase, 2, e), ss, rs, top_who(half_of, phase, d))

    def expand_send():
        for e, d in enumerate((1, 3)):
            send(expand_of(y), expand_of(y), s_ey.at[e], r_ey.at[e], at_y(d))

    def expand_relay():
        for e, d in enumerate((1, 3)):
            yy = ys[4 - d]
            await_at(expand_of(yy), s_ey.at[e], r_ey.at[e], at_y(d))
            send(expand_of(yy, e), expand_of(yy, e), s_ef.at[e], r_ef.at[e], at_y(d))

    def expand_ready():
        for e, d in enumerate((1, 3)):
            await_at(expand_of(ys[2], e), s_ef.at[e], r_ef.at[e], at_y(d))

    steps = [(dx, dy) for dy in range(4) for dx in range(4) if dx or dy]
    steps.sort(key=lambda d: min(d[0], 4 - d[0]) + min(d[1], 4 - d[1]))
    keeper = y // 2
    sibling = at_x(0, other)

    def scatter(which):
        for d in (4, 3, 5, 2, 6, 1, 7, 0):
            for b in range(2):
                src, dst = rs_send.at[which, b, ms[d]], rs_recv.at[which, x, y]
                ss, rs = s_rs.at[which, 8 * b + d], r_rs.at[which, 4 * x + y]
                who = {"band": z * 4 + 2 * c + b, "mp": ms[d]}
                if d:
                    send(src, dst, ss, rs, who)
                else:
                    send_if(y != 2 * c + b, src, dst, ss, rs, who)

        @pl.when(c == keeper)
        def _():
            rs_recv[which, x, y] = rs_send[which, y % 2, m]

    def gathered_sum(which):
        await_if(c != keeper, rs_recv.at[which, x, y], s_rs.at[which, 0], r_rs.at[which, 4 * x + y], sibling)
        for dx, dy in steps:
            xx, yy = xs[(-dx) % 4], ys[(-dy) % 4]
            await_at(rs_recv.at[which, xx, yy], s_rs.at[which, 0], r_rs.at[which, 4 * xx + yy], sibling)
        total = rs_recv[which, 0, 0].astype(F32)
        for j in range(1, 16):
            total = total + rs_recv[which, j // 4, j % 4].astype(F32)
        return total

    def share():
        dst, rs = mids.at[y % 2, m], r_ag.at[8 * (y % 2) + m]
        for e, (dx, dy) in reversed(list(enumerate(steps))):
            who = {"band": z * 4 + ys[dy], "mp": 2 * xs[dx] + keeper}
            send(own_mid, dst, s_ag.at[e], rs, who)
        send_if(c != keeper, own_mid, dst, s_ag.at[15], rs, sibling)

        @pl.when(c == keeper)
        def _():
            mids[y % 2, m] = own_mid[...]

    def shared():
        for d in range(8):
            for b in range(2):
                j = ms[(-d) % 8]
                dst, ss, rs = mids.at[b, j], s_ag.at[0], r_ag.at[8 * b + j]
                if d:
                    await_at(dst, ss, rs, sibling)
                else:
                    await_if(y != 2 * c + b, dst, ss, rs, sibling)

    def share_out():
        for d in range(1, 8):
            send(outs.at[m], outs.at[m], s_out.at[d - 1], r_out.at[d - 1], at_m(d))

    def shared_out():
        for d in range(1, 8):
            await_at(outs.at[ms[(-d) % 8]], s_out.at[d - 1], r_out.at[d - 1], at_m(d))

    def swap(which, partial):
        swap_send[which] = partial.astype(BF)
        send(swap_send.at[which], swap_recv.at[which], s_swap.at[which], r_swap.at[which], at_x(0, other))

    def swapped(which):
        await_at(swap_recv.at[which], s_swap.at[which], r_swap.at[which], at_x(0, other))
        return swap_send[which].astype(F32) + swap_recv[which].astype(F32)

    begin(0)
    top_hop(1, 1)
    top_hop(-1, 1)
    expand_hop(1, 1)
    expand_hop(-1, 1)
    second_y()
    send(deep_tabs.at[c], deep_tabs.at[c], s_dt.at[0], r_dt.at[0], sibling)
    for d in (1, 2, 3):
        send(tabs.at[x], tabs.at[x], s_tab.at[d - 1], r_tab.at[d - 1], at_x(d, c))

    for i in range(3):
        deep_x[24 * i : 24 * i + 24, :] = deep_ref[i].astype(F32)
    deep_x[USED:T, :] = jnp.zeros((T - USED, 2048), F32)
    deep_n[y] = norm_rows(deep_x[...], deep_gain_ref[0:1, :])
    for d in (1, 3, 2):
        send_if(c == keeper, deep_n.at[y], deep_n.at[y], s_n.at[d - 1], r_n.at[y], at_y(d))


    begin(1)
    begin(2)
    top_step(1)
    expand_step(1)
    begin_z(0)
    top_step(2)
    expand_step(2)
    await_at(deep_tabs.at[other], s_dt.at[0], r_dt.at[0], sibling)
    deep_tab = thirds(deep_tabs[...].reshape(16, 128))
    deep_iota = lax.broadcasted_iota(jnp.int32, (128, T), 0) + deep_keys_ref[0:1, :]

    def deep_rows(g, carry):
        for e in range(8):
            n = 8 * g + e
            r = n // 24
            col = n - 24 * r
            want = (r + 2) * 11 + lax.rem(col, 6) + 5
            hot = jnp.where(deep_iota == want, 1.0, 0.0).astype(BF)
            got = dot(deep_tab, hot)
            deep_raw[n] = got[0:16] + got[16:32] + got[32:48]
        return carry

    step(0, 1)
    top_step(3)
    expand_step(3)
    second_x()
    lax.fori_loop(0, 4, deep_rows, 0)
    step(0, 2)
    top_step(4)
    expand_step(4)
    top_send(0, 0)
    top_send(1, 0)
    expand_send()
    lax.fori_loop(4, 9, deep_rows, 0)
    step(0, 3)
    begin_z(1)
    begin_z(2)
    top_relay(0, 0)
    top_relay(1, 0)
    for h in range(16):
        deep_bias[h * T : h * T + USED, :] = deep_raw[:, h, :] + mask_deep_ref[0:USED, :]
        deep_bias[h * T + USED : (h + 1) * T, :] = mask_deep_ref[USED:T, :]

    for d in (1, 2, 3):
        await_at(tabs.at[xs[(-d) % 4]], s_tab.at[d - 1], r_tab.at[d - 1], at_x(d, c))
    top_tab = thirds(tabs[...].reshape(32, 256))
    top_iota = lax.broadcasted_iota(jnp.int32, (256, EXT), 0) + keys_ref[0:1, :]

    def top_rows(g, carry):
        for e in range(4):
            n = 4 * g + e
            i = n // 12
            want = (i + 5) * 23 + (n - 12 * i) + 11
            hot = jnp.where(top_iota == want, 1.0, 0.0).astype(BF)
            got = dot(top_tab, hot)
            top_raw[n] = got[0:32] + got[32:64] + got[64:96]
        return carry

    lax.fori_loop(0, 6, top_rows, 0)
    step(0, 4)
    expand_relay()
    for b in range(2):
        yy = 2 * c + b
        await_if(y != yy, deep_n.at[yy], s_n.at[0], r_n.at[yy], sibling)

    finish(0)
    two = heads_ref[0 : 2 * T, 0:64]
    out = [0.0] * 8
    for e in range(2):
        acc = jnp.zeros((BANDS * T, 256), F32)
        for j in range(8):
            rows = deep_n[pl.ds(2 * c, 2), :, 256 * j : 256 * j + 256].reshape(BANDS * T, 256)
            acc = acc + dot(rows, dw[e, j, :, :, 0:256].reshape(256, 256))
        qkv = acc.astype(BF)
        bias = deep_bias[pl.ds(pl.multiple_of((8 * e + 2 * y) * T, 2 * T), 2 * T), :]
        mixed = []
        for b in range(BANDS):
            rows = qkv[b * T : (b + 1) * T]
            mixed.append(attend(rows[:, 0:64], rows[:, 64:128], rows[:, 128:192], bias, two))
        mixed = jnp.concatenate(mixed, axis=0)
        wide = jnp.concatenate([jnp.zeros((BANDS * T, 192), BF), mixed], axis=1)
        for j in range(8):
            out[j] = out[j] + dot_t(wide, dw[e, j, :, :, 0:256].reshape(256, 256))
    for j in range(8):
        rs_send[0, :, j] = out[j].astype(BF).reshape(BANDS, T, 256)
    scatter(0)
    step(1, 1)
    step(2, 1)
    lax.fori_loop(6, 12, top_rows, 0)
    step(1, 2)
    step(2, 2)
    column = pl.ds(pl.multiple_of(m * 256, 256), 256)
    own_mid[...] = (deep_x[:, column] + gathered_sum(0)).astype(BF)
    share()
    top_ready(0, 0)
    top_send(0, 1)
    top_ready(1, 0)
    top_send(1, 1)
    step(1, 3)
    step(2, 3)
    second_z()
    lax.fori_loop(12, 18, top_rows, 0)
    step_key = keys_ref[1:2, :]
    gone = ((step_key < 0) & (band == 0)) | ((step_key > 0) & (band == 31))
    mask_one = mask_one_ref[...] + jnp.where(gone, NEG, 0.0)
    for w in range(4):
        for h in range(2):
            g = (2 * w + h) * T
            bias_zero[g : g + USED, :] = top_raw[:, 8 * w + h, 0:T] + mask_zero_ref[0:USED, :]
            bias_zero[g + USED : g + T, :] = mask_zero_ref[USED:T, :]
            bias_one[g : g + USED, :] = top_raw[:, 8 * w + 2 + h, :] + mask_one[0:USED, :]
            bias_one[g + USED : g + T, :] = mask_one[USED:T, :]
    heads = heads_ref[...]
    own_skip = dot(pick_ref[x], skip_ref[...].reshape(288, 512))
    step(1, 4)
    step(2, 4)
    shared()
    normed_two = []
    for b in range(BANDS):
        middle = jnp.concatenate([mids[b, j] for j in range(8)], axis=1).astype(F32)
        normed_two.append(norm_rows(middle, deep_gain_ref[1:2, :]))
    normed_two = jnp.concatenate(normed_two, axis=0)
    finish(1)
    finish(2)
    out = [0.0] * 8
    for e in range(2):
        acc = jnp.zeros((BANDS * T, 256), F32)
        for j in range(8):
            block = dw[e, j, :, :, 256:512].reshape(256, 256)
            acc = acc + dot(normed_two[:, 256 * j : 256 * j + 256], block)
        hidden = gelu(acc).astype(BF)
        for j in range(8):
            out[j] = out[j] + dot_t(hidden, dw[e, j, :, :, 512:768].reshape(256, 256))
    for j in range(8):
        rs_send[1, :, j] = out[j].astype(BF).reshape(BANDS, T, 256)
    scatter(1)
    top_relay(0, 1)
    top_relay(1, 1)
    step(3, 1)
    outs[m] = (own_mid[...].astype(F32) + gathered_sum(1)).astype(BF)
    share_out()
    step(3, 2)
    expand_ready()
    shared_out()
    acc = jnp.zeros((T, 256), F32)
    for j in range(8):
        acc = acc + dot(outs[j], dw[c, j, :, :, 768:1024].reshape(256, 256))
    grown = acc.astype(BF)
    for w in range(4):
        chosen = dot(grow_ref[w], grown) * part_ref[...]
        piece = chosen[:, 0:64] + chosen[:, 64:128] + chosen[:, 128:192] + chosen[:, 192:256]
        grow_send[w] = jnp.concatenate([piece, jnp.zeros((T, 64), F32)], axis=1).astype(BF)
    for d in range(1, 8):
        send(grow_send.at[ms[d] // 2], grow_recv.at[m], s_grow.at[d - 1], r_grow.at[d - 1], at_m(d))
    step(3, 3)
    grow_recv[m] = grow_send[x]
    for d in range(1, 8):
        await_at(grow_recv.at[ms[(-d) % 8]], s_grow.at[d - 1], r_grow.at[d - 1], at_m(d))
    window = jnp.concatenate([grow_recv[j][:, 0:64] for j in range(8)], axis=1)
    state = (own_skip + window.astype(F32)).astype(BF)

    for layer in range(2):
        if layer == 0:
            top_ready(0, 1)
            top_ready(1, 1)
        else:
            step(3, 4)
        base = 768 * layer
        normed = norm_rows(state.astype(F32), top_gain_ref[layer, 0:1, :])
        parts = []
        for w in range(4):
            block = tw[w, :, :, :, base : base + 256].reshape(512, 256)
            parts.append(dot(normed, block).astype(BF))
        q = jnp.concatenate([p[:, 0:64] for p in parts], axis=1)
        k = jnp.concatenate([p[:, 64:128] for p in parts], axis=1)
        v = jnp.concatenate([p[:, 128:192] for p in parts], axis=1)
        if layer == 0:
            mixed = attend(q, k, v, bias_zero[...], heads)
        else:
            kv = jnp.concatenate([k, v], axis=1)
            halo_send[...] = dot(take_ref[...], kv).astype(BF)
            halo[0:T, :] = kv
            for e, (band_step, x_step, r0, nr, c0, nc, off, size) in enumerate(PIECES):
                src = halo_send.at[pl.ds(off - T, size)]
                dst = halo.at[pl.ds(off, size)]
                send(src, dst, s_halo.at[e], r_halo.at[e], at_piece(-band_step, -x_step))
            for e, (band_step, x_step, r0, nr, c0, nc, off, size) in enumerate(PIECES):
                dst = halo.at[pl.ds(off, size)]
                await_at(dst, s_halo.at[e], r_halo.at[e], at_piece(-band_step, -x_step))
            mixed = attend(q, halo[:, 0:256], halo[:, 256:512], bias_one[...], heads)
        total = jnp.zeros((T, 512), F32)
        for w in range(4):
            block = tw[w, :, :, :, base : base + 256].reshape(512, 256)
            wide = jnp.concatenate([jnp.zeros((T, 192), BF), mixed[:, 64 * w : 64 * w + 64]], axis=1)
            total = total + dot_t(wide, block)
        swap(2 * layer, total)
        middle = (state.astype(F32) + swapped(2 * layer)).astype(BF)
        normed = norm_rows(middle.astype(F32), top_gain_ref[layer, 1:2, :])
        total = jnp.zeros((T, 512), F32)
        for w in range(4):
            block = tw[w, :, :, :, base + 256 : base + 512].reshape(512, 256)
            hidden = gelu(dot(normed, block)).astype(BF)
            total = total + dot_t(hidden, tw[w, :, :, :, base + 512 : base + 768].reshape(512, 256))
        swap(2 * layer + 1, total)
        state = (middle.astype(F32) + swapped(2 * layer + 1)).astype(BF)

    for half in range(2):
        fin[x, half] = state[:, 256 * half : 256 * half + 256]
    for d in (1, 2, 3):
        for e in range(2):
            core = lax.rem(c + e, 2)
            ss, rs = s_fin.at[d - 1, e], r_fin.at[d - 1, e]
            send(fin.at[x, c], fin.at[x, c], ss, rs, at_x(d, core))
    for d in (1, 2, 3):
        for e in range(2):
            core = lax.rem(c + e, 2)
            ss, rs = s_fin.at[d - 1, e], r_fin.at[d - 1, e]
            await_at(fin.at[xs[(-d) % 4], core], ss, rs, at_x(d, core))
    for half in range(2):
        stacked = jnp.concatenate([fin[w, half] for w in range(4)], axis=0)
        rows = dot(place_ref[...], stacked).astype(BF).reshape(6, 48, 256)
        out_ref[:, :, 256 * half : 256 * half + 256] = rows
    for cp in sends:
        cp.wait_send()
    for cond, cp in conditional:
        pl.when(cond)(cp.wait_send)


def local(
    skip_features,
    deep_features,
    top_gains,
    top_heads_in,
    top_heads_out,
    top_hidden_in,
    top_hidden_out,
    top_offsets,
    deep_gains,
    deep_offsets,
    deep_heads_in,
    deep_heads_out,
    deep_hidden_in,
    deep_hidden_out,
    expand_weight,
):
    constants = [jnp.asarray(a) for a in tables()]
    operands = [
        skip_features,
        deep_features,
        top_gains,
        deep_gains,
        top_offsets.transpose(0, 2, 1, 3),
        deep_offsets.transpose(1, 0, 2),
        deep_heads_in.transpose(1, 0, 2),
        deep_heads_out.T,
        deep_hidden_in,
        deep_hidden_out.T,
        expand_weight,
        top_heads_in.transpose(0, 2, 1, 3),
        top_heads_out.transpose(0, 2, 1),
        top_hidden_in,
        top_hidden_out.transpose(0, 2, 1),
        *constants,
    ]
    dma = pltpu.SemaphoreType.DMA
    shapes = [(3, 3), (4, 2, 8), (4,), (8,), (2,), (2,), (8,), (3,), (3,), (2, 2, 2), (2, 2, 2), (3,)]
    shapes += [(3, 2, 9), (1,), (2, 16), (16,), (7,), (7,), (4,), (8,), (3, 2)]
    vmem = pl.BlockSpec(memory_space=pltpu.VMEM)
    return pl.pallas_call(
        kernel,
        out_shape=jax.ShapeDtypeStruct((6, 48, 512), BF),
        in_specs=[vmem] * len(operands),
        out_specs=vmem,
        scratch_shapes=[
            pltpu.VMEM((2, 8, 4, 64, 1024), BF),
            pltpu.VMEM((4, 64, 768), BF),
            pltpu.VMEM((4, 8, 4, 16, 1536), BF),
            pltpu.VMEM((4, 8, 256), F32),
            pltpu.VMEM((2, 8, 128), F32),
            pltpu.VMEM((USED, 16, T), F32),
            pltpu.VMEM((16 * T, T), F32),
            pltpu.VMEM((USED, 32, EXT), F32),
            pltpu.VMEM((8 * T, T), F32),
            pltpu.VMEM((8 * T, EXT), F32),
            pltpu.VMEM((T, 2048), F32),
            pltpu.VMEM((4, T, 2048), BF),
            pltpu.VMEM((2, BANDS, 8, T, 256), BF),
            pltpu.VMEM((2, 4, 4, T, 256), BF),
            pltpu.VMEM((T, 256), BF),
            pltpu.VMEM((BANDS, 8, T, 256), BF),
            pltpu.VMEM((8, T, 256), BF),
            pltpu.VMEM((4, T, 128), BF),
            pltpu.VMEM((8, T, 128), BF),
            pltpu.VMEM((4, T, 512), BF),
            pltpu.VMEM((4, T, 512), BF),
            pltpu.VMEM((EXT - T, 512), BF),
            pltpu.VMEM((EXT, 512), BF),
            pltpu.VMEM((4, 2, T, 256), BF),
        ]
        + [dma(s) for s in shapes for _ in range(2)],
        compiler_params=pltpu.CompilerParams(
            collective_id=0, has_side_effects=True, vmem_limit_bytes=56 * 2**20
        ),
    )(*operands)


def solution(mesh):
    placed = (
        P("band", None, None),
        P("band", None, None),
        P(),
        P(None, "band", None, "mp"),
        P(None, "mp", "band"),
        P(None, "band", "mp"),
        P(None, "mp", "band"),
        P(None, "mp", None, None),
        P(),
        P("mp", None, None),
        P("band", None, "mp"),
        P("mp", "band"),
        P("band", "mp"),
        P("mp", "band"),
        P("band", None, "mp"),
    )
    return jax.shard_map(
        local, mesh=mesh, in_specs=placed, out_specs=P("band", None, None), check_vma=False
    )
```

```python
import functools

import jax
import jax.numpy as jnp
import numpy as np
from jax import lax
from jax.experimental import pallas as pl
from jax.experimental.pallas import tpu as pltpu
from jax.sharding import PartitionSpec as P

BF = jnp.bfloat16
F32 = jnp.float32
EPS = 1e-05
NEG = -1e30
T = 80
USED = 72
EXT = 400
SCALE = 32 ** (-0.5)
MESH = pl.DeviceIdType.MESH
BANDS = 2

PIECES = (
    (-1, 0, 3, 3, 0, 12, 80, 48),
    (1, 0, 0, 3, 0, 12, 128, 48),
    (0, -1, 0, 6, 6, 6, 176, 48),
    (0, 1, 0, 6, 0, 6, 224, 48),
    (-1, -1, 3, 3, 6, 6, 272, 32),
    (-1, 1, 3, 3, 0, 6, 304, 32),
    (1, -1, 0, 3, 6, 6, 336, 32),
    (1, 1, 0, 3, 0, 6, 368, 32),
)


@functools.lru_cache(None)
def tables():
    key_row = np.zeros(EXT, np.int32)
    key_col = np.zeros(EXT, np.int32)
    key_ok = np.zeros(EXT, bool)
    key_step = np.zeros(EXT, np.int32)
    t = np.arange(USED)
    key_row[:USED], key_col[:USED], key_ok[:USED] = t // 12, t % 12, True
    take = np.zeros((EXT, T), np.float32)
    for band_step, x_step, r0, nr, c0, nc, off, _ in PIECES:
        p = np.arange(nr * nc)
        r, c = r0 + p // nc, c0 + p % nc
        key_row[off : off + nr * nc] = r + 6 * band_step
        key_col[off : off + nr * nc] = c + 12 * x_step
        key_ok[off : off + nr * nc] = True
        key_step[off : off + nr * nc] = band_step
        take[off + p, r * 12 + c] = 1.0
    keys = np.zeros((8, EXT), np.int32)
    keys[0] = np.where(key_ok, 23 * key_row + key_col, -100000)
    keys[1] = key_step
    q_row, q_col = np.zeros(T, np.int32), np.zeros(T, np.int32)
    q_row[:USED], q_col[:USED] = t // 12, t % 12
    same = ((q_row >= 3)[:, None] == (key_row >= 3)[None]) & (
        (q_col >= 6)[:, None] == (key_col >= 6)[None]
    )
    mask_one = np.where(same & key_ok[None], 0.0, NEG).astype(np.float32)
    mask_zero = np.where((np.arange(T) < USED)[None], 0.0, NEG).astype(np.float32)
    mask_zero = np.broadcast_to(mask_zero, (T, T)).copy()
    deep_row, deep_col = np.zeros(T, np.int32), np.zeros(T, np.int32)
    deep_row[:USED], deep_col[:USED] = t // 24, t % 24
    deep_keys = np.full((8, T), -100000, np.int32)
    deep_keys[:, :USED] = 11 * deep_row[:USED] + deep_col[:USED] % 6
    ok = (np.arange(T) < USED)[None] & ((deep_col // 6)[:, None] == (deep_col // 6)[None])
    mask_deep = np.where(ok, 0.0, NEG).astype(np.float32)
    grow = np.zeros((4, T, T), np.float32)
    part = np.zeros((T, 4), np.float32)
    i, k = t // 12, t % 12
    for w in range(4):
        grow[w, t, (i // 2) * 24 + 6 * w + k // 2] = 1.0
    part[t, 2 * (i % 2) + k % 2] = 1.0
    part = np.repeat(part[:, :, None], 64, axis=2).reshape(T, 256)
    pick = np.zeros((4, T, 288), np.float32)
    place = np.zeros((288, 4 * T), np.float32)
    for w in range(4):
        pick[w, t, i * 48 + 12 * w + k] = 1.0
        place[i * 48 + 12 * w + k, w * T + t] = 1.0
    heads = np.zeros((8 * T, 256), np.float32)
    for h in range(8):
        heads[h * T : (h + 1) * T, h * 32 : (h + 1) * 32] = 1.0
    return (
        keys,
        mask_one,
        mask_zero,
        deep_keys,
        mask_deep,
        grow.astype(jnp.bfloat16),
        part,
        pick.astype(jnp.bfloat16),
        place.astype(jnp.bfloat16),
        take[T:].astype(jnp.bfloat16),
        heads.astype(jnp.bfloat16),
    )


def dot(a, b):
    return jnp.dot(a, b, preferred_element_type=F32)


def dot_t(a, b):
    return lax.dot_general(a, b, (((1,), (1,)), ((), ())), preferred_element_type=F32)


def thirds(values):
    first = values.astype(BF)
    rest = values - first.astype(F32)
    second = rest.astype(BF)
    third = (rest - second.astype(F32)).astype(BF)
    return jnp.concatenate([first, second, third], axis=0)


def norm_rows(values, scales):
    centred = values - jnp.mean(values, axis=-1, keepdims=True)
    spread = jnp.mean(centred * centred, axis=-1, keepdims=True)
    return (centred * lax.rsqrt(spread + EPS) * scales).astype(BF)


def gelu(values):
    return values * 0.5 * (1.0 + lax.erf(values * (0.5**0.5)))


def attend(q, k, v, bias, heads):
    count = heads.shape[0] // T
    stacked = jnp.concatenate([q] * count, axis=0) * heads
    scores = dot_t(stacked, k) * SCALE + bias
    weights = jnp.exp(scores - jnp.max(scores, axis=-1, keepdims=True))
    weights = (weights * (1.0 / jnp.sum(weights, axis=-1, keepdims=True))).astype(BF)
    mixed = dot(weights, v) * heads.astype(F32)
    total = mixed[0:T]
    for h in range(1, count):
        total = total + mixed[h * T : (h + 1) * T]
    return total.astype(BF)


def kernel(
    skip_ref,
    deep_ref,
    top_gain_ref,
    deep_gain_ref,
    top_tab_ref,
    deep_tab_ref,
    heads_in_ref,
    heads_out_ref,
    hidden_in_ref,
    hidden_out_ref,
    expand_ref,
    top_heads_in_ref,
    top_heads_out_ref,
    top_hidden_in_ref,
    top_hidden_out_ref,
    keys_ref,
    mask_one_ref,
    mask_zero_ref,
    deep_keys_ref,
    mask_deep_ref,
    grow_ref,
    part_ref,
    pick_ref,
    place_ref,
    take_ref,
    heads_ref,
    out_ref,
    dw,
    quarters,
    tw,
    tabs,
    deep_tabs,
    deep_raw,
    deep_bias,
    top_raw,
    bias_zero,
    bias_one,
    deep_x,
    deep_n,
    rs_send,
    rs_recv,
    own_mid,
    mids,
    outs,
    grow_send,
    grow_recv,
    swap_send,
    swap_recv,
    halo_send,
    halo,
    fin,
    s_q,
    r_q,
    s_z,
    r_z,
    s_n,
    r_n,
    s_ez,
    r_ez,
    s_ey,
    r_ey,
    s_ef,
    r_ef,
    s_tz,
    r_tz,
    s_ty,
    r_ty,
    s_tx,
    r_tx,
    s_tf,
    r_tf,
    s_tg,
    r_tg,
    s_tab,
    r_tab,
    s_f,
    r_f,
    s_dt,
    r_dt,
    s_rs,
    r_rs,
    s_ag,
    r_ag,
    s_out,
    r_out,
    s_grow,
    r_grow,
    s_swap,
    r_swap,
    s_halo,
    r_halo,
    s_fin,
    r_fin,
):
    band = lax.axis_index("band")
    m = lax.axis_index("mp")
    z, y, x, c = band // 4, band % 4, m // 2, m % 2
    zs = [lax.rem(z + d, 8) for d in range(8)]
    ys = [lax.rem(y + d, 4) for d in range(4)]
    xs = [lax.rem(x + d, 4) for d in range(4)]
    ms = [lax.rem(m + d, 8) for d in range(8)]
    other = 1 - c

    def at_z(d):
        return {"band": zs[d % 8] * 4 + y, "mp": m}

    def at_y(d):
        return {"band": z * 4 + ys[d % 4], "mp": m}

    def at_m(d):
        return {"band": band, "mp": ms[d % 8]}

    def at_plane(dx, dy):
        return {"band": z * 4 + ys[dy % 4], "mp": xs[dx % 4] * 2 + c}

    def at_x(d, core):
        return {"band": band, "mp": xs[d % 4] * 2 + core}

    def at_piece(band_step, x_step):
        return {"band": lax.rem(band + band_step + 32, 32), "mp": xs[x_step % 4] * 2 + c}

    barrier = pltpu.get_barrier_semaphore()
    greeted = [at_z(1), at_z(7), at_x(0, other)]
    greeted += [at_y(d) for d in (1, 2, 3)] + [at_x(d, c) for d in (1, 2, 3)]
    for who in greeted:
        pl.semaphore_signal(barrier, inc=1, device_id=who, device_id_type=MESH)

    sends = []

    def copy(src, dst, ss, rs, who):
        return pltpu.make_async_remote_copy(
            src_ref=src, dst_ref=dst, send_sem=ss, recv_sem=rs, device_id=who, device_id_type=MESH
        )

    def send(src, dst, ss, rs, who):
        cp = copy(src, dst, ss, rs, who)
        cp.start()
        sends.append(cp)

    conditional = []

    def send_if(cond, src, dst, ss, rs, who):
        cp = copy(src, dst, ss, rs, who)
        pl.when(cond)(cp.start)
        conditional.append((cond, cp))

    def await_if(cond, dst, ss, rs, who):
        pl.when(cond)(copy(dst, dst, ss, rs, who).wait_recv)

    def await_at(dst, ss, rs, who):
        copy(dst, dst, ss, rs, who).wait_recv()

    for yy in range(4):
        lanes = slice(64 * yy, 64 * yy + 64)
        quarters[yy, :, 0:256] = jnp.concatenate(
            [heads_in_ref[0, :, lanes], heads_in_ref[1, :, lanes], heads_in_ref[2, :, lanes], heads_out_ref[:, lanes]],
            axis=1,
        )
        lanes = slice(256 * yy, 256 * yy + 256)
        quarters[yy, :, 256:512] = hidden_in_ref[:, lanes]
        quarters[yy, :, 512:768] = hidden_out_ref[:, lanes]
    dw[c, z, y, :, 0:768] = quarters[y]
    dw[c, z, y, :, 768:1024] = jnp.concatenate([expand_ref[:, i, :] for i in range(4)], axis=1)
    for layer in range(2):
        pieces = [top_heads_in_ref[layer, i] for i in range(3)] + [top_heads_out_ref[layer]]
        pieces += [top_hidden_in_ref[layer], top_hidden_out_ref[layer]]
        tw[x, z, y, :, 768 * layer : 768 * layer + 768] = jnp.concatenate(pieces, axis=1)
    flat = jnp.concatenate([deep_tab_ref[a] for a in range(5)] + [jnp.zeros((8, 73), F32)], axis=1)
    deep_tabs[c] = flat
    tabs[x] = jnp.zeros((8, 256), F32)
    for layer in range(2):
        flat = jnp.concatenate([top_tab_ref[layer, a] for a in range(11)] + [jnp.zeros((2, 3), F32)], axis=1)
        tabs[x, 2 * layer : 2 * layer + 2, :] = flat
    pl.semaphore_wait(barrier, len(greeted))

    def plane(zz, s, part):
        some = pl.ds(2 * part, 2)
        if s == 3:
            return tw.at[some, zz, :, :, pl.ds(768, 768)]
        return dw.at[c, zz, some, :, pl.ds(256 * s, 256)]

    def own(yy, s):
        return dw.at[c, z, yy, :, pl.ds(256 * s, 256)]

    def slot(way, dist):
        return dist - 1 if way > 0 else 3 + dist

    def part_of(way, dist):
        return None if dist < 4 else (0 if way > 0 else 1)

    def limit(part, way):
        return 4 if (part == 0) == (way > 0) else 3

    def hop(s, part, way, dist):
        ref = plane(zs[(-way * (dist - 1)) % 8], s, part)
        k = slot(way, dist)
        send(ref, ref, s_z.at[s, part, k], r_z.at[s, part, k], at_z(way))

    def hops(s):
        for part in range(2):
            for way in (1, -1):
                hop(s, part, way, 1)

    def forward(s, zz, part, k):
        if s < 3:
            ref = plane(zz, s, part)
            send(ref, ref, s_f.at[s, part, k], r_f.at[s, part, k], at_x(0, other))

    def finish(s):
        for part in range(2):
            for way, most in ((0, 1), (1, limit(part, 1)), (-1, limit(part, -1))):
                for dist in range(1, most + 1):
                    k = 8 if way == 0 else slot(way, dist)
                    zz = zs[(-way * dist) % 8]
                    ref = dw.at[other, zz, pl.ds(2 * part, 2), :, pl.ds(256 * s, 256)]
                    await_at(ref, s_f.at[s, part, k], r_f.at[s, part, k], at_x(0, other))

    def begin(s):
        for d in (1, 3, 2):
            src = quarters.at[ys[d], :, pl.ds(256 * s, 256)]
            send(src, own(y, s), s_q.at[s, d - 1], r_q.at[s, d - 1], at_y(d))

    def second(yy=None, xx=None):
        return tw.at[x if xx is None else xx, z, pl.ds(0, 4) if yy is None else yy, :, pl.ds(768, 768)]

    def second_y():
        for d in (1, 3, 2):
            send(second(y), second(y), s_ty.at[d - 1], r_ty.at[d - 1], at_y(d))

    def second_x():
        for d in (1, 3, 2):
            await_at(second(ys[(-d) % 4]), s_ty.at[d - 1], r_ty.at[d - 1], at_y(d))
        for d in (1, 3, 2):
            send(second(), second(), s_tx.at[d - 1], r_tx.at[d - 1], at_x(d, c))

    def second_z():
        for d in (1, 3, 2):
            await_at(second(None, xs[(-d) % 4]), s_tx.at[d - 1], r_tx.at[d - 1], at_x(d, c))
        hops(3)

    def begin_z(s):
        for d in (1, 3, 2):
            await_at(own(ys[(-d) % 4], s), s_q.at[s, d - 1], r_q.at[s, d - 1], at_y(d))
        hops(s)
        for part in range(2):
            forward(s, z, part, 8)

    def step(s, dist):
        for part in range(2):
            for way in (1, -1):
                if dist > limit(part, way):
                    continue
                k = slot(way, dist)
                ref = plane(zs[(-way * dist) % 8], s, part)
                await_at(ref, s_z.at[s, part, k], r_z.at[s, part, k], at_z(way))
                if dist < limit(part, way):
                    hop(s, part, way, dist + 1)
                forward(s, zs[(-way * dist) % 8], part, k)

    def expand_part(zz, part=None):
        rows = pl.ds(0, 64) if part is None else pl.ds(32 * part, 32)
        return dw.at[c, zz, y, rows, pl.ds(768, 256)]

    def top_part(zz, part=None):
        lanes = pl.ds(0, 768) if part is None else pl.ds(384 * part, 384)
        return tw.at[x, zz, y, :, lanes]

    def top_hop(way, dist):
        origin, k, part = zs[(-way * (dist - 1)) % 8], slot(way, dist), part_of(way, dist)
        ref = top_part(origin, part)
        send(ref, ref, s_tz.at[k], r_tz.at[k], at_z(way))

    def top_step(dist):
        for way in (1, -1):
            origin, k, part = zs[(-way * dist) % 8], slot(way, dist), part_of(way, dist)
            await_at(top_part(origin, part), s_tz.at[k], r_tz.at[k], at_z(way))
            if dist < 4:
                top_hop(way, dist + 1)

    def expand_hop(way, dist):
        origin, k, part = zs[(-way * (dist - 1)) % 8], slot(way, dist), part_of(way, dist)
        ref = expand_part(origin, part)
        send(ref, ref, s_ez.at[k], r_ez.at[k], at_z(way))

    def expand_step(dist):
        for way in (1, -1):
            origin, k, part = zs[(-way * dist) % 8], slot(way, dist), part_of(way, dist)
            await_at(expand_part(origin, part), s_ez.at[k], r_ez.at[k], at_z(way))
            if dist < 4:
                expand_hop(way, dist + 1)

    def expand_of(yy, half=None):
        zz = pl.ds(0, 8) if half is None else pl.ds(4 * half, 4)
        return dw.at[c, zz, yy, :, pl.ds(768, 256)]

    def top_of(half_of, xx, yy, half=None):
        zz = pl.ds(0, 8) if half is None else pl.ds(4 * half, 4)
        xx = pl.ds(0, 4) if xx is None else xx
        yy = pl.ds(0, 4) if yy is None else yy
        return tw.at[xx, zz, yy, :, pl.ds(384 * half_of, 384)]

    def top_ref(half_of, phase, d, half=None):
        along_y = (half_of == 0) == (phase == 0)
        if along_y:
            return top_of(half_of, x if phase == 0 else None, ys[d % 4], half)
        return top_of(half_of, xs[d % 4], y if phase == 0 else None, half)

    def top_who(half_of, phase, d):
        return at_y(d) if (half_of == 0) == (phase == 0) else at_x(d, c)

    def top_send(half_of, phase):
        ref = top_ref(half_of, phase, 0)
        for e, d in enumerate((1, 3)):
            ss, rs = s_tf.at[half_of, phase, e], r_tf.at[half_of, phase, e]
            send(ref, ref, ss, rs, top_who(half_of, phase, d))

    def top_relay(half_of, phase):
        for e, d in enumerate((1, 3)):
            ss, rs = s_tf.at[half_of, phase, e], r_tf.at[half_of, phase, e]
            await_at(top_ref(half_of, phase, -d), ss, rs, top_who(half_of, phase, d))
            half = top_ref(half_of, phase, -d, e)
            ss, rs = s_tg.at[half_of, phase, e], r_tg.at[half_of, phase, e]
            send(half, half, ss, rs, top_who(half_of, phase, d))

    def top_ready(half_of, phase):
        for e, d in enumerate((1, 3)):
            ss, rs = s_tg.at[half_of, phase, e], r_tg.at[half_of, phase, e]
            await_at(top_ref(half_of, phase, 2, e), ss, rs, top_who(half_of, phase, d))

    def expand_send():
        for e, d in enumerate((1, 3)):
            send(expand_of(y), expand_of(y), s_ey.at[e], r_ey.at[e], at_y(d))

    def expand_relay():
        for e, d in enumerate((1, 3)):
            yy = ys[4 - d]
            await_at(expand_of(yy), s_ey.at[e], r_ey.at[e], at_y(d))
            send(expand_of(yy, e), expand_of(yy, e), s_ef.at[e], r_ef.at[e], at_y(d))

    def expand_ready():
        for e, d in enumerate((1, 3)):
            await_at(expand_of(ys[2], e), s_ef.at[e], r_ef.at[e], at_y(d))

    steps = [(dx, dy) for dy in range(4) for dx in range(4) if dx or dy]
    steps.sort(key=lambda d: min(d[0], 4 - d[0]) + min(d[1], 4 - d[1]))
    keeper = y // 2
    sibling = at_x(0, other)

    def scatter(which):
        for d in (4, 3, 5, 2, 6, 1, 7, 0):
            for b in range(2):
                src, dst = rs_send.at[which, b, ms[d]], rs_recv.at[which, x, y]
                ss, rs = s_rs.at[which, 8 * b + d], r_rs.at[which, 4 * x + y]
                who = {"band": z * 4 + 2 * c + b, "mp": ms[d]}
                if d:
                    send(src, dst, ss, rs, who)
                else:
                    send_if(y != 2 * c + b, src, dst, ss, rs, who)

        @pl.when(c == keeper)
        def _():
            rs_recv[which, x, y] = rs_send[which, y % 2, m]

    def gathered_sum(which):
        await_if(c != keeper, rs_recv.at[which, x, y], s_rs.at[which, 0], r_rs.at[which, 4 * x + y], sibling)
        for dx, dy in steps:
            xx, yy = xs[(-dx) % 4], ys[(-dy) % 4]
            await_at(rs_recv.at[which, xx, yy], s_rs.at[which, 0], r_rs.at[which, 4 * xx + yy], sibling)
        total = rs_recv[which, 0, 0].astype(F32)
        for j in range(1, 16):
            total = total + rs_recv[which, j // 4, j % 4].astype(F32)
        return total

    def share():
        dst, rs = mids.at[y % 2, m], r_ag.at[8 * (y % 2) + m]
        for e, (dx, dy) in reversed(list(enumerate(steps))):
            who = {"band": z * 4 + ys[dy], "mp": 2 * xs[dx] + keeper}
            send(own_mid, dst, s_ag.at[e], rs, who)
        send_if(c != keeper, own_mid, dst, s_ag.at[15], rs, sibling)

        @pl.when(c == keeper)
        def _():
            mids[y % 2, m] = own_mid[...]

    def shared():
        for d in range(8):
            for b in range(2):
                j = ms[(-d) % 8]
                dst, ss, rs = mids.at[b, j], s_ag.at[0], r_ag.at[8 * b + j]
                if d:
                    await_at(dst, ss, rs, sibling)
                else:
                    await_if(y != 2 * c + b, dst, ss, rs, sibling)

    def share_out():
        for d in range(1, 8):
            send(outs.at[m], outs.at[m], s_out.at[d - 1], r_out.at[d - 1], at_m(d))

    def shared_out():
        for d in range(1, 8):
            await_at(outs.at[ms[(-d) % 8]], s_out.at[d - 1], r_out.at[d - 1], at_m(d))

    def swap(which, partial):
        swap_send[which] = partial.astype(BF)
        send(swap_send.at[which], swap_recv.at[which], s_swap.at[which], r_swap.at[which], at_x(0, other))

    def swapped(which):
        await_at(swap_recv.at[which], s_swap.at[which], r_swap.at[which], at_x(0, other))
        return swap_send[which].astype(F32) + swap_recv[which].astype(F32)

    begin(0)
    top_hop(1, 1)
    top_hop(-1, 1)
    expand_hop(1, 1)
    expand_hop(-1, 1)
    second_y()
    send(deep_tabs.at[c], deep_tabs.at[c], s_dt.at[0], r_dt.at[0], sibling)
    for d in (1, 2, 3):
        send(tabs.at[x], tabs.at[x], s_tab.at[d - 1], r_tab.at[d - 1], at_x(d, c))

    for i in range(3):
        deep_x[24 * i : 24 * i + 24, :] = deep_ref[i].astype(F32)
    deep_x[USED:T, :] = jnp.zeros((T - USED, 2048), F32)
    deep_n[y] = norm_rows(deep_x[...], deep_gain_ref[0:1, :])
    for d in (1, 3, 2):
        send_if(c == keeper, deep_n.at[y], deep_n.at[y], s_n.at[d - 1], r_n.at[y], at_y(d))


    begin(1)
    begin(2)
    top_step(1)
    expand_step(1)
    begin_z(0)
    top_step(2)
    expand_step(2)
    await_at(deep_tabs.at[other], s_dt.at[0], r_dt.at[0], sibling)
    deep_tab = thirds(deep_tabs[...].reshape(16, 128))
    deep_iota = lax.broadcasted_iota(jnp.int32, (128, T), 0) + deep_keys_ref[0:1, :]

    def deep_rows(g, carry):
        for e in range(8):
            n = 8 * g + e
            r = n // 24
            col = n - 24 * r
            want = (r + 2) * 11 + lax.rem(col, 6) + 5
            hot = jnp.where(deep_iota == want, 1.0, 0.0).astype(BF)
            got = dot(deep_tab, hot)
            deep_raw[n] = got[0:16] + got[16:32] + got[32:48]
        return carry

    step(0, 1)
    top_step(3)
    expand_step(3)
    second_x()
    lax.fori_loop(0, 4, deep_rows, 0)
    step(0, 2)
    top_step(4)
    expand_step(4)
    top_send(0, 0)
    top_send(1, 0)
    expand_send()
    lax.fori_loop(4, 9, deep_rows, 0)
    step(0, 3)
    begin_z(1)
    begin_z(2)
    top_relay(0, 0)
    top_relay(1, 0)
    for h in range(16):
        deep_bias[h * T : h * T + USED, :] = deep_raw[:, h, :] + mask_deep_ref[0:USED, :]
        deep_bias[h * T + USED : (h + 1) * T, :] = mask_deep_ref[USED:T, :]

    for d in (1, 2, 3):
        await_at(tabs.at[xs[(-d) % 4]], s_tab.at[d - 1], r_tab.at[d - 1], at_x(d, c))
    top_tab = thirds(tabs[...].reshape(32, 256))
    top_iota = lax.broadcasted_iota(jnp.int32, (256, EXT), 0) + keys_ref[0:1, :]

    def top_rows(g, carry):
        for e in range(4):
            n = 4 * g + e
            i = n // 12
            want = (i + 5) * 23 + (n - 12 * i) + 11
            hot = jnp.where(top_iota == want, 1.0, 0.0).astype(BF)
            got = dot(top_tab, hot)
            top_raw[n] = got[0:32] + got[32:64] + got[64:96]
        return carry

    lax.fori_loop(0, 6, top_rows, 0)
    step(0, 4)
    expand_relay()
    for b in range(2):
        yy = 2 * c + b
        await_if(y != yy, deep_n.at[yy], s_n.at[0], r_n.at[yy], sibling)

    finish(0)
    two = heads_ref[0 : 2 * T, 0:64]
    out = [0.0] * 8
    for e in range(2):
        acc = jnp.zeros((BANDS * T, 256), F32)
        for j in range(8):
            rows = deep_n[pl.ds(2 * c, 2), :, 256 * j : 256 * j + 256].reshape(BANDS * T, 256)
            acc = acc + dot(rows, dw[e, j, :, :, 0:256].reshape(256, 256))
        qkv = acc.astype(BF)
        bias = deep_bias[pl.ds(pl.multiple_of((8 * e + 2 * y) * T, 2 * T), 2 * T), :]
        mixed = []
        for b in range(BANDS):
            rows = qkv[b * T : (b + 1) * T]
            mixed.append(attend(rows[:, 0:64], rows[:, 64:128], rows[:, 128:192], bias, two))
        mixed = jnp.concatenate(mixed, axis=0)
        wide = jnp.concatenate([jnp.zeros((BANDS * T, 192), BF), mixed], axis=1)
        for j in range(8):
            out[j] = out[j] + dot_t(wide, dw[e, j, :, :, 0:256].reshape(256, 256))
    for j in range(8):
        rs_send[0, :, j] = out[j].astype(BF).reshape(BANDS, T, 256)
    scatter(0)
    step(1, 1)
    step(2, 1)
    lax.fori_loop(6, 12, top_rows, 0)
    step(1, 2)
    step(2, 2)
    column = pl.ds(pl.multiple_of(m * 256, 256), 256)
    own_mid[...] = (deep_x[:, column] + gathered_sum(0)).astype(BF)
    share()
    step(1, 3)
    step(2, 3)
    second_z()
    lax.fori_loop(12, 18, top_rows, 0)
    step_key = keys_ref[1:2, :]
    gone = ((step_key < 0) & (band == 0)) | ((step_key > 0) & (band == 31))
    mask_one = mask_one_ref[...] + jnp.where(gone, NEG, 0.0)
    for w in range(4):
        for h in range(2):
            g = (2 * w + h) * T
            bias_zero[g : g + USED, :] = top_raw[:, 8 * w + h, 0:T] + mask_zero_ref[0:USED, :]
            bias_zero[g + USED : g + T, :] = mask_zero_ref[USED:T, :]
            bias_one[g : g + USED, :] = top_raw[:, 8 * w + 2 + h, :] + mask_one[0:USED, :]
            bias_one[g + USED : g + T, :] = mask_one[USED:T, :]
    heads = heads_ref[...]
    own_skip = dot(pick_ref[x], skip_ref[...].reshape(288, 512))
    step(1, 4)
    step(2, 4)
    top_ready(0, 0)
    top_send(0, 1)
    top_ready(1, 0)
    top_send(1, 1)
    shared()
    normed_two = []
    for b in range(BANDS):
        middle = jnp.concatenate([mids[b, j] for j in range(8)], axis=1).astype(F32)
        normed_two.append(norm_rows(middle, deep_gain_ref[1:2, :]))
    normed_two = jnp.concatenate(normed_two, axis=0)
    finish(1)
    finish(2)
    out = [0.0] * 8
    for e in range(2):
        acc = jnp.zeros((BANDS * T, 256), F32)
        for j in range(8):
            block = dw[e, j, :, :, 256:512].reshape(256, 256)
            acc = acc + dot(normed_two[:, 256 * j : 256 * j + 256], block)
        hidden = gelu(acc).astype(BF)
        for j in range(8):
            out[j] = out[j] + dot_t(hidden, dw[e, j, :, :, 512:768].reshape(256, 256))
    for j in range(8):
        rs_send[1, :, j] = out[j].astype(BF).reshape(BANDS, T, 256)
    scatter(1)
    step(3, 1)
    outs[m] = (own_mid[...].astype(F32) + gathered_sum(1)).astype(BF)
    share_out()
    top_relay(0, 1)
    top_relay(1, 1)
    step(3, 2)
    expand_ready()
    shared_out()
    acc = jnp.zeros((T, 256), F32)
    for j in range(8):
        acc = acc + dot(outs[j], dw[c, j, :, :, 768:1024].reshape(256, 256))
    grown = acc.astype(BF)
    for w in range(4):
        chosen = dot(grow_ref[w], grown) * part_ref[...]
        piece = chosen[:, 0:64] + chosen[:, 64:128] + chosen[:, 128:192] + chosen[:, 192:256]
        grow_send[w] = jnp.concatenate([piece, jnp.zeros((T, 64), F32)], axis=1).astype(BF)
    for d in range(1, 8):
        send(grow_send.at[ms[d] // 2], grow_recv.at[m], s_grow.at[d - 1], r_grow.at[d - 1], at_m(d))
    step(3, 3)
    grow_recv[m] = grow_send[x]
    for d in range(1, 8):
        await_at(grow_recv.at[ms[(-d) % 8]], s_grow.at[d - 1], r_grow.at[d - 1], at_m(d))
    window = jnp.concatenate([grow_recv[j][:, 0:64] for j in range(8)], axis=1)
    state = (own_skip + window.astype(F32)).astype(BF)

    for layer in range(2):
        if layer == 0:
            top_ready(0, 1)
        else:
            step(3, 4)
        base = 768 * layer
        normed = norm_rows(state.astype(F32), top_gain_ref[layer, 0:1, :])
        parts = []
        for w in range(4):
            block = tw[w, :, :, :, base : base + 256].reshape(512, 256)
            parts.append(dot(normed, block).astype(BF))
        q = jnp.concatenate([p[:, 0:64] for p in parts], axis=1)
        k = jnp.concatenate([p[:, 64:128] for p in parts], axis=1)
        v = jnp.concatenate([p[:, 128:192] for p in parts], axis=1)
        if layer == 0:
            mixed = attend(q, k, v, bias_zero[...], heads)
        else:
            kv = jnp.concatenate([k, v], axis=1)
            halo_send[...] = dot(take_ref[...], kv).astype(BF)
            halo[0:T, :] = kv
            for e, (band_step, x_step, r0, nr, c0, nc, off, size) in enumerate(PIECES):
                src = halo_send.at[pl.ds(off - T, size)]
                dst = halo.at[pl.ds(off, size)]
                send(src, dst, s_halo.at[e], r_halo.at[e], at_piece(-band_step, -x_step))
            for e, (band_step, x_step, r0, nr, c0, nc, off, size) in enumerate(PIECES):
                dst = halo.at[pl.ds(off, size)]
                await_at(dst, s_halo.at[e], r_halo.at[e], at_piece(-band_step, -x_step))
            mixed = attend(q, halo[:, 0:256], halo[:, 256:512], bias_one[...], heads)
        total = jnp.zeros((T, 512), F32)
        for w in range(4):
            block = tw[w, :, :, :, base : base + 256].reshape(512, 256)
            wide = jnp.concatenate([jnp.zeros((T, 192), BF), mixed[:, 64 * w : 64 * w + 64]], axis=1)
            total = total + dot_t(wide, block)
        swap(2 * layer, total)
        if layer == 0:
            top_ready(1, 1)
        middle = (state.astype(F32) + swapped(2 * layer)).astype(BF)
        normed = norm_rows(middle.astype(F32), top_gain_ref[layer, 1:2, :])
        total = jnp.zeros((T, 512), F32)
        for w in range(4):
            block = tw[w, :, :, :, base + 256 : base + 512].reshape(512, 256)
            hidden = gelu(dot(normed, block)).astype(BF)
            total = total + dot_t(hidden, tw[w, :, :, :, base + 512 : base + 768].reshape(512, 256))
        swap(2 * layer + 1, total)
        state = (middle.astype(F32) + swapped(2 * layer + 1)).astype(BF)

    for half in range(2):
        fin[x, half] = state[:, 256 * half : 256 * half + 256]
    for d in (1, 2, 3):
        for e in range(2):
            core = lax.rem(c + e, 2)
            ss, rs = s_fin.at[d - 1, e], r_fin.at[d - 1, e]
            send(fin.at[x, c], fin.at[x, c], ss, rs, at_x(d, core))
    for d in (1, 2, 3):
        for e in range(2):
            core = lax.rem(c + e, 2)
            ss, rs = s_fin.at[d - 1, e], r_fin.at[d - 1, e]
            await_at(fin.at[xs[(-d) % 4], core], ss, rs, at_x(d, core))
    for half in range(2):
        stacked = jnp.concatenate([fin[w, half] for w in range(4)], axis=0)
        rows = dot(place_ref[...], stacked).astype(BF).reshape(6, 48, 256)
        out_ref[:, :, 256 * half : 256 * half + 256] = rows
    for cp in sends:
        cp.wait_send()
    for cond, cp in conditional:
        pl.when(cond)(cp.wait_send)


def local(
    skip_features,
    deep_features,
    top_gains,
    top_heads_in,
    top_heads_out,
    top_hidden_in,
    top_hidden_out,
    top_offsets,
    deep_gains,
    deep_offsets,
    deep_heads_in,
    deep_heads_out,
    deep_hidden_in,
    deep_hidden_out,
    expand_weight,
):
    constants = [jnp.asarray(a) for a in tables()]
    operands = [
        skip_features,
        deep_features,
        top_gains,
        deep_gains,
        top_offsets.transpose(0, 2, 1, 3),
        deep_offsets.transpose(1, 0, 2),
        deep_heads_in.transpose(1, 0, 2),
        deep_heads_out.T,
        deep_hidden_in,
        deep_hidden_out.T,
        expand_weight,
        top_heads_in.transpose(0, 2, 1, 3),
        top_heads_out.transpose(0, 2, 1),
        top_hidden_in,
        top_hidden_out.transpose(0, 2, 1),
        *constants,
    ]
    dma = pltpu.SemaphoreType.DMA
    shapes = [(3, 3), (4, 2, 8), (4,), (8,), (2,), (2,), (8,), (3,), (3,), (2, 2, 2), (2, 2, 2), (3,)]
    shapes += [(3, 2, 9), (1,), (2, 16), (16,), (7,), (7,), (4,), (8,), (3, 2)]
    vmem = pl.BlockSpec(memory_space=pltpu.VMEM)
    return pl.pallas_call(
        kernel,
        out_shape=jax.ShapeDtypeStruct((6, 48, 512), BF),
        in_specs=[vmem] * len(operands),
        out_specs=vmem,
        scratch_shapes=[
            pltpu.VMEM((2, 8, 4, 64, 1024), BF),
            pltpu.VMEM((4, 64, 768), BF),
            pltpu.VMEM((4, 8, 4, 16, 1536), BF),
            pltpu.VMEM((4, 8, 256), F32),
            pltpu.VMEM((2, 8, 128), F32),
            pltpu.VMEM((USED, 16, T), F32),
            pltpu.VMEM((16 * T, T), F32),
            pltpu.VMEM((USED, 32, EXT), F32),
            pltpu.VMEM((8 * T, T), F32),
            pltpu.VMEM((8 * T, EXT), F32),
            pltpu.VMEM((T, 2048), F32),
            pltpu.VMEM((4, T, 2048), BF),
            pltpu.VMEM((2, BANDS, 8, T, 256), BF),
            pltpu.VMEM((2, 4, 4, T, 256), BF),
            pltpu.VMEM((T, 256), BF),
            pltpu.VMEM((BANDS, 8, T, 256), BF),
            pltpu.VMEM((8, T, 256), BF),
            pltpu.VMEM((4, T, 128), BF),
            pltpu.VMEM((8, T, 128), BF),
            pltpu.VMEM((4, T, 512), BF),
            pltpu.VMEM((4, T, 512), BF),
            pltpu.VMEM((EXT - T, 512), BF),
            pltpu.VMEM((EXT, 512), BF),
            pltpu.VMEM((4, 2, T, 256), BF),
        ]
        + [dma(s) for s in shapes for _ in range(2)],
        compiler_params=pltpu.CompilerParams(
            collective_id=0, has_side_effects=True, vmem_limit_bytes=56 * 2**20
        ),
    )(*operands)


def solution(mesh):
    placed = (
        P("band", None, None),
        P("band", None, None),
        P(),
        P(None, "band", None, "mp"),
        P(None, "mp", "band"),
        P(None, "band", "mp"),
        P(None, "mp", "band"),
        P(None, "mp", None, None),
        P(),
        P("mp", None, None),
        P("band", None, "mp"),
        P("mp", "band"),
        P("band", "mp"),
        P("mp", "band"),
        P("band", None, "mp"),
    )
    return jax.shard_map(
        local, mesh=mesh, in_specs=placed, out_specs=P("band", None, None), check_vma=False
    )
```

```python
import functools

import jax
import jax.numpy as jnp
import numpy as np
from jax import lax
from jax.experimental import pallas as pl
from jax.experimental.pallas import tpu as pltpu
from jax.sharding import PartitionSpec as P

BF = jnp.bfloat16
F32 = jnp.float32
EPS = 1e-05
NEG = -1e30
T = 80
USED = 72
EXT = 400
SCALE = 32 ** (-0.5)
MESH = pl.DeviceIdType.MESH
FETCHED = (0, 16, 20, 21, 22, 23, 24, 25)
BANDS = 2

PIECES = (
    (-1, 0, 3, 3, 0, 12, 80, 48),
    (1, 0, 0, 3, 0, 12, 128, 48),
    (0, -1, 0, 6, 6, 6, 176, 48),
    (0, 1, 0, 6, 0, 6, 224, 48),
    (-1, -1, 3, 3, 6, 6, 272, 32),
    (-1, 1, 3, 3, 0, 6, 304, 32),
    (1, -1, 0, 3, 6, 6, 336, 32),
    (1, 1, 0, 3, 0, 6, 368, 32),
)


@functools.lru_cache(None)
def tables():
    key_row = np.zeros(EXT, np.int32)
    key_col = np.zeros(EXT, np.int32)
    key_ok = np.zeros(EXT, bool)
    key_step = np.zeros(EXT, np.int32)
    t = np.arange(USED)
    key_row[:USED], key_col[:USED], key_ok[:USED] = t // 12, t % 12, True
    take = np.zeros((EXT, T), np.float32)
    for band_step, x_step, r0, nr, c0, nc, off, _ in PIECES:
        p = np.arange(nr * nc)
        r, c = r0 + p // nc, c0 + p % nc
        key_row[off : off + nr * nc] = r + 6 * band_step
        key_col[off : off + nr * nc] = c + 12 * x_step
        key_ok[off : off + nr * nc] = True
        key_step[off : off + nr * nc] = band_step
        take[off + p, r * 12 + c] = 1.0
    keys = np.zeros((8, EXT), np.int32)
    keys[0] = np.where(key_ok, 23 * key_row + key_col, -100000)
    keys[1] = key_step
    q_row, q_col = np.zeros(T, np.int32), np.zeros(T, np.int32)
    q_row[:USED], q_col[:USED] = t // 12, t % 12
    same = ((q_row >= 3)[:, None] == (key_row >= 3)[None]) & (
        (q_col >= 6)[:, None] == (key_col >= 6)[None]
    )
    mask_one = np.where(same & key_ok[None], 0.0, NEG).astype(np.float32)
    mask_zero = np.where((np.arange(T) < USED)[None], 0.0, NEG).astype(np.float32)
    mask_zero = np.broadcast_to(mask_zero, (T, T)).copy()
    deep_row, deep_col = np.zeros(T, np.int32), np.zeros(T, np.int32)
    deep_row[:USED], deep_col[:USED] = t // 24, t % 24
    deep_keys = np.full((8, T), -100000, np.int32)
    deep_keys[:, :USED] = 11 * deep_row[:USED] + deep_col[:USED] % 6
    ok = (np.arange(T) < USED)[None] & ((deep_col // 6)[:, None] == (deep_col // 6)[None])
    mask_deep = np.where(ok, 0.0, NEG).astype(np.float32)
    grow = np.zeros((4, T, T), np.float32)
    part = np.zeros((T, 4), np.float32)
    i, k = t // 12, t % 12
    for w in range(4):
        grow[w, t, (i // 2) * 24 + 6 * w + k // 2] = 1.0
    part[t, 2 * (i % 2) + k % 2] = 1.0
    part = np.repeat(part[:, :, None], 64, axis=2).reshape(T, 256)
    pick = np.zeros((4, T, 288), np.float32)
    place = np.zeros((288, 4 * T), np.float32)
    for w in range(4):
        pick[w, t, i * 48 + 12 * w + k] = 1.0
        place[i * 48 + 12 * w + k, w * T + t] = 1.0
    heads = np.zeros((8 * T, 256), np.float32)
    for h in range(8):
        heads[h * T : (h + 1) * T, h * 32 : (h + 1) * 32] = 1.0
    return (
        keys,
        mask_one,
        mask_zero,
        deep_keys,
        mask_deep,
        grow.astype(jnp.bfloat16),
        part,
        pick.astype(jnp.bfloat16),
        place.astype(jnp.bfloat16),
        take[T:].astype(jnp.bfloat16),
        heads.astype(jnp.bfloat16),
    )


def dot(a, b):
    return jnp.dot(a, b, preferred_element_type=F32)


def dot_t(a, b):
    return lax.dot_general(a, b, (((1,), (1,)), ((), ())), preferred_element_type=F32)


def thirds(values):
    first = values.astype(BF)
    rest = values - first.astype(F32)
    second = rest.astype(BF)
    third = (rest - second.astype(F32)).astype(BF)
    return jnp.concatenate([first, second, third], axis=0)


def norm_rows(values, scales):
    centred = values - jnp.mean(values, axis=-1, keepdims=True)
    spread = jnp.mean(centred * centred, axis=-1, keepdims=True)
    return (centred * lax.rsqrt(spread + EPS) * scales).astype(BF)


def gelu(values):
    return values * 0.5 * (1.0 + lax.erf(values * (0.5**0.5)))


def attend(q, k, v, bias, heads):
    count = heads.shape[0] // T
    stacked = jnp.concatenate([q] * count, axis=0) * heads
    scores = dot_t(stacked, k) * SCALE + bias
    weights = jnp.exp(scores - jnp.max(scores, axis=-1, keepdims=True))
    weights = (weights * (1.0 / jnp.sum(weights, axis=-1, keepdims=True))).astype(BF)
    mixed = dot(weights, v) * heads.astype(F32)
    total = mixed[0:T]
    for h in range(1, count):
        total = total + mixed[h * T : (h + 1) * T]
    return total.astype(BF)


def kernel(
    skip_hbm,
    deep_ref,
    top_gain_ref,
    deep_gain_ref,
    top_tab_ref,
    deep_tab_ref,
    heads_in_ref,
    heads_out_ref,
    hidden_in_ref,
    hidden_out_ref,
    expand_ref,
    top_heads_in_ref,
    top_heads_out_ref,
    top_hidden_in_ref,
    top_hidden_out_ref,
    keys_ref,
    mask_one_hbm,
    mask_zero_ref,
    deep_keys_ref,
    mask_deep_ref,
    grow_hbm,
    part_hbm,
    pick_hbm,
    place_hbm,
    take_hbm,
    heads_hbm,
    out_ref,
    dw,
    quarters,
    tw,
    tabs,
    deep_tabs,
    deep_raw,
    deep_bias,
    top_raw,
    bias_zero,
    bias_one,
    deep_x,
    deep_n,
    rs_send,
    rs_recv,
    own_mid,
    mids,
    outs,
    grow_send,
    grow_recv,
    swap_send,
    swap_recv,
    halo_send,
    halo,
    fin,
    skip_ref,
    mask_one_ref,
    grow_ref,
    part_ref,
    pick_ref,
    place_ref,
    take_ref,
    heads_ref,
    s_fetch,
    s_q,
    r_q,
    s_z,
    r_z,
    s_n,
    r_n,
    s_ez,
    r_ez,
    s_ey,
    r_ey,
    s_ef,
    r_ef,
    s_tz,
    r_tz,
    s_ty,
    r_ty,
    s_tx,
    r_tx,
    s_tf,
    r_tf,
    s_tg,
    r_tg,
    s_tab,
    r_tab,
    s_f,
    r_f,
    s_dt,
    r_dt,
    s_rs,
    r_rs,
    s_ag,
    r_ag,
    s_out,
    r_out,
    s_grow,
    r_grow,
    s_swap,
    r_swap,
    s_halo,
    r_halo,
    s_fin,
    r_fin,
):
    band = lax.axis_index("band")
    m = lax.axis_index("mp")
    z, y, x, c = band // 4, band % 4, m // 2, m % 2
    zs = [lax.rem(z + d, 8) for d in range(8)]
    ys = [lax.rem(y + d, 4) for d in range(4)]
    xs = [lax.rem(x + d, 4) for d in range(4)]
    ms = [lax.rem(m + d, 8) for d in range(8)]
    other = 1 - c

    def at_z(d):
        return {"band": zs[d % 8] * 4 + y, "mp": m}

    def at_y(d):
        return {"band": z * 4 + ys[d % 4], "mp": m}

    def at_m(d):
        return {"band": band, "mp": ms[d % 8]}

    def at_plane(dx, dy):
        return {"band": z * 4 + ys[dy % 4], "mp": xs[dx % 4] * 2 + c}

    def at_x(d, core):
        return {"band": band, "mp": xs[d % 4] * 2 + core}

    def at_piece(band_step, x_step):
        return {"band": lax.rem(band + band_step + 32, 32), "mp": xs[x_step % 4] * 2 + c}

    fetched = [
        (skip_hbm, skip_ref),
        (mask_one_hbm, mask_one_ref),
        (grow_hbm, grow_ref),
        (part_hbm, part_ref),
        (pick_hbm, pick_ref),
        (place_hbm, place_ref),
        (take_hbm, take_ref),
        (heads_hbm, heads_ref),
    ]
    fetched = [pltpu.make_async_copy(a, b, s_fetch.at[i]) for i, (a, b) in enumerate(fetched)]
    for cp in fetched:
        cp.start()

    barrier = pltpu.get_barrier_semaphore()
    greeted = [at_z(1), at_z(7), at_x(0, other)]
    greeted += [at_y(d) for d in (1, 2, 3)] + [at_x(d, c) for d in (1, 2, 3)]
    for who in greeted:
        pl.semaphore_signal(barrier, inc=1, device_id=who, device_id_type=MESH)

    sends = []

    def copy(src, dst, ss, rs, who):
        return pltpu.make_async_remote_copy(
            src_ref=src, dst_ref=dst, send_sem=ss, recv_sem=rs, device_id=who, device_id_type=MESH
        )

    def send(src, dst, ss, rs, who):
        cp = copy(src, dst, ss, rs, who)
        cp.start()
        sends.append(cp)

    conditional = []

    def send_if(cond, src, dst, ss, rs, who):
        cp = copy(src, dst, ss, rs, who)
        pl.when(cond)(cp.start)
        conditional.append((cond, cp))

    def await_if(cond, dst, ss, rs, who):
        pl.when(cond)(copy(dst, dst, ss, rs, who).wait_recv)

    def await_at(dst, ss, rs, who):
        copy(dst, dst, ss, rs, who).wait_recv()

    for yy in range(4):
        lanes = slice(64 * yy, 64 * yy + 64)
        quarters[yy, :, 0:256] = jnp.concatenate(
            [heads_in_ref[0, :, lanes], heads_in_ref[1, :, lanes], heads_in_ref[2, :, lanes], heads_out_ref[:, lanes]],
            axis=1,
        )
        lanes = slice(256 * yy, 256 * yy + 256)
        quarters[yy, :, 256:512] = hidden_in_ref[:, lanes]
        quarters[yy, :, 512:768] = hidden_out_ref[:, lanes]
    dw[c, z, y, :, 0:768] = quarters[y]
    dw[c, z, y, :, 768:1024] = jnp.concatenate([expand_ref[:, i, :] for i in range(4)], axis=1)
    for layer in range(2):
        pieces = [top_heads_in_ref[layer, i] for i in range(3)] + [top_heads_out_ref[layer]]
        pieces += [top_hidden_in_ref[layer], top_hidden_out_ref[layer]]
        tw[x, z, y, :, 768 * layer : 768 * layer + 768] = jnp.concatenate(pieces, axis=1)
    flat = jnp.concatenate([deep_tab_ref[a] for a in range(5)] + [jnp.zeros((8, 73), F32)], axis=1)
    deep_tabs[c] = flat
    tabs[x] = jnp.zeros((8, 256), F32)
    for layer in range(2):
        flat = jnp.concatenate([top_tab_ref[layer, a] for a in range(11)] + [jnp.zeros((2, 3), F32)], axis=1)
        tabs[x, 2 * layer : 2 * layer + 2, :] = flat
    pl.semaphore_wait(barrier, len(greeted))

    def plane(zz, s, part):
        some = pl.ds(2 * part, 2)
        if s == 3:
            return tw.at[some, zz, :, :, pl.ds(768, 768)]
        return dw.at[c, zz, some, :, pl.ds(256 * s, 256)]

    def own(yy, s):
        return dw.at[c, z, yy, :, pl.ds(256 * s, 256)]

    def slot(way, dist):
        return dist - 1 if way > 0 else 3 + dist

    def part_of(way, dist):
        return None if dist < 4 else (0 if way > 0 else 1)

    def limit(part, way):
        return 4 if (part == 0) == (way > 0) else 3

    def hop(s, part, way, dist):
        ref = plane(zs[(-way * (dist - 1)) % 8], s, part)
        k = slot(way, dist)
        send(ref, ref, s_z.at[s, part, k], r_z.at[s, part, k], at_z(way))

    def hops(s):
        for part in range(2):
            for way in (1, -1):
                hop(s, part, way, 1)

    def forward(s, zz, part, k):
        if s < 3:
            ref = plane(zz, s, part)
            send(ref, ref, s_f.at[s, part, k], r_f.at[s, part, k], at_x(0, other))

    def finish(s):
        for part in range(2):
            for way, most in ((0, 1), (1, limit(part, 1)), (-1, limit(part, -1))):
                for dist in range(1, most + 1):
                    k = 8 if way == 0 else slot(way, dist)
                    zz = zs[(-way * dist) % 8]
                    ref = dw.at[other, zz, pl.ds(2 * part, 2), :, pl.ds(256 * s, 256)]
                    await_at(ref, s_f.at[s, part, k], r_f.at[s, part, k], at_x(0, other))

    def begin(s):
        for d in (1, 3, 2):
            src = quarters.at[ys[d], :, pl.ds(256 * s, 256)]
            send(src, own(y, s), s_q.at[s, d - 1], r_q.at[s, d - 1], at_y(d))

    def second(yy=None, xx=None):
        return tw.at[x if xx is None else xx, z, pl.ds(0, 4) if yy is None else yy, :, pl.ds(768, 768)]

    def second_y():
        for d in (1, 3, 2):
            send(second(y), second(y), s_ty.at[d - 1], r_ty.at[d - 1], at_y(d))

    def second_x():
        for d in (1, 3, 2):
            await_at(second(ys[(-d) % 4]), s_ty.at[d - 1], r_ty.at[d - 1], at_y(d))
        for d in (1, 3, 2):
            send(second(), second(), s_tx.at[d - 1], r_tx.at[d - 1], at_x(d, c))

    def second_z():
        for d in (1, 3, 2):
            await_at(second(None, xs[(-d) % 4]), s_tx.at[d - 1], r_tx.at[d - 1], at_x(d, c))
        hops(3)

    def begin_z(s):
        for d in (1, 3, 2):
            await_at(own(ys[(-d) % 4], s), s_q.at[s, d - 1], r_q.at[s, d - 1], at_y(d))
        hops(s)
        for part in range(2):
            forward(s, z, part, 8)

    def step(s, dist):
        for part in range(2):
            for way in (1, -1):
                if dist > limit(part, way):
                    continue
                k = slot(way, dist)
                ref = plane(zs[(-way * dist) % 8], s, part)
                await_at(ref, s_z.at[s, part, k], r_z.at[s, part, k], at_z(way))
                if dist < limit(part, way):
                    hop(s, part, way, dist + 1)
                forward(s, zs[(-way * dist) % 8], part, k)

    def expand_part(zz, part=None):
        rows = pl.ds(0, 64) if part is None else pl.ds(32 * part, 32)
        return dw.at[c, zz, y, rows, pl.ds(768, 256)]

    def top_part(zz, part=None):
        lanes = pl.ds(0, 768) if part is None else pl.ds(384 * part, 384)
        return tw.at[x, zz, y, :, lanes]

    def top_hop(way, dist):
        origin, k, part = zs[(-way * (dist - 1)) % 8], slot(way, dist), part_of(way, dist)
        ref = top_part(origin, part)
        send(ref, ref, s_tz.at[k], r_tz.at[k], at_z(way))

    def top_step(dist):
        for way in (1, -1):
            origin, k, part = zs[(-way * dist) % 8], slot(way, dist), part_of(way, dist)
            await_at(top_part(origin, part), s_tz.at[k], r_tz.at[k], at_z(way))
            if dist < 4:
                top_hop(way, dist + 1)

    def expand_hop(way, dist):
        origin, k, part = zs[(-way * (dist - 1)) % 8], slot(way, dist), part_of(way, dist)
        ref = expand_part(origin, part)
        send(ref, ref, s_ez.at[k], r_ez.at[k], at_z(way))

    def expand_step(dist):
        for way in (1, -1):
            origin, k, part = zs[(-way * dist) % 8], slot(way, dist), part_of(way, dist)
            await_at(expand_part(origin, part), s_ez.at[k], r_ez.at[k], at_z(way))
            if dist < 4:
                expand_hop(way, dist + 1)

    def expand_of(yy, half=None):
        zz = pl.ds(0, 8) if half is None else pl.ds(4 * half, 4)
        return dw.at[c, zz, yy, :, pl.ds(768, 256)]

    def top_of(half_of, xx, yy, half=None):
        zz = pl.ds(0, 8) if half is None else pl.ds(4 * half, 4)
        xx = pl.ds(0, 4) if xx is None else xx
        yy = pl.ds(0, 4) if yy is None else yy
        return tw.at[xx, zz, yy, :, pl.ds(384 * half_of, 384)]

    def top_ref(half_of, phase, d, half=None):
        along_y = (half_of == 0) == (phase == 0)
        if along_y:
            return top_of(half_of, x if phase == 0 else None, ys[d % 4], half)
        return top_of(half_of, xs[d % 4], y if phase == 0 else None, half)

    def top_who(half_of, phase, d):
        return at_y(d) if (half_of == 0) == (phase == 0) else at_x(d, c)

    def top_send(half_of, phase):
        ref = top_ref(half_of, phase, 0)
        for e, d in enumerate((1, 3)):
            ss, rs = s_tf.at[half_of, phase, e], r_tf.at[half_of, phase, e]
            send(ref, ref, ss, rs, top_who(half_of, phase, d))

    def top_relay(half_of, phase):
        for e, d in enumerate((1, 3)):
            ss, rs = s_tf.at[half_of, phase, e], r_tf.at[half_of, phase, e]
            await_at(top_ref(half_of, phase, -d), ss, rs, top_who(half_of, phase, d))
            half = top_ref(half_of, phase, -d, e)
            ss, rs = s_tg.at[half_of, phase, e], r_tg.at[half_of, phase, e]
            send(half, half, ss, rs, top_who(half_of, phase, d))

    def top_ready(half_of, phase):
        for e, d in enumerate((1, 3)):
            ss, rs = s_tg.at[half_of, phase, e], r_tg.at[half_of, phase, e]
            await_at(top_ref(half_of, phase, 2, e), ss, rs, top_who(half_of, phase, d))

    def expand_send():
        for e, d in enumerate((1, 3)):
            send(expand_of(y), expand_of(y), s_ey.at[e], r_ey.at[e], at_y(d))

    def expand_relay():
        for e, d in enumerate((1, 3)):
            yy = ys[4 - d]
            await_at(expand_of(yy), s_ey.at[e], r_ey.at[e], at_y(d))
            send(expand_of(yy, e), expand_of(yy, e), s_ef.at[e], r_ef.at[e], at_y(d))

    def expand_ready():
        for e, d in enumerate((1, 3)):
            await_at(expand_of(ys[2], e), s_ef.at[e], r_ef.at[e], at_y(d))

    steps = [(dx, dy) for dy in range(4) for dx in range(4) if dx or dy]
    steps.sort(key=lambda d: min(d[0], 4 - d[0]) + min(d[1], 4 - d[1]))
    keeper = y // 2
    sibling = at_x(0, other)

    def scatter(which):
        for d in (4, 3, 5, 2, 6, 1, 7, 0):
            for b in range(2):
                src, dst = rs_send.at[which, b, ms[d]], rs_recv.at[which, x, y]
                ss, rs = s_rs.at[which, 8 * b + d], r_rs.at[which, 4 * x + y]
                who = {"band": z * 4 + 2 * c + b, "mp": ms[d]}
                if d:
                    send(src, dst, ss, rs, who)
                else:
                    send_if(y != 2 * c + b, src, dst, ss, rs, who)

        @pl.when(c == keeper)
        def _():
            rs_recv[which, x, y] = rs_send[which, y % 2, m]

    def gathered_sum(which):
        await_if(c != keeper, rs_recv.at[which, x, y], s_rs.at[which, 0], r_rs.at[which, 4 * x + y], sibling)
        for dx, dy in steps:
            xx, yy = xs[(-dx) % 4], ys[(-dy) % 4]
            await_at(rs_recv.at[which, xx, yy], s_rs.at[which, 0], r_rs.at[which, 4 * xx + yy], sibling)
        total = rs_recv[which, 0, 0].astype(F32)
        for j in range(1, 16):
            total = total + rs_recv[which, j // 4, j % 4].astype(F32)
        return total

    def share():
        dst, rs = mids.at[y % 2, m], r_ag.at[8 * (y % 2) + m]
        for e, (dx, dy) in reversed(list(enumerate(steps))):
            who = {"band": z * 4 + ys[dy], "mp": 2 * xs[dx] + keeper}
            send(own_mid, dst, s_ag.at[e], rs, who)
        send_if(c != keeper, own_mid, dst, s_ag.at[15], rs, sibling)

        @pl.when(c == keeper)
        def _():
            mids[y % 2, m] = own_mid[...]

    def shared():
        for d in range(8):
            for b in range(2):
                j = ms[(-d) % 8]
                dst, ss, rs = mids.at[b, j], s_ag.at[0], r_ag.at[8 * b + j]
                if d:
                    await_at(dst, ss, rs, sibling)
                else:
                    await_if(y != 2 * c + b, dst, ss, rs, sibling)

    def share_out():
        for d in range(1, 8):
            send(outs.at[m], outs.at[m], s_out.at[d - 1], r_out.at[d - 1], at_m(d))

    def shared_out():
        for d in range(1, 8):
            await_at(outs.at[ms[(-d) % 8]], s_out.at[d - 1], r_out.at[d - 1], at_m(d))

    def swap(which, partial):
        swap_send[which] = partial.astype(BF)
        send(swap_send.at[which], swap_recv.at[which], s_swap.at[which], r_swap.at[which], at_x(0, other))

    def swapped(which):
        await_at(swap_recv.at[which], s_swap.at[which], r_swap.at[which], at_x(0, other))
        return swap_send[which].astype(F32) + swap_recv[which].astype(F32)

    begin(0)
    top_hop(1, 1)
    top_hop(-1, 1)
    expand_hop(1, 1)
    expand_hop(-1, 1)
    second_y()
    send(deep_tabs.at[c], deep_tabs.at[c], s_dt.at[0], r_dt.at[0], sibling)
    for d in (1, 2, 3):
        send(tabs.at[x], tabs.at[x], s_tab.at[d - 1], r_tab.at[d - 1], at_x(d, c))

    for cp in fetched:
        cp.wait()
    for i in range(3):
        deep_x[24 * i : 24 * i + 24, :] = deep_ref[i].astype(F32)
    deep_x[USED:T, :] = jnp.zeros((T - USED, 2048), F32)
    deep_n[y] = norm_rows(deep_x[...], deep_gain_ref[0:1, :])
    for d in (1, 3, 2):
        send_if(c == keeper, deep_n.at[y], deep_n.at[y], s_n.at[d - 1], r_n.at[y], at_y(d))


    begin(1)
    begin(2)
    top_step(1)
    expand_step(1)
    begin_z(0)
    top_step(2)
    expand_step(2)
    await_at(deep_tabs.at[other], s_dt.at[0], r_dt.at[0], sibling)
    deep_tab = thirds(deep_tabs[...].reshape(16, 128))
    deep_iota = lax.broadcasted_iota(jnp.int32, (128, T), 0) + deep_keys_ref[0:1, :]

    def deep_rows(g, carry):
        for e in range(8):
            n = 8 * g + e
            r = n // 24
            col = n - 24 * r
            want = (r + 2) * 11 + lax.rem(col, 6) + 5
            hot = jnp.where(deep_iota == want, 1.0, 0.0).astype(BF)
            got = dot(deep_tab, hot)
            deep_raw[n] = got[0:16] + got[16:32] + got[32:48]
        return carry

    step(0, 1)
    top_step(3)
    expand_step(3)
    second_x()
    lax.fori_loop(0, 4, deep_rows, 0)
    step(0, 2)
    top_step(4)
    expand_step(4)
    top_send(0, 0)
    top_send(1, 0)
    expand_send()
    lax.fori_loop(4, 9, deep_rows, 0)
    step(0, 3)
    top_relay(0, 0)
    top_relay(1, 0)
    for h in range(16):
        deep_bias[h * T : h * T + USED, :] = deep_raw[:, h, :] + mask_deep_ref[0:USED, :]
        deep_bias[h * T + USED : (h + 1) * T, :] = mask_deep_ref[USED:T, :]

    for d in (1, 2, 3):
        await_at(tabs.at[xs[(-d) % 4]], s_tab.at[d - 1], r_tab.at[d - 1], at_x(d, c))
    top_tab = thirds(tabs[...].reshape(32, 256))
    top_iota = lax.broadcasted_iota(jnp.int32, (256, EXT), 0) + keys_ref[0:1, :]

    def top_rows(g, carry):
        for e in range(4):
            n = 4 * g + e
            i = n // 12
            want = (i + 5) * 23 + (n - 12 * i) + 11
            hot = jnp.where(top_iota == want, 1.0, 0.0).astype(BF)
            got = dot(top_tab, hot)
            top_raw[n] = got[0:32] + got[32:64] + got[64:96]
        return carry

    lax.fori_loop(0, 6, top_rows, 0)
    step(0, 4)
    expand_relay()
    for b in range(2):
        yy = 2 * c + b
        await_if(y != yy, deep_n.at[yy], s_n.at[0], r_n.at[yy], sibling)

    begin_z(1)
    begin_z(2)
    finish(0)
    two = heads_ref[0 : 2 * T, 0:64]
    out = [0.0] * 8
    for e in range(2):
        acc = jnp.zeros((BANDS * T, 256), F32)
        for j in range(8):
            rows = deep_n[pl.ds(2 * c, 2), :, 256 * j : 256 * j + 256].reshape(BANDS * T, 256)
            acc = acc + dot(rows, dw[e, j, :, :, 0:256].reshape(256, 256))
        qkv = acc.astype(BF)
        bias = deep_bias[pl.ds(pl.multiple_of((8 * e + 2 * y) * T, 2 * T), 2 * T), :]
        mixed = []
        for b in range(BANDS):
            rows = qkv[b * T : (b + 1) * T]
            mixed.append(attend(rows[:, 0:64], rows[:, 64:128], rows[:, 128:192], bias, two))
        mixed = jnp.concatenate(mixed, axis=0)
        wide = jnp.concatenate([jnp.zeros((BANDS * T, 192), BF), mixed], axis=1)
        for j in range(8):
            out[j] = out[j] + dot_t(wide, dw[e, j, :, :, 0:256].reshape(256, 256))
    for j in range(8):
        rs_send[0, :, j] = out[j].astype(BF).reshape(BANDS, T, 256)
    scatter(0)
    step(1, 1)
    step(2, 1)
    lax.fori_loop(6, 12, top_rows, 0)
    step(1, 2)
    step(2, 2)
    column = pl.ds(pl.multiple_of(m * 256, 256), 256)
    own_mid[...] = (deep_x[:, column] + gathered_sum(0)).astype(BF)
    share()
    step(1, 3)
    step(2, 3)
    second_z()
    lax.fori_loop(12, 18, top_rows, 0)
    step_key = keys_ref[1:2, :]
    gone = ((step_key < 0) & (band == 0)) | ((step_key > 0) & (band == 31))
    mask_one = mask_one_ref[...] + jnp.where(gone, NEG, 0.0)
    for w in range(4):
        for h in range(2):
            g = (2 * w + h) * T
            bias_zero[g : g + USED, :] = top_raw[:, 8 * w + h, 0:T] + mask_zero_ref[0:USED, :]
            bias_zero[g + USED : g + T, :] = mask_zero_ref[USED:T, :]
            bias_one[g : g + USED, :] = top_raw[:, 8 * w + 2 + h, :] + mask_one[0:USED, :]
            bias_one[g + USED : g + T, :] = mask_one[USED:T, :]
    heads = heads_ref[...]
    own_skip = dot(pick_ref[x], skip_ref[...].reshape(288, 512))
    step(1, 4)
    step(2, 4)
    top_ready(0, 0)
    top_send(0, 1)
    top_ready(1, 0)
    top_send(1, 1)
    shared()
    normed_two = []
    for b in range(BANDS):
        middle = jnp.concatenate([mids[b, j] for j in range(8)], axis=1).astype(F32)
        normed_two.append(norm_rows(middle, deep_gain_ref[1:2, :]))
    normed_two = jnp.concatenate(normed_two, axis=0)
    finish(1)
    finish(2)
    out = [0.0] * 8
    for e in range(2):
        acc = jnp.zeros((BANDS * T, 256), F32)
        for j in range(8):
            block = dw[e, j, :, :, 256:512].reshape(256, 256)
            acc = acc + dot(normed_two[:, 256 * j : 256 * j + 256], block)
        hidden = gelu(acc).astype(BF)
        for j in range(8):
            out[j] = out[j] + dot_t(hidden, dw[e, j, :, :, 512:768].reshape(256, 256))
    for j in range(8):
        rs_send[1, :, j] = out[j].astype(BF).reshape(BANDS, T, 256)
    scatter(1)
    step(3, 1)
    outs[m] = (own_mid[...].astype(F32) + gathered_sum(1)).astype(BF)
    share_out()
    top_relay(0, 1)
    top_relay(1, 1)
    step(3, 2)
    expand_ready()
    shared_out()
    acc = jnp.zeros((T, 256), F32)
    for j in range(8):
        acc = acc + dot(outs[j], dw[c, j, :, :, 768:1024].reshape(256, 256))
    grown = acc.astype(BF)
    for w in range(4):
        chosen = dot(grow_ref[w], grown) * part_ref[...]
        piece = chosen[:, 0:64] + chosen[:, 64:128] + chosen[:, 128:192] + chosen[:, 192:256]
        grow_send[w] = jnp.concatenate([piece, jnp.zeros((T, 64), F32)], axis=1).astype(BF)
    for d in range(1, 8):
        send(grow_send.at[ms[d] // 2], grow_recv.at[m], s_grow.at[d - 1], r_grow.at[d - 1], at_m(d))
    step(3, 3)
    grow_recv[m] = grow_send[x]
    for d in range(1, 8):
        await_at(grow_recv.at[ms[(-d) % 8]], s_grow.at[d - 1], r_grow.at[d - 1], at_m(d))
    window = jnp.concatenate([grow_recv[j][:, 0:64] for j in range(8)], axis=1)
    state = (own_skip + window.astype(F32)).astype(BF)

    for layer in range(2):
        if layer == 0:
            top_ready(0, 1)
        else:
            step(3, 4)
        base = 768 * layer
        normed = norm_rows(state.astype(F32), top_gain_ref[layer, 0:1, :])
        parts = []
        for w in range(4):
            block = tw[w, :, :, :, base : base + 256].reshape(512, 256)
            parts.append(dot(normed, block).astype(BF))
        q = jnp.concatenate([p[:, 0:64] for p in parts], axis=1)
        k = jnp.concatenate([p[:, 64:128] for p in parts], axis=1)
        v = jnp.concatenate([p[:, 128:192] for p in parts], axis=1)
        if layer == 0:
            mixed = attend(q, k, v, bias_zero[...], heads)
        else:
            kv = jnp.concatenate([k, v], axis=1)
            halo_send[...] = dot(take_ref[...], kv).astype(BF)
            halo[0:T, :] = kv
            for e, (band_step, x_step, r0, nr, c0, nc, off, size) in enumerate(PIECES):
                src = halo_send.at[pl.ds(off - T, size)]
                dst = halo.at[pl.ds(off, size)]
                send(src, dst, s_halo.at[e], r_halo.at[e], at_piece(-band_step, -x_step))
            for e, (band_step, x_step, r0, nr, c0, nc, off, size) in enumerate(PIECES):
                dst = halo.at[pl.ds(off, size)]
                await_at(dst, s_halo.at[e], r_halo.at[e], at_piece(-band_step, -x_step))
            mixed = attend(q, halo[:, 0:256], halo[:, 256:512], bias_one[...], heads)
        total = jnp.zeros((T, 512), F32)
        for w in range(4):
            block = tw[w, :, :, :, base : base + 256].reshape(512, 256)
            wide = jnp.concatenate([jnp.zeros((T, 192), BF), mixed[:, 64 * w : 64 * w + 64]], axis=1)
            total = total + dot_t(wide, block)
        swap(2 * layer, total)
        if layer == 0:
            top_ready(1, 1)
        middle = (state.astype(F32) + swapped(2 * layer)).astype(BF)
        normed = norm_rows(middle.astype(F32), top_gain_ref[layer, 1:2, :])
        total = jnp.zeros((T, 512), F32)
        for w in range(4):
            block = tw[w, :, :, :, base + 256 : base + 512].reshape(512, 256)
            hidden = gelu(dot(normed, block)).astype(BF)
            total = total + dot_t(hidden, tw[w, :, :, :, base + 512 : base + 768].reshape(512, 256))
        swap(2 * layer + 1, total)
        state = (middle.astype(F32) + swapped(2 * layer + 1)).astype(BF)

    for half in range(2):
        fin[x, half] = state[:, 256 * half : 256 * half + 256]
    for d in (1, 2, 3):
        for e in range(2):
            core = lax.rem(c + e, 2)
            ss, rs = s_fin.at[d - 1, e], r_fin.at[d - 1, e]
            send(fin.at[x, c], fin.at[x, c], ss, rs, at_x(d, core))
    for d in (1, 2, 3):
        for e in range(2):
            core = lax.rem(c + e, 2)
            ss, rs = s_fin.at[d - 1, e], r_fin.at[d - 1, e]
            await_at(fin.at[xs[(-d) % 4], core], ss, rs, at_x(d, core))
    for half in range(2):
        stacked = jnp.concatenate([fin[w, half] for w in range(4)], axis=0)
        rows = dot(place_ref[...], stacked).astype(BF).reshape(6, 48, 256)
        out_ref[:, :, 256 * half : 256 * half + 256] = rows
    for cp in sends:
        cp.wait_send()
    for cond, cp in conditional:
        pl.when(cond)(cp.wait_send)


def local(
    skip_features,
    deep_features,
    top_gains,
    top_heads_in,
    top_heads_out,
    top_hidden_in,
    top_hidden_out,
    top_offsets,
    deep_gains,
    deep_offsets,
    deep_heads_in,
    deep_heads_out,
    deep_hidden_in,
    deep_hidden_out,
    expand_weight,
):
    constants = [jnp.asarray(a) for a in tables()]
    operands = [
        skip_features,
        deep_features,
        top_gains,
        deep_gains,
        top_offsets.transpose(0, 2, 1, 3),
        deep_offsets.transpose(1, 0, 2),
        deep_heads_in.transpose(1, 0, 2),
        deep_heads_out.T,
        deep_hidden_in,
        deep_hidden_out.T,
        expand_weight,
        top_heads_in.transpose(0, 2, 1, 3),
        top_heads_out.transpose(0, 2, 1),
        top_hidden_in,
        top_hidden_out.transpose(0, 2, 1),
        *constants,
    ]
    dma = pltpu.SemaphoreType.DMA
    shapes = [(3, 3), (4, 2, 8), (4,), (8,), (2,), (2,), (8,), (3,), (3,), (2, 2, 2), (2, 2, 2), (3,)]
    shapes += [(3, 2, 9), (1,), (2, 16), (16,), (7,), (7,), (4,), (8,), (3, 2)]
    vmem = pl.BlockSpec(memory_space=pltpu.VMEM)
    hbm = pl.BlockSpec(memory_space=pl.ANY)
    return pl.pallas_call(
        kernel,
        out_shape=jax.ShapeDtypeStruct((6, 48, 512), BF),
        in_specs=[hbm if i in FETCHED else vmem for i in range(len(operands))],
        out_specs=vmem,
        scratch_shapes=[
            pltpu.VMEM((2, 8, 4, 64, 1024), BF),
            pltpu.VMEM((4, 64, 768), BF),
            pltpu.VMEM((4, 8, 4, 16, 1536), BF),
            pltpu.VMEM((4, 8, 256), F32),
            pltpu.VMEM((2, 8, 128), F32),
            pltpu.VMEM((USED, 16, T), F32),
            pltpu.VMEM((16 * T, T), F32),
            pltpu.VMEM((USED, 32, EXT), F32),
            pltpu.VMEM((8 * T, T), F32),
            pltpu.VMEM((8 * T, EXT), F32),
            pltpu.VMEM((T, 2048), F32),
            pltpu.VMEM((4, T, 2048), BF),
            pltpu.VMEM((2, BANDS, 8, T, 256), BF),
            pltpu.VMEM((2, 4, 4, T, 256), BF),
            pltpu.VMEM((T, 256), BF),
            pltpu.VMEM((BANDS, 8, T, 256), BF),
            pltpu.VMEM((8, T, 256), BF),
            pltpu.VMEM((4, T, 128), BF),
            pltpu.VMEM((8, T, 128), BF),
            pltpu.VMEM((4, T, 512), BF),
            pltpu.VMEM((4, T, 512), BF),
            pltpu.VMEM((EXT - T, 512), BF),
            pltpu.VMEM((EXT, 512), BF),
            pltpu.VMEM((4, 2, T, 256), BF),
        ]
        + [pltpu.VMEM(operands[i].shape, operands[i].dtype) for i in FETCHED]
        + [dma((len(FETCHED),))]
        + [dma(s) for s in shapes for _ in range(2)],
        compiler_params=pltpu.CompilerParams(
            collective_id=0, has_side_effects=True, vmem_limit_bytes=56 * 2**20
        ),
    )(*operands)


def solution(mesh):
    placed = (
        P("band", None, None),
        P("band", None, None),
        P(),
        P(None, "band", None, "mp"),
        P(None, "mp", "band"),
        P(None, "band", "mp"),
        P(None, "mp", "band"),
        P(None, "mp", None, None),
        P(),
        P("mp", None, None),
        P("band", None, "mp"),
        P("mp", "band"),
        P("band", "mp"),
        P("mp", "band"),
        P("band", None, "mp"),
    )
    return jax.shard_map(
        local, mesh=mesh, in_specs=placed, out_specs=P("band", None, None), check_vma=False
    )
```
